32 devices in a mesh: img: 4 (over y, x), row: 4 (over z), col: 2 (over core).
Axes of the slice: x: 2, y: 2, z: 4, core: 2. Of those that a mesh axis runs over, the one named last changes fastest.
Arguments:
- tokens: bfloat16 [4, 128, 32, 1152], P('img', 'row', 'col'), may hold values from -30 to 30
- qkv_weight: bfloat16 [1152, 1728], replicated, may hold values from -1 to 1
- out_weight: bfloat16 [1152, 576], replicated, may hold values from -0.25 to 0.25
- upstream: bfloat16 [4, 128, 32, 1152], P('img', 'row', 'col'), may hold values from -6 to 6
Outputs:
- sublayer_out: bfloat16 [4, 128, 32, 1152], P('img', 'row', 'col')
- tokens_grad: bfloat16 [4, 128, 32, 1152], P('img', 'row', 'col')
- qkv_grad: float32 [1152, 1728], P(('row', 'col'))
- out_grad: float32 [1152, 576], P(('row', 'col'))
The draws below stay inside these ranges and needn't reach their ends.
All inputs are finite; a program needn't handle non-finite values.
Results may differ from the reference program's by a relative error of at most 0.015.
Values may be sent and summed in bfloat16 or wider, within the bound.
No kernel may reach another device: no remote copies, remote signals or barrier semaphores. Data moves between devices by JAX's collectives and lax.ppermute only.
A program may use at most 128 MiB of HBM per device.

```python
import jax
import jax.numpy as jnp
from jax import lax

D = 1152
H = 8
DH = 72
REACH = 8
WINDOW = 17
FRAME_ROWS = 128
FRAME_COLS = 32
IMAGES = 4


def draw_tokens(key, part):
    key = jax.random.fold_in(key, 11)
    first_key = jax.random.fold_in(key, 0)
    shape = (IMAGES, FRAME_ROWS, FRAME_COLS, D)
    values = jax.random.truncated_normal(first_key, -4.0, 4.0, shape, jnp.float32)
    return values.astype(jnp.bfloat16)


def draw_qkv_weight(key, part):
    key = jax.random.fold_in(key, 23)
    first_key = jax.random.fold_in(key, 0)
    inner = H * DH
    weights = jax.random.truncated_normal(first_key, -4.0, 4.0, (D, 3 * inner), jnp.float32) * D ** (-0.5)
    return weights.astype(jnp.bfloat16)


def levels(key, dims, pieces, least, largest):
    def one(axis_at, shards_of):
        steps = jax.random.uniform(jax.random.fold_in(jax.random.fold_in(key, 6), axis_at), (shards_of,), jnp.float32, least / len(pieces), largest / len(pieces))
        return jnp.repeat(jnp.exp(steps), dims[axis_at] // shards_of).reshape((-1,) + (1,) * (len(dims) - axis_at - 1))

    level = one(*pieces[0])
    for cut in pieces[1:]:
        level = level * one(*cut)
    return level


def gaussian(rng, shape, width, bound, cuts=(), held_as=jnp.bfloat16):
    factor_of = levels(rng, shape, cuts, -0.22, 0.18) if cuts else 1.0
    entries = jax.random.normal(rng, shape, jnp.float32) * width * factor_of
    return jnp.minimum(jnp.maximum(entries, -bound), bound).astype(held_as)


def setup_inputs(seed: int = 0) -> dict:
    arg_keys = jax.random.split(jax.random.key(seed), 5)
    tokens = draw_tokens(jax.random.fold_in(arg_keys[4], 71), 0)
    qkv_weight = draw_qkv_weight(jax.random.fold_in(arg_keys[4], 71), 0)
    out_weight = gaussian(arg_keys[2], (D, H * DH), (H * DH) ** -0.5, 0.25)
    upstream = gaussian(arg_keys[3], (IMAGES, FRAME_ROWS, FRAME_COLS, D), 1.0, 6.0, ((0, 4), (1, 4), (2, 2)))
    return dict(tokens=tokens, qkv_weight=qkv_weight, out_weight=out_weight, upstream=upstream)


band_step = 2

def clamp_starts(first_row, count, extent):
    places = first_row + jnp.arange(count, dtype=jnp.int32)
    return jnp.clip(places - REACH, 0, extent - WINDOW).astype(jnp.int32)

def reference(tokens, qkv_weight, out_weight, upstream):
    inner = H * DH
    scale = DH ** (-0.5)
    token_count = FRAME_ROWS * FRAME_COLS
    band_rows = band_step + 2 * REACH
    offsets = jnp.arange(WINDOW, dtype=jnp.int32)
    col_index = clamp_starts(0, FRAME_COLS, FRAME_COLS)[:, None] + offsets[None, :]
    qkv_total = jnp.zeros((D, 3 * inner), jnp.float32)
    out_total = jnp.zeros((D, inner), jnp.float32)
    results = []
    grads_in = []
    for image_idx in range(IMAGES):
        token_rows = tokens[image_idx].reshape(token_count, D)
        grad_rows = upstream[image_idx].reshape(token_count, D)
        projected = jnp.dot(token_rows, qkv_weight, preferred_element_type=jnp.float32).astype(jnp.bfloat16)
        projected = projected.reshape(FRAME_ROWS, FRAME_COLS, 3 * inner)
        grad_att = jnp.dot(grad_rows, out_weight, preferred_element_type=jnp.float32).astype(jnp.bfloat16)
        grad_att = grad_att.reshape(FRAME_ROWS, FRAME_COLS, inner)
        queries = projected[:, :, :inner]
        keys_all = projected[:, :, inner:2 * inner]
        values_all = projected[:, :, 2 * inner:]

        def block_step(carry, first_row):
            dkey_full, dvalue_full = carry
            band_start = jnp.clip(first_row - REACH, 0, FRAME_ROWS - band_rows).astype(jnp.int32)
            row_index = clamp_starts(first_row, band_step, FRAME_ROWS)[:, None] - band_start + offsets[None, :]

            def gather_window(field):
                col_taken = jnp.take(field, col_index, axis=1)
                row_taken = jnp.take(col_taken, row_index, axis=0)
                return row_taken.transpose(0, 2, 1, 3, 4).reshape(band_step * FRAME_COLS, WINDOW * WINDOW, H, DH)
            key_band = lax.dynamic_slice_in_dim(keys_all, band_start, band_rows, 0).astype(jnp.float32)
            value_band = lax.dynamic_slice_in_dim(values_all, band_start, band_rows, 0).astype(jnp.float32)
            key_win, scatter_back = jax.vjp(gather_window, key_band)
            value_win = gather_window(value_band)
            query_blk = lax.dynamic_slice_in_dim(queries, first_row, band_step, 0).astype(jnp.float32)
            query_blk = query_blk.reshape(band_step * FRAME_COLS, H, DH)
            grad_blk = lax.dynamic_slice_in_dim(grad_att, first_row, band_step, 0).astype(jnp.float32)
            grad_blk = grad_blk.reshape(band_step * FRAME_COLS, H, DH)
            scores = jnp.einsum('qhd,qkhd->qhk', query_blk, key_win) * scale
            row_max = lax.optimization_barrier(jnp.max(scores, axis=2, keepdims=True))
            shifted = jnp.exp(scores - row_max)
            attn_prob = shifted / lax.optimization_barrier(jnp.sum(shifted, axis=2, keepdims=True))
            prob_low = lax.optimization_barrier(attn_prob.astype(jnp.bfloat16)).astype(jnp.float32)
            attended = jnp.einsum('qhk,qkhd->qhd', prob_low, value_win)
            dprob = jnp.einsum('qhd,qkhd->qhk', grad_blk, value_win)
            row_dot = lax.optimization_barrier(jnp.sum(attn_prob * dprob, axis=2, keepdims=True))
            dscore = (attn_prob * (dprob - row_dot) * scale).astype(jnp.bfloat16)
            dscore = lax.optimization_barrier(dscore).astype(jnp.float32)
            dquery = jnp.einsum('qhk,qkhd->qhd', dscore, key_win)
            dkey_band = scatter_back(jnp.einsum('qhk,qhd->qkhd', dscore, query_blk))[0]
            dvalue_band = scatter_back(jnp.einsum('qhk,qhd->qkhd', prob_low, grad_blk))[0]
            dkey_full = lax.dynamic_update_slice_in_dim(dkey_full, lax.dynamic_slice_in_dim(dkey_full, band_start, band_rows, 0) + dkey_band, band_start, 0)
            dvalue_full = lax.dynamic_update_slice_in_dim(dvalue_full, lax.dynamic_slice_in_dim(dvalue_full, band_start, band_rows, 0) + dvalue_band, band_start, 0)
            return ((dkey_full, dvalue_full), (attended.astype(jnp.bfloat16).reshape(band_step * FRAME_COLS, inner), dquery.reshape(band_step * FRAME_COLS, inner)))
        firsts = jnp.arange(0, FRAME_ROWS, band_step, dtype=jnp.int32)
        zero_field = jnp.zeros((FRAME_ROWS, FRAME_COLS, inner), jnp.float32)
        (dkey_full, dvalue_full), (attended_blocks, dquery_blocks) = lax.scan(block_step, (zero_field, zero_field), firsts)
        attended = attended_blocks.reshape(token_count, inner)
        sublayer_out = jnp.dot(attended, out_weight.T, preferred_element_type=jnp.float32).astype(jnp.bfloat16)
        dqkv = jnp.concatenate([dquery_blocks.reshape(token_count, inner), dkey_full.reshape(token_count, inner), dvalue_full.reshape(token_count, inner)], axis=1).astype(jnp.bfloat16)
        tokens_grad = jnp.dot(dqkv, qkv_weight.T, preferred_element_type=jnp.float32).astype(jnp.bfloat16)
        qkv_total = qkv_total + jnp.dot(token_rows.T, dqkv, preferred_element_type=jnp.float32)
        out_total = out_total + jnp.dot(grad_rows.T, attended, preferred_element_type=jnp.float32)
        results.append(sublayer_out.reshape(FRAME_ROWS, FRAME_COLS, D))
        grads_in.append(tokens_grad.reshape(FRAME_ROWS, FRAME_COLS, D))
    return (jnp.stack(results), jnp.stack(grads_in), qkv_total, out_total)
```

```python
import jax
import jax.numpy as jnp
from jax import lax
from jax.experimental import pallas as pl
from jax.experimental.pallas import tpu as pltpu
from jax.sharding import PartitionSpec as P

H = 8
DH = 72
INNER = H * DH
REACH = 8
WINDOW = 17
SIDE = 8
PAIRS = H // 2
SLAB = 256
V_SHIFT = 64
MASKED = -1e30
SCALE = DH ** (-0.5)


def shifted_pairs(count, by):
    return [(i, i + by) for i in range(count) if 0 <= i + by < count]


def nt_dot(a, b):
    return lax.dot_general(a, b, (((1,), (1,)), ((), ())), preferred_element_type=jnp.float32)


def attention_kernel(
    start_ref,
    q_ref,
    g_ref,
    own_ref,
    rows_ref,
    cols_ref,
    corner_ref,
    bias_ref,
    o_ref,
    dq_ref,
    tile_grad_ref,
    side_grad_ref,
    kv,
    kvt,
    acc,
    ot,
    dqt,
):
    strips = own_ref.shape[0]
    chunk_own = own_ref.shape[1]
    chunk_side = cols_ref.shape[1]
    chunk = chunk_own + chunk_side
    band = 3 * chunk
    last = strips + 1

    def place(slot, own, side):
        kv[slot, :chunk_own] = own
        kv[slot, chunk_own:] = side
        kvt[slot, :, :chunk_own] = own.T
        padded = jnp.concatenate([side, jnp.zeros((128 - chunk_side, 2 * INNER), side.dtype)], axis=0) if chunk_side < 128 else side
        kvt[slot, :, chunk_own:] = padded.T[:, :chunk_side]

    for s in range(strips):
        place(s + 1, own_ref[s], cols_ref[s])
    place(0, rows_ref[0], corner_ref[0])
    place(last, rows_ref[1], corner_ref[1])
    acc[...] = jnp.zeros_like(acc)

    lane = lax.broadcasted_iota(jnp.int32, (1, SLAB), 1)

    def lanes_of(first):
        inside = (lane >= first) & (lane < first + DH)
        return jnp.where(inside, 1.0, 0.0).astype(jnp.bfloat16)

    def strip(s, carry):
        top = start_ref[s]
        rows = pl.ds(pl.multiple_of(s * chunk_own, chunk_own), chunk_own)
        bias = bias_ref[s]
        bias = jnp.concatenate([bias, bias], axis=1)
        for i in range(PAIRS):
            q = q_ref[rows, 128 * i : 128 * i + SLAB]
            g = g_ref[rows, 128 * i : 128 * i + SLAB]
            q2 = jnp.concatenate([q * lanes_of(16 * i), q * lanes_of(16 * i + DH)], axis=0)
            g2 = jnp.concatenate(
                [g * lanes_of(V_SHIFT + 16 * i), g * lanes_of(V_SHIFT + 16 * i + DH)], axis=0
            )
            k_lanes = slice(128 * i, 128 * i + SLAB)
            v_lanes = slice(512 + 128 * i, 512 + 128 * i + SLAB)
            keys = kv[pl.ds(top, 3), :, k_lanes].reshape(band, SLAB)
            values = kv[pl.ds(top, 3), :, v_lanes].reshape(band, SLAB)
            scores = nt_dot(keys, q2) * SCALE + bias
            shifted = jnp.exp(scores - jnp.max(scores, axis=0, keepdims=True))
            prob = shifted * (1.0 / jnp.sum(shifted, axis=0, keepdims=True))
            prob_low = prob.astype(jnp.bfloat16)
            dprob = nt_dot(values, g2)
            row_dot = jnp.sum(prob * dprob, axis=0, keepdims=True)
            dscore = (prob * (dprob - row_dot) * SCALE).astype(jnp.bfloat16)
            dk = jnp.dot(dscore, q2, preferred_element_type=jnp.float32)
            dv = jnp.dot(prob_low, g2, preferred_element_type=jnp.float32)
            acc[pl.ds(top, 3), :, k_lanes] += dk.reshape(3, chunk, SLAB)
            acc[pl.ds(top, 3), :, v_lanes] += dv.reshape(3, chunk, SLAB)
            k_rows = slice(2 * DH * i, 2 * DH * (i + 1))
            v_rows = slice(INNER + 2 * DH * i, INNER + 2 * DH * (i + 1))
            att = jnp.zeros((2 * DH, SLAB), jnp.float32)
            dqv = jnp.zeros((2 * DH, SLAB), jnp.float32)
            for j in range(3):
                part = slice(chunk * j, chunk * (j + 1))
                att += jnp.dot(kvt[top + j, v_rows, :], prob_low[part], preferred_element_type=jnp.float32)
                dqv += jnp.dot(kvt[top + j, k_rows, :], dscore[part], preferred_element_type=jnp.float32)
            first = 2 * DH * i
            ot[first : first + DH, :] = att[:DH, :chunk_own]
            ot[first + DH : first + 2 * DH, :] = att[DH:, chunk_own:]
            dqt[first : first + DH, :] = dqv[:DH, :chunk_own]
            dqt[first + DH : first + 2 * DH, :] = dqv[DH:, chunk_own:]
        o_ref[rows, :] = ot[...].T[:, :INNER].astype(jnp.bfloat16)
        dq_ref[rows, :] = dqt[...].T[:, :INNER].astype(jnp.bfloat16)
        return carry

    lax.fori_loop(0, strips, strip, 0)
    tile_grad_ref[...] = acc[:, :chunk_own, :]
    side_grad_ref[...] = acc[:, chunk_own:, :].astype(jnp.bfloat16)


def attention(start, projected, grads, own, rows, cols, corner, bias):
    strips, chunk_own, width = own.shape
    chunk_side = cols.shape[1]
    chunk = chunk_own + chunk_side
    token_count = strips * chunk_own
    whole = lambda a: pl.BlockSpec(a.shape, lambda _: (0,) * a.ndim)
    outs = (
        jax.ShapeDtypeStruct((token_count, INNER), jnp.bfloat16),
        jax.ShapeDtypeStruct((token_count, INNER), jnp.bfloat16),
        jax.ShapeDtypeStruct((strips + 2, chunk_own, width), jnp.float32),
        jax.ShapeDtypeStruct((strips + 2, chunk_side, width), jnp.bfloat16),
    )
    return pl.pallas_call(
        attention_kernel,
        grid=(1,),
        out_shape=outs,
        in_specs=[
            pl.BlockSpec(memory_space=pltpu.SMEM),
            pl.BlockSpec((token_count, 640), lambda _: (0, 0)),
            whole(grads),
            whole(own),
            whole(rows),
            whole(cols),
            whole(corner),
            whole(bias),
        ],
        out_specs=tuple(whole(o) for o in outs),
        scratch_shapes=[
            pltpu.VMEM((strips + 2, chunk, width), jnp.bfloat16),
            pltpu.VMEM((strips + 2, width, chunk), jnp.bfloat16),
            pltpu.VMEM((strips + 2, chunk, width), jnp.float32),
            pltpu.VMEM((640, chunk_own), jnp.float32),
            pltpu.VMEM((640, chunk_own), jnp.float32),
        ],
        compiler_params=pltpu.CompilerParams(vmem_limit_bytes=48 * 1024 * 1024),
        cost_estimate=pl.CostEstimate(
            flops=12 * token_count * 3 * chunk * 2 * INNER,
            bytes_accessed=16 * 1024 * 1024,
            transcendentals=token_count * 3 * chunk * H,
        ),
        name="window_attention",
    )(start, projected, grads, own, rows, cols, corner, bias)


def window_starts(places, extent):
    return jnp.clip(places - REACH, 0, extent - WINDOW)


def window_bias(tile_rows, tile_cols, two_columns):
    row_id = lax.axis_index("row")
    col_id = lax.axis_index("col")
    frame_rows = tile_rows * lax.axis_size("row")
    frame_cols = tile_cols * lax.axis_size("col")
    strips = tile_rows // SIDE
    col_first = col_id * tile_cols
    strip_id = jnp.arange(strips, dtype=jnp.int32)
    first_chunk = row_id * strips - 1
    band_chunk = jnp.clip(row_id * strips + strip_id - 1, 0, frame_rows // SIDE - 3)
    side = jnp.arange(SIDE, dtype=jnp.int32)
    own_cols = col_first + jnp.arange(tile_cols, dtype=jnp.int32)
    low, high = col_first - REACH + side, col_first + tile_cols + side
    spans = [own_cols, jnp.where(col_id == 0, high, low)] if two_columns else [own_cols, low, high]
    chunk_rows = jnp.concatenate([jnp.repeat(side, span.shape[0]) for span in spans])
    chunk_cols = jnp.concatenate([jnp.tile(span, SIDE) for span in spans])
    in_band = jnp.concatenate([SIDE * j + chunk_rows for j in range(3)])
    key_col = jnp.tile(chunk_cols, 3)
    key_row = SIDE * band_chunk[:, None] + in_band[None, :]
    query_row = row_id * tile_rows + SIDE * strip_id[:, None] + jnp.repeat(side, tile_cols)[None, :]
    row_start = window_starts(query_row, frame_rows)
    col_start = window_starts(jnp.tile(own_cols, SIDE), frame_cols)
    row_off = key_row[:, :, None] - row_start[:, None, :]
    col_off = key_col[:, None] - col_start[None, :]
    row_ok = (row_off >= 0) & (row_off < WINDOW)
    col_ok = (col_off >= 0) & (col_off < WINDOW)
    bias = jnp.where(row_ok & col_ok[None], 0.0, MASKED).astype(jnp.float32)
    return (band_chunk - first_chunk).astype(jnp.int32), bias


def swap_halves(block, axis_dim):
    own = lax.axis_index("col")
    kept = lax.dynamic_index_in_dim(block, own, axis_dim, keepdims=False)
    sent = lax.dynamic_index_in_dim(block, 1 - own, axis_dim, keepdims=False)
    return kept, lax.ppermute(sent, "col", [(0, 1), (1, 0)])


def exchange_sum(block, axis):
    got = lax.all_to_all(block, axis, split_axis=0, concat_axis=0, tiled=True)
    return jnp.sum(got.astype(jnp.float32), axis=0).astype(jnp.bfloat16)


def summed_shares(part):
    rows, cols, images = (lax.axis_size(a) for a in ("row", "col", "img"))
    width = part.shape[1]
    share = part.shape[0] // (rows * cols)
    if cols != 2 or share % images:
        held = lax.psum_scatter(part, ("row", "col"), scatter_dimension=0, tiled=True)
        return lax.psum(held, "img").astype(jnp.float32)
    kept, got = swap_halves(part.reshape(rows, 2, share, width), 1)
    held = (kept.astype(jnp.float32) + got.astype(jnp.float32)).astype(jnp.bfloat16)
    small = share // images
    held = held.reshape(rows, images, small, width).transpose(1, 0, 2, 3)
    held = exchange_sum(held, "img")
    held = exchange_sum(held, "row")
    return lax.all_gather(held, "img", axis=0, tiled=True).astype(jnp.float32)


def local(tokens, qkv_weight, out_weight, upstream):
    _, tile_rows, tile_cols, width = tokens.shape
    token_count = tile_rows * tile_cols
    strips = tile_rows // SIDE
    chunk_own = SIDE * tile_cols
    row_count, col_count = lax.axis_size("row"), lax.axis_size("col")
    two_columns = col_count == 2
    col_id = lax.axis_index("col")
    token_rows = tokens.reshape(token_count, width)
    grad_rows = upstream.reshape(token_count, width)
    down, up = shifted_pairs(row_count, 1), shifted_pairs(row_count, -1)
    swap = [(0, 1), (1, 0)]

    projected = jnp.dot(token_rows, qkv_weight, preferred_element_type=jnp.float32).astype(
        jnp.bfloat16
    )
    keyvals = projected[:, INNER:]
    above = lax.ppermute(keyvals[token_count - chunk_own :], "row", down)
    below = lax.ppermute(keyvals[:chunk_own], "row", up)

    def side_columns(block, rows):
        block = block.reshape(rows, tile_cols, 2 * INNER)
        if two_columns:
            near = lax.dynamic_slice_in_dim(block, (1 - col_id) * (tile_cols - REACH), REACH, 1)
            got = [lax.ppermute(near, "col", swap)]
        else:
            got = [
                lax.ppermute(block[:, tile_cols - REACH :], "col", shifted_pairs(col_count, 1)),
                lax.ppermute(block[:, :REACH], "col", shifted_pairs(col_count, -1)),
            ]
        got = [g.reshape(rows // SIDE, SIDE * REACH, 2 * INNER) for g in got]
        return got[0] if two_columns else jnp.concatenate(got, axis=1)

    cols = side_columns(keyvals, tile_rows)
    rows = jnp.stack([above, below])
    corner = side_columns(rows, 2 * SIDE)
    start, bias = window_bias(tile_rows, tile_cols, two_columns)
    grad_att = jnp.dot(grad_rows, out_weight, preferred_element_type=jnp.float32).astype(
        jnp.bfloat16
    )
    grads = jnp.pad(grad_att, ((0, 0), (V_SHIFT, 0)))
    own = keyvals.reshape(strips, chunk_own, 2 * INNER)
    attended, dquery, tile_grad, side_grad = attention(
        start, projected, grads, own, rows, cols, corner, bias
    )

    def outer(a, b):
        return lax.dot_general(
            a, b, (((0,), (0,)), ((), ())), preferred_element_type=jnp.float32
        ).astype(jnp.bfloat16)

    early = jnp.concatenate([outer(token_rows, dquery), outer(grad_rows, attended)], axis=1)
    early = summed_shares(early)
    sublayer_out = lax.dot_general(
        attended, out_weight, (((1,), (1,)), ((), ())), preferred_element_type=jnp.float32
    ).astype(jnp.bfloat16)

    def spread(side, first):
        side = side.reshape(strips + 2, SIDE, REACH, 2 * INNER).astype(jnp.float32)
        zeros = jnp.zeros((strips + 2, SIDE, tile_cols - REACH, 2 * INNER), jnp.float32)
        order = [side, zeros] if first else [zeros, side]
        return jnp.concatenate(order, axis=2).reshape(strips + 2, chunk_own, 2 * INNER)

    if two_columns:
        got = lax.ppermute(side_grad, "col", swap)
        tile_grad += jnp.where(col_id == 0, spread(got, False), spread(got, True))
    else:
        half = SIDE * REACH
        to_left = lax.ppermute(side_grad[:, :half], "col", shifted_pairs(col_count, -1))
        to_right = lax.ppermute(side_grad[:, half:], "col", shifted_pairs(col_count, 1))
        tile_grad += spread(to_left, False) + spread(to_right, True)
    from_below = lax.ppermute(tile_grad[0].astype(jnp.bfloat16), "row", up)
    from_above = lax.ppermute(tile_grad[strips + 1].astype(jnp.bfloat16), "row", down)
    dkv = tile_grad[1 : strips + 1]
    dkv = dkv.at[0].add(from_above.astype(jnp.float32))
    dkv = dkv.at[strips - 1].add(from_below.astype(jnp.float32))
    dkv = dkv.reshape(token_count, 2 * INNER).astype(jnp.bfloat16)
    late = summed_shares(outer(token_rows, dkv))
    dqkv = jnp.concatenate([dquery, dkv], axis=1)
    tokens_grad = lax.dot_general(
        dqkv, qkv_weight, (((1,), (1,)), ((), ())), preferred_element_type=jnp.float32
    ).astype(jnp.bfloat16)
    return (
        sublayer_out.reshape(tokens.shape),
        tokens_grad.reshape(tokens.shape),
        jnp.concatenate([early[:, :INNER], late], axis=1),
        early[:, INNER:],
    )


def solution(mesh):
    return jax.shard_map(
        local,
        mesh=mesh,
        in_specs=(P("img", "row", "col", None), P(), P(), P("img", "row", "col", None)),
        out_specs=(
            P("img", "row", "col", None),
            P("img", "row", "col", None),
            P(("row", "col"), None),
            P(("row", "col"), None),
        ),
        check_vma=False,
    )
```

```python
import jax
import jax.numpy as jnp
from jax import lax
from jax.experimental import pallas as pl
from jax.experimental.pallas import tpu as pltpu
from jax.sharding import PartitionSpec as P

H = 8
DH = 72
INNER = H * DH
REACH = 8
WINDOW = 17
SIDE = 8
PAIRS = H // 2
SLAB = 256
V_SHIFT = 64
MASKED = -1e30
SCALE = DH ** (-0.5)


def shifted_pairs(count, by):
    return [(i, i + by) for i in range(count) if 0 <= i + by < count]


def dot(a, b):
    return jnp.dot(a, b, preferred_element_type=jnp.float32)


def nt_dot(a, b):
    return lax.dot_general(a, b, (((1,), (1,)), ((), ())), preferred_element_type=jnp.float32)


def attention_kernel(
    start_ref,
    q_ref,
    own_ref,
    g_ref,
    halo_ref,
    weight_ref,
    bias_ref,
    o_ref,
    dq_ref,
    grad_ref,
    kv,
    kvt,
    acc,
    qt,
    gt,
    ot,
    dqt,
):
    strips = bias_ref.shape[0]
    chunk = kv.shape[1]
    chunk_own = own_ref.shape[0] // strips
    chunk_side = chunk - chunk_own
    band = 3 * chunk
    token_count = own_ref.shape[0]
    side_first = token_count + 2 * chunk_own
    last = strips + 1
    own_at = [token_count] + [chunk_own * s for s in range(strips)] + [token_count + chunk_own]
    side_order = [strips] + list(range(strips)) + [strips + 1]
    side_at = [side_first + chunk_side * s for s in side_order]

    def place(slot, first, part):
        count = part.shape[0]
        kv[slot, first : first + count] = part
        if count < 128:
            filler = jnp.zeros((128 - count, 2 * INNER), part.dtype)
            part = jnp.concatenate([part, filler], axis=0)
        kvt[slot, :, first : first + count] = part.T[:, :count]

    qt[...] = q_ref[...].T
    gt[...] = g_ref[...].T
    for s in range(strips):
        place(s + 1, 0, own_ref[chunk_own * s : chunk_own * (s + 1)])
    halo_kv = dot(halo_ref[...], weight_ref[:, INNER - 64 :]).astype(jnp.bfloat16)[:, 64:]
    for slot in range(strips + 2):
        at = side_at[slot] - token_count
        place(slot, chunk_own, halo_kv[at : at + chunk_side])
    place(0, 0, halo_kv[:chunk_own])
    place(last, 0, halo_kv[chunk_own : 2 * chunk_own])
    acc[...] = jnp.zeros_like(acc)

    row = lax.broadcasted_iota(jnp.int32, (2 * DH, chunk_own), 0)
    first_head = row < DH
    mask_a = jnp.where(first_head, 1.0, 0.0).astype(jnp.bfloat16)
    mask_b = jnp.where(first_head, 0.0, 1.0).astype(jnp.bfloat16)
    ones = jnp.ones((16, chunk), jnp.bfloat16)

    def pair_block(part, above):
        block = jnp.concatenate([part * mask_a, part * mask_b], axis=1)
        parts = [block]
        if above:
            parts = [jnp.zeros((above, block.shape[1]), block.dtype)] + parts
        below = SLAB - 2 * DH - above
        if below:
            parts = parts + [jnp.zeros((below, block.shape[1]), block.dtype)]
        return jnp.concatenate(parts, axis=0)

    def pick(both):
        return jnp.where(first_head, both[:, :chunk_own], both[:, chunk_own:])

    def strip(s, carry):
        top = start_ref[s]
        rows = pl.ds(pl.multiple_of(s * chunk_own, chunk_own), chunk_own)
        bias = bias_ref[s]
        bias = jnp.concatenate([bias, bias], axis=1)
        for i in range(PAIRS):
            heads = slice(2 * DH * i, 2 * DH * (i + 1))
            k_lanes = slice(128 * i, 128 * i + SLAB)
            v_lanes = slice(512 + 128 * i, 512 + 128 * i + SLAB)
            grads = gt[heads, rows]
            q2 = pair_block(qt[heads, rows], 16 * i)
            g2 = pair_block(grads, V_SHIFT + 16 * i)
            keys = kv[pl.ds(top, 3), :, k_lanes].reshape(band, SLAB)
            values = kv[pl.ds(top, 3), :, v_lanes].reshape(band, SLAB)
            scores = dot(keys, q2) * SCALE + bias
            prob = jnp.exp(scores - jnp.max(scores, axis=0, keepdims=True)).astype(jnp.bfloat16)
            total = jnp.zeros((16, SLAB), jnp.float32)
            att = jnp.zeros((2 * DH, SLAB), jnp.float32)
            for j in range(3):
                part = prob[chunk * j : chunk * (j + 1)]
                v_rows = slice(INNER + 2 * DH * i, INNER + 2 * DH * (i + 1))
                att += dot(kvt[top + j, v_rows, :], part)
                total += dot(ones, part)
            inv = 1.0 / total[:1]
            att = pick(att * inv)
            ot[heads, :] = att
            dots = att * grads.astype(jnp.float32)
            row_dot = jnp.concatenate(
                [
                    jnp.sum(dots[:DH], axis=0, keepdims=True),
                    jnp.sum(dots[DH:], axis=0, keepdims=True),
                ],
                axis=1,
            )
            inv_scale = inv * SCALE
            dprob = dot(values, g2)
            dscore = prob.astype(jnp.float32) * (dprob * inv_scale - row_dot * inv_scale)
            dscore = dscore.astype(jnp.bfloat16)
            dqv = jnp.zeros((2 * DH, SLAB), jnp.float32)
            for j in range(3):
                dqv += dot(kvt[top + j, heads, :], dscore[chunk * j : chunk * (j + 1)])
            dqt[heads, :] = pick(dqv)
            dk = nt_dot(dscore, q2)
            dv = nt_dot(prob, (g2.astype(jnp.float32) * inv).astype(jnp.bfloat16))
            acc[pl.ds(top, 3), :, k_lanes] += dk.reshape(3, chunk, SLAB)
            acc[pl.ds(top, 3), :, v_lanes] += dv.reshape(3, chunk, SLAB)
        o_ref[rows, :] = ot[...].T[:, :INNER].astype(jnp.bfloat16)
        dq_ref[rows, :] = dqt[...].T[:, :INNER].astype(jnp.bfloat16)
        return carry

    lax.fori_loop(0, strips, strip, 0)
    for slot in range(strips + 2):
        grad_ref[own_at[slot] : own_at[slot] + chunk_own, :] = acc[slot, :chunk_own].astype(
            jnp.bfloat16
        )
        grad_ref[side_at[slot] : side_at[slot] + chunk_side, :] = acc[slot, chunk_own:].astype(
            jnp.bfloat16
        )


def attention(start, projected, own, grads, halo, weight, bias):
    strips, band, chunk_own = bias.shape
    chunk = band // 3
    token_count, width = own.shape
    key_count = token_count + halo.shape[0]
    whole = lambda a: pl.BlockSpec(a.shape, lambda _: (0,) * a.ndim)
    outs = (
        jax.ShapeDtypeStruct((token_count, INNER), jnp.bfloat16),
        jax.ShapeDtypeStruct((token_count, INNER), jnp.bfloat16),
        jax.ShapeDtypeStruct((key_count, width), jnp.bfloat16),
    )
    return pl.pallas_call(
        attention_kernel,
        grid=(1,),
        out_shape=outs,
        in_specs=[
            pl.BlockSpec(memory_space=pltpu.SMEM),
            pl.BlockSpec((token_count, 640), lambda _: (0, 0)),
            whole(own),
            whole(grads),
            whole(halo),
            whole(weight),
            whole(bias),
        ],
        out_specs=tuple(whole(o) for o in outs),
        scratch_shapes=[
            pltpu.VMEM((strips + 2, chunk, width), jnp.bfloat16),
            pltpu.VMEM((strips + 2, width, chunk), jnp.bfloat16),
            pltpu.VMEM((strips + 2, chunk, width), jnp.float32),
            pltpu.VMEM((640, token_count), jnp.bfloat16),
            pltpu.VMEM((INNER, token_count), jnp.bfloat16),
            pltpu.VMEM((640, chunk_own), jnp.float32),
            pltpu.VMEM((640, chunk_own), jnp.float32),
        ],
        compiler_params=pltpu.CompilerParams(vmem_limit_bytes=52 * 1024 * 1024),
        cost_estimate=pl.CostEstimate(
            flops=12 * token_count * band * 2 * INNER,
            bytes_accessed=16 * 1024 * 1024,
            transcendentals=token_count * band * H,
        ),
        name="window_attention",
    )(start, projected, own, grads, halo, weight, bias)


def window_starts(places, extent):
    return jnp.clip(places - REACH, 0, extent - WINDOW)


def window_bias(tile_rows, tile_cols, two_columns):
    row_id = lax.axis_index("row")
    col_id = lax.axis_index("col")
    frame_rows = tile_rows * lax.axis_size("row")
    frame_cols = tile_cols * lax.axis_size("col")
    strips = tile_rows // SIDE
    col_first = col_id * tile_cols
    strip_id = jnp.arange(strips, dtype=jnp.int32)
    first_chunk = row_id * strips - 1
    band_chunk = jnp.clip(row_id * strips + strip_id - 1, 0, frame_rows // SIDE - 3)
    side = jnp.arange(SIDE, dtype=jnp.int32)
    own_cols = col_first + jnp.arange(tile_cols, dtype=jnp.int32)
    low, high = col_first - REACH + side, col_first + tile_cols + side
    spans = [own_cols, jnp.where(col_id == 0, high, low)] if two_columns else [own_cols, low, high]
    chunk_rows = jnp.concatenate([jnp.repeat(side, span.shape[0]) for span in spans])
    chunk_cols = jnp.concatenate([jnp.tile(span, SIDE) for span in spans])
    in_band = jnp.concatenate([SIDE * j + chunk_rows for j in range(3)])
    key_col = jnp.tile(chunk_cols, 3)
    key_row = SIDE * band_chunk[:, None] + in_band[None, :]
    query_row = row_id * tile_rows + SIDE * strip_id[:, None] + jnp.repeat(side, tile_cols)[None, :]
    row_start = window_starts(query_row, frame_rows)
    col_start = window_starts(jnp.tile(own_cols, SIDE), frame_cols)
    row_off = key_row[:, :, None] - row_start[:, None, :]
    col_off = key_col[:, None] - col_start[None, :]
    row_ok = (row_off >= 0) & (row_off < WINDOW)
    col_ok = (col_off >= 0) & (col_off < WINDOW)
    bias = jnp.where(row_ok & col_ok[None], 0.0, MASKED).astype(jnp.float32)
    return (band_chunk - first_chunk).astype(jnp.int32), bias


def swap_halves(block, axis_dim):
    own = lax.axis_index("col")
    kept = lax.dynamic_index_in_dim(block, own, axis_dim, keepdims=False)
    sent = lax.dynamic_index_in_dim(block, 1 - own, axis_dim, keepdims=False)
    return kept, lax.ppermute(sent, "col", [(0, 1), (1, 0)])


def exchange_sum(block, axis):
    got = lax.all_to_all(block, axis, split_axis=0, concat_axis=0, tiled=True)
    return jnp.sum(got.astype(jnp.float32), axis=0).astype(jnp.bfloat16)


def summed_shares(part):
    rows, cols, images = (lax.axis_size(a) for a in ("row", "col", "img"))
    width = part.shape[1]
    share = part.shape[0] // (rows * cols)
    if cols != 2:
        held = lax.psum_scatter(part, ("row", "col"), scatter_dimension=0, tiled=True)
        return lax.psum(held, "img").astype(jnp.float32)
    kept, got = swap_halves(part.reshape(rows, 2, share, width), 1)
    held = (kept.astype(jnp.float32) + got.astype(jnp.float32)).astype(jnp.bfloat16)
    small = -(-share // (8 * images)) * 8
    held = jnp.pad(held, ((0, 0), (0, images * small - share), (0, 0)))
    held = held.reshape(rows, images, small, width).transpose(1, 0, 2, 3)
    held = exchange_sum(held, "img")
    held = exchange_sum(held, "row")
    held = jnp.broadcast_to(held[None], (images, small, width))
    held = lax.all_to_all(held, "img", split_axis=0, concat_axis=0, tiled=True)
    return held.reshape(images * small, width)[:share].astype(jnp.float32)


def local(tokens, qkv_weight, out_weight, upstream):
    _, tile_rows, tile_cols, width = tokens.shape
    token_count = tile_rows * tile_cols
    strips = tile_rows // SIDE
    chunk_own = SIDE * tile_cols
    row_count, col_count = lax.axis_size("row"), lax.axis_size("col")
    two_columns = col_count == 2
    col_id = lax.axis_index("col")
    token_rows = tokens.reshape(token_count, width)
    grad_rows = upstream.reshape(token_count, width)
    grid = tokens.reshape(tile_rows, tile_cols, width)
    turns = (0,) if two_columns else (-1, 1)

    def moved(block, down, turn=None):
        pairs = []
        for r in range(row_count):
            for c in range(col_count):
                to_c = c if turn is None else (1 - c if turn == 0 else c + turn)
                if 0 <= r + down < row_count and 0 <= to_c < col_count:
                    pairs.append((r * col_count + c, (r + down) * col_count + to_c))
        return lax.ppermute(block, ("row", "col"), pairs)

    def edge(block, turn):
        if turn == 0:
            return lax.dynamic_slice_in_dim(block, (1 - col_id) * (tile_cols - REACH), REACH, 1)
        return block[:, tile_cols - REACH :] if turn == 1 else block[:, :REACH]

    def side_of(rows, down):
        got = [moved(edge(rows, t), down, t) for t in sorted(turns, reverse=True)]
        got = [g.reshape(-1, SIDE * REACH, width) for g in got]
        got = got[0] if two_columns else jnp.concatenate(got, axis=1)
        return got.reshape(-1, width)

    bottom, top = grid[tile_rows - SIDE :], grid[:SIDE]
    above = moved(bottom, 1).reshape(chunk_own, width)
    below = moved(top, -1).reshape(chunk_own, width)
    halo = jnp.concatenate(
        [above, below, side_of(grid, 0), side_of(bottom, 1), side_of(top, -1)], axis=0
    )

    projected = dot(token_rows, qkv_weight).astype(jnp.bfloat16)
    grad_att = dot(grad_rows, out_weight).astype(jnp.bfloat16)
    start, bias = window_bias(tile_rows, tile_cols, two_columns)
    attended, dquery, ext_grad = attention(
        start, projected, projected[:, INNER:], grad_att, halo, qkv_weight, bias
    )

    def outer(a, b):
        return lax.dot_general(
            a, b, (((0,), (0,)), ((), ())), preferred_element_type=jnp.float32
        ).astype(jnp.bfloat16)

    early = jnp.concatenate([outer(token_rows, dquery), outer(grad_rows, attended)], axis=1)
    late = outer(jnp.concatenate([token_rows, halo], axis=0), ext_grad)
    early = summed_shares(early)
    late = summed_shares(late)
    sublayer_out = nt_dot(attended, out_weight).astype(jnp.bfloat16)

    def spread(side, first):
        side = side.reshape(-1, SIDE, REACH, 2 * INNER).astype(jnp.float32)
        zeros = jnp.zeros((side.shape[0], SIDE, tile_cols - REACH, 2 * INNER), jnp.float32)
        order = [side, zeros] if first else [zeros, side]
        return jnp.concatenate(order, axis=2).reshape(-1, 2 * INNER)

    side_first = token_count + 2 * chunk_own
    inner_grad, side_grad = ext_grad[:side_first].astype(jnp.float32), ext_grad[side_first:]
    if two_columns:
        got = moved(side_grad, 0, 0)
        returned = jnp.where(col_id == 0, spread(got, False), spread(got, True))
    else:
        halves = side_grad.reshape(strips + 2, 2, SIDE * REACH, 2 * INNER)
        returned = spread(moved(halves[:, 0], 0, -1), False) + spread(moved(halves[:, 1], 0, 1), True)
    inner_grad = inner_grad + returned
    dkv = inner_grad[:token_count]
    to_above = inner_grad[token_count : token_count + chunk_own].astype(jnp.bfloat16)
    to_below = inner_grad[token_count + chunk_own :].astype(jnp.bfloat16)
    from_below = moved(to_above, -1).astype(jnp.float32)
    from_above = moved(to_below, 1).astype(jnp.float32)
    rest = jnp.zeros((token_count - chunk_own, 2 * INNER), jnp.float32)
    dkv = dkv + jnp.concatenate([from_above, rest], axis=0)
    dkv = dkv + jnp.concatenate([rest, from_below], axis=0)
    dqkv = jnp.concatenate([dquery, dkv.astype(jnp.bfloat16)], axis=1)
    tokens_grad = nt_dot(dqkv, qkv_weight).astype(jnp.bfloat16)
    return (
        sublayer_out.reshape(tokens.shape),
        tokens_grad.reshape(tokens.shape),
        jnp.concatenate([early[:, :INNER], late], axis=1),
        early[:, INNER:],
    )


def solution(mesh):
    return jax.shard_map(
        local,
        mesh=mesh,
        in_specs=(P("img", "row", "col", None), P(), P(), P("img", "row", "col", None)),
        out_specs=(
            P("img", "row", "col", None),
            P("img", "row", "col", None),
            P(("row", "col"), None),
            P(("row", "col"), None),
        ),
        check_vma=False,
    )
```

```python
import jax
import jax.numpy as jnp
from jax import lax
from jax.experimental import pallas as pl
from jax.experimental.pallas import tpu as pltpu
from jax.sharding import PartitionSpec as P

H = 8
DH = 72
INNER = H * DH
REACH = 8
WINDOW = 17
SIDE = 8
PAIRS = H // 2
SLAB = 256
V_SHIFT = 64
MASKED = -1e30
SCALE = DH ** (-0.5)


def shifted_pairs(count, by):
    return [(i, i + by) for i in range(count) if 0 <= i + by < count]


def dot(a, b):
    return jnp.dot(a, b, preferred_element_type=jnp.float32)


def nt_dot(a, b):
    return lax.dot_general(a, b, (((1,), (1,)), ((), ())), preferred_element_type=jnp.float32)


def attention_kernel(
    start_ref,
    q_ref,
    own_ref,
    g_ref,
    rows_ref,
    cols_ref,
    corner_ref,
    bias_ref,
    o_ref,
    dq_ref,
    grad_ref,
    kv,
    kvt,
    acc,
    qt,
    ot,
    dqt,
):
    strips = bias_ref.shape[0]
    chunk = kv.shape[1]
    chunk_own = own_ref.shape[0] // strips
    chunk_side = chunk - chunk_own
    band = 3 * chunk
    token_count = own_ref.shape[0]
    side_first = token_count + 2 * chunk_own
    last = strips + 1
    own_at = [token_count] + [chunk_own * s for s in range(strips)] + [token_count + chunk_own]
    side_order = [strips] + list(range(strips)) + [strips + 1]
    side_at = [side_first + chunk_side * s for s in side_order]

    def place(slot, first, part):
        count = part.shape[0]
        kv[slot, first : first + count] = part
        if count < 128:
            filler = jnp.zeros((128 - count, 2 * INNER), part.dtype)
            part = jnp.concatenate([part, filler], axis=0)
        kvt[slot, :, first : first + count] = part.T[:, :count]

    qt[...] = q_ref[...].T
    dqt[INNER:, :] = jnp.zeros((64, chunk_own), jnp.float32)
    ot[:64, :] = jnp.zeros((64, chunk_own), jnp.float32)
    for s in range(strips):
        place(s + 1, 0, own_ref[chunk_own * s : chunk_own * (s + 1)])
    for s in range(strips):
        place(s + 1, chunk_own, cols_ref[chunk_side * s : chunk_side * (s + 1)])
    for slot, at in ((0, 0), (last, 1)):
        place(slot, 0, rows_ref[chunk_own * at : chunk_own * (at + 1)])
        place(slot, chunk_own, corner_ref[chunk_side * at : chunk_side * (at + 1)])
    acc[...] = jnp.zeros_like(acc)

    row = lax.broadcasted_iota(jnp.int32, (2 * DH, chunk_own), 0)
    first_head = row < DH
    mask_a = jnp.where(first_head, 1.0, 0.0).astype(jnp.bfloat16)
    mask_b = jnp.where(first_head, 0.0, 1.0).astype(jnp.bfloat16)
    ones = jnp.ones((16, chunk), jnp.bfloat16)

    def pair_block(part, above):
        block = jnp.concatenate([part * mask_a, part * mask_b], axis=1)
        parts = [block]
        if above:
            parts = [jnp.zeros((above, block.shape[1]), block.dtype)] + parts
        below = SLAB - 2 * DH - above
        if below:
            parts = parts + [jnp.zeros((below, block.shape[1]), block.dtype)]
        return jnp.concatenate(parts, axis=0)

    def pick(both):
        return jnp.where(first_head, both[:, :chunk_own], both[:, chunk_own:])

    def strip(s, carry):
        top = start_ref[s]
        rows = pl.ds(pl.multiple_of(s * chunk_own, chunk_own), chunk_own)
        bias = bias_ref[s]
        bias = jnp.concatenate([bias, bias], axis=1)
        heads = [slice(2 * DH * i, 2 * DH * (i + 1)) for i in range(PAIRS)]
        k_lanes = [slice(128 * i, 128 * i + SLAB) for i in range(PAIRS)]
        v_lanes = [slice(512 + 128 * i, 512 + 128 * i + SLAB) for i in range(PAIRS)]

        def band_of(lanes):
            return kv[pl.ds(top, 3), :, lanes].reshape(band, SLAB)

        def from_keys(lines, weights):
            got = jnp.zeros((2 * DH, SLAB), jnp.float32)
            for j in range(3):
                got += dot(kvt[top + j, lines, :], weights[chunk * j : chunk * (j + 1)])
            return got

        q2 = [pair_block(qt[heads[i], rows], 16 * i) for i in range(PAIRS)]
        g2 = [pair_block(g_ref[heads[i], rows], V_SHIFT + 16 * i) for i in range(PAIRS)]
        prob, inv, row_dot, dscore = [], [], [], []
        for i in range(PAIRS):
            scores = dot(band_of(k_lanes[i]), q2[i]) * SCALE + bias
            top_score = jnp.max(scores, axis=0, keepdims=True)
            prob.append(jnp.exp(scores - top_score).astype(jnp.bfloat16))
        for i in range(PAIRS):
            total = jnp.zeros((16, SLAB), jnp.float32)
            for j in range(3):
                total += dot(ones, prob[i][chunk * j : chunk * (j + 1)])
            inv.append(1.0 / total[:1])
            v_rows = slice(INNER + heads[i].start, INNER + heads[i].stop)
            att = pick(from_keys(v_rows, prob[i]) * inv[i])
            ot[64 + heads[i].start : 64 + heads[i].stop, :] = att
            dots = att * g_ref[heads[i], rows].astype(jnp.float32)
            row_dot.append(
                jnp.concatenate(
                    [
                        jnp.sum(dots[:DH], axis=0, keepdims=True),
                        jnp.sum(dots[DH:], axis=0, keepdims=True),
                    ],
                    axis=1,
                )
            )
        for i in range(PAIRS):
            dprob = dot(band_of(v_lanes[i]), g2[i])
            inv_scale = inv[i] * SCALE
            change = dprob * inv_scale - row_dot[i] * inv_scale
            dscore.append((prob[i].astype(jnp.float32) * change).astype(jnp.bfloat16))
        for i in range(PAIRS):
            dv = nt_dot(prob[i], (g2[i].astype(jnp.float32) * inv[i]).astype(jnp.bfloat16))
            acc[pl.ds(top, 3), :, v_lanes[i]] += dv.reshape(3, chunk, SLAB)
        for i in range(PAIRS):
            dqt[heads[i], :] = pick(from_keys(heads[i], dscore[i]))
            dk = nt_dot(dscore[i], q2[i])
            acc[pl.ds(top, 3), :, k_lanes[i]] += dk.reshape(3, chunk, SLAB)
        o_ref[rows, :] = ot[...].T.astype(jnp.bfloat16)
        dq_ref[rows, :] = dqt[...].T.astype(jnp.bfloat16)
        return carry

    lax.fori_loop(0, strips, strip, 0)
    for slot in range(strips + 2):
        grad_ref[own_at[slot] : own_at[slot] + chunk_own, :] = acc[slot, :chunk_own].astype(
            jnp.bfloat16
        )
        grad_ref[side_at[slot] : side_at[slot] + chunk_side, :] = acc[slot, chunk_own:].astype(
            jnp.bfloat16
        )


def attention(start, projected, own, grads, rows, cols, corner, bias):
    strips, band, chunk_own = bias.shape
    chunk = band // 3
    token_count, width = own.shape
    key_count = token_count + rows.shape[0] + cols.shape[0] + corner.shape[0]
    whole = lambda a: pl.BlockSpec(a.shape, lambda _: (0,) * a.ndim)
    outs = (
        jax.ShapeDtypeStruct((token_count, INNER + 64), jnp.bfloat16),
        jax.ShapeDtypeStruct((token_count, INNER + 64), jnp.bfloat16),
        jax.ShapeDtypeStruct((key_count, width), jnp.bfloat16),
    )
    return pl.pallas_call(
        attention_kernel,
        grid=(1,),
        out_shape=outs,
        in_specs=[
            pl.BlockSpec(memory_space=pltpu.SMEM),
            pl.BlockSpec((token_count, 640), lambda _: (0, 0)),
            whole(own),
            whole(grads),
            whole(rows),
            whole(cols),
            whole(corner),
            whole(bias),
        ],
        out_specs=tuple(whole(o) for o in outs),
        scratch_shapes=[
            pltpu.VMEM((strips + 2, chunk, width), jnp.bfloat16),
            pltpu.VMEM((strips + 2, width, chunk), jnp.bfloat16),
            pltpu.VMEM((strips + 2, chunk, width), jnp.float32),
            pltpu.VMEM((640, token_count), jnp.bfloat16),
            pltpu.VMEM((640, chunk_own), jnp.float32),
            pltpu.VMEM((640, chunk_own), jnp.float32),
        ],
        compiler_params=pltpu.CompilerParams(vmem_limit_bytes=52 * 1024 * 1024),
        cost_estimate=pl.CostEstimate(
            flops=12 * token_count * band * 2 * INNER,
            bytes_accessed=16 * 1024 * 1024,
            transcendentals=token_count * band * H,
        ),
        name="window_attention",
    )(start, projected, own, grads, rows, cols, corner, bias)


def outer_kernel(own_ref, *refs):
    pairs = (len(refs) - 3) // 2
    operands, (sent_ref, kept_ref, turned) = refs[: 2 * pairs], refs[2 * pairs :]
    share = sent_ref.shape[0] // 4
    for p in range(pairs):
        turned[p] = operands[2 * p][...].T
    for out_ref, half in ((sent_ref, 1 - own_ref[0]), (kept_ref, own_ref[0])):
        products = []
        for p in range(pairs):
            picked = [
                turned[p, pl.ds(pl.multiple_of((2 * r + half) * share, 16), share), :]
                for r in range(4)
            ]
            products.append(dot(jnp.concatenate(picked, axis=0), operands[2 * p + 1][...]))
        if pairs == 1:
            out_ref[...] = products[0].astype(jnp.bfloat16)
        else:
            first, second = products
            out_ref[:, :512] = first[:, :512].astype(jnp.bfloat16)
            out_ref[:, 512:640] = (first[:, 512:] + second[:, :128]).astype(jnp.bfloat16)
            out_ref[:, 640:] = second[:, 128:].astype(jnp.bfloat16)


def outer_halves(*operands):
    rows, width = operands[0].shape
    whole = lambda a: pl.BlockSpec(a.shape, lambda _: (0,) * a.ndim)
    out = jax.ShapeDtypeStruct((width // 2, 2 * INNER), jnp.bfloat16)
    own = lax.axis_index("col").astype(jnp.int32).reshape(1)
    return pl.pallas_call(
        outer_kernel,
        grid=(1,),
        out_shape=(out, out),
        in_specs=[pl.BlockSpec(memory_space=pltpu.SMEM)] + [whole(a) for a in operands],
        out_specs=(whole(out), whole(out)),
        scratch_shapes=[pltpu.VMEM((len(operands) // 2, width, rows), jnp.bfloat16)],
        compiler_params=pltpu.CompilerParams(vmem_limit_bytes=40 * 1024 * 1024),
        cost_estimate=pl.CostEstimate(
            flops=2 * rows * width * 2 * INNER, bytes_accessed=5 * 1024 * 1024, transcendentals=0
        ),
        name="weight_grad_halves",
    )(own, *operands)


def window_starts(places, extent):
    return jnp.clip(places - REACH, 0, extent - WINDOW)


def window_bias(tile_rows, tile_cols, two_columns):
    row_id = lax.axis_index("row")
    col_id = lax.axis_index("col")
    frame_rows = tile_rows * lax.axis_size("row")
    frame_cols = tile_cols * lax.axis_size("col")
    strips = tile_rows // SIDE
    col_first = col_id * tile_cols
    strip_id = jnp.arange(strips, dtype=jnp.int32)
    first_chunk = row_id * strips - 1
    band_chunk = jnp.clip(row_id * strips + strip_id - 1, 0, frame_rows // SIDE - 3)
    side = jnp.arange(SIDE, dtype=jnp.int32)
    own_cols = col_first + jnp.arange(tile_cols, dtype=jnp.int32)
    low, high = col_first - REACH + side, col_first + tile_cols + side
    spans = [own_cols, jnp.where(col_id == 0, high, low)] if two_columns else [own_cols, low, high]
    chunk_rows = jnp.concatenate([jnp.repeat(side, span.shape[0]) for span in spans])
    chunk_cols = jnp.concatenate([jnp.tile(span, SIDE) for span in spans])
    in_band = jnp.concatenate([SIDE * j + chunk_rows for j in range(3)])
    key_col = jnp.tile(chunk_cols, 3)
    key_row = SIDE * band_chunk[:, None] + in_band[None, :]
    query_row = row_id * tile_rows + SIDE * strip_id[:, None] + jnp.repeat(side, tile_cols)[None, :]
    row_start = window_starts(query_row, frame_rows)
    col_start = window_starts(jnp.tile(own_cols, SIDE), frame_cols)
    row_off = key_row[:, :, None] - row_start[:, None, :]
    col_off = key_col[:, None] - col_start[None, :]
    row_ok = (row_off >= 0) & (row_off < WINDOW)
    col_ok = (col_off >= 0) & (col_off < WINDOW)
    bias = jnp.where(row_ok & col_ok[None], 0.0, MASKED).astype(jnp.float32)
    return (band_chunk - first_chunk).astype(jnp.int32), bias


def exchange_sum(block, axis):
    got = lax.all_to_all(block, axis, split_axis=0, concat_axis=0, tiled=True)
    return jnp.sum(got.astype(jnp.float32), axis=0).astype(jnp.bfloat16)


def image_shares(sent, kept):
    rows, images = lax.axis_size("row"), lax.axis_size("img")
    width = sent.shape[1]
    share = sent.shape[0] // rows
    kept = kept.reshape(rows, share, width)
    got = lax.ppermute(sent, "col", [(0, 1), (1, 0)]).reshape(rows, share, width)
    held = (kept.astype(jnp.float32) + got.astype(jnp.float32)).astype(jnp.bfloat16)
    small = -(-share // (8 * images)) * 8
    held = jnp.pad(held, ((0, 0), (0, images * small - share), (0, 0)))
    held = held.reshape(rows, images, small, width).transpose(1, 0, 2, 3)
    return held


def row_shares(early, late, share):
    rows, images = lax.axis_size("row"), lax.axis_size("img")
    _, small, width = early.shape
    held = exchange_sum(jnp.concatenate([early, late], axis=1), "row")
    held = jnp.broadcast_to(held[None], (images, 2 * small, width))
    held = lax.all_to_all(held, "img", split_axis=0, concat_axis=0, tiled=True)
    held = held.reshape(images, 2, small, width).astype(jnp.float32)
    early = held[:, 0].reshape(images * small, width)[:share]
    late = held[:, 1].reshape(images * small, width)[:share]
    return early, late


def plain_shares(part):
    held = lax.psum_scatter(part, ("row", "col"), scatter_dimension=0, tiled=True)
    return lax.psum(held, "img").astype(jnp.float32)


def local(tokens, qkv_weight, out_weight, upstream):
    _, tile_rows, tile_cols, width = tokens.shape
    token_count = tile_rows * tile_cols
    strips = tile_rows // SIDE
    chunk_own = SIDE * tile_cols
    row_count, col_count = lax.axis_size("row"), lax.axis_size("col")
    two_columns = col_count == 2
    col_id = lax.axis_index("col")
    token_rows = tokens.reshape(token_count, width)
    grad_rows = upstream.reshape(token_count, width)
    turns = (0,) if two_columns else (-1, 1)

    def moved(block, down, turn=None):
        pairs = []
        for r in range(row_count):
            for c in range(col_count):
                to_c = c if turn is None else (1 - c if turn == 0 else c + turn)
                if 0 <= r + down < row_count and 0 <= to_c < col_count:
                    pairs.append((r * col_count + c, (r + down) * col_count + to_c))
        return lax.ppermute(block, ("row", "col"), pairs)

    def edge(block, turn):
        if turn == 0:
            return lax.dynamic_slice_in_dim(block, (1 - col_id) * (tile_cols - REACH), REACH, 1)
        return block[:, tile_cols - REACH :] if turn == 1 else block[:, :REACH]

    def side_of(block):
        block = block.reshape(-1, tile_cols, 2 * INNER)
        got = [moved(edge(block, t), 0, t) for t in sorted(turns, reverse=True)]
        got = [g.reshape(-1, SIDE * REACH, 2 * INNER) for g in got]
        got = got[0] if two_columns else jnp.concatenate(got, axis=1)
        return got.reshape(-1, 2 * INNER)

    projected = dot(token_rows, qkv_weight).astype(jnp.bfloat16)
    keyvals = projected[:, INNER:]
    above = moved(keyvals[token_count - chunk_own :], 1)
    below = moved(keyvals[:chunk_own], -1)
    cols = side_of(keyvals)
    rows = jnp.concatenate([above, below], axis=0)
    corner = side_of(rows)
    grad_att = lax.dot_general(
        out_weight, grad_rows, (((0,), (1,)), ((), ())), preferred_element_type=jnp.float32
    ).astype(jnp.bfloat16)
    start, bias = window_bias(tile_rows, tile_cols, two_columns)
    attended, dquery, ext_grad = attention(
        start, projected, keyvals, grad_att, rows, cols, corner, bias
    )

    def outer(a, b):
        return lax.dot_general(
            a, b, (((0,), (0,)), ((), ())), preferred_element_type=jnp.float32
        ).astype(jnp.bfloat16)

    simple = two_columns and row_count == 4
    if simple:
        early = image_shares(*outer_halves(token_rows, dquery, grad_rows, attended))
        early, ext_grad = lax.optimization_barrier((early, ext_grad))
        early = exchange_sum(early, "img")
    dquery, attended = dquery[:, :INNER], attended[:, 64:]
    sublayer_out = nt_dot(attended, out_weight).astype(jnp.bfloat16)

    def spread(side, first):
        side = side.reshape(-1, SIDE, REACH, 2 * INNER).astype(jnp.float32)
        zeros = jnp.zeros((side.shape[0], SIDE, tile_cols - REACH, 2 * INNER), jnp.float32)
        order = [side, zeros] if first else [zeros, side]
        return jnp.concatenate(order, axis=2).reshape(-1, 2 * INNER)

    side_first = token_count + 2 * chunk_own
    inner_grad, side_grad = ext_grad[:side_first].astype(jnp.float32), ext_grad[side_first:]
    if two_columns:
        got = moved(side_grad, 0, 0)
        returned = jnp.where(col_id == 0, spread(got, False), spread(got, True))
    else:
        halves = side_grad.reshape(strips + 2, 2, SIDE * REACH, 2 * INNER)
        returned = spread(moved(halves[:, 0], 0, -1), False) + spread(moved(halves[:, 1], 0, 1), True)
    inner_grad = inner_grad + returned
    dkv = inner_grad[:token_count]
    to_above = inner_grad[token_count : token_count + chunk_own].astype(jnp.bfloat16)
    to_below = inner_grad[token_count + chunk_own :].astype(jnp.bfloat16)
    from_below = moved(to_above, -1).astype(jnp.float32)
    from_above = moved(to_below, 1).astype(jnp.float32)
    rest = jnp.zeros((token_count - chunk_own, 2 * INNER), jnp.float32)
    dkv = dkv + jnp.concatenate([from_above, rest], axis=0)
    dkv = dkv + jnp.concatenate([rest, from_below], axis=0)
    dkv = dkv.astype(jnp.bfloat16)
    if simple:
        late = exchange_sum(image_shares(*outer_halves(token_rows, dkv)), "img")
        early, late = row_shares(early, late, width // (row_count * col_count))
    else:
        early = jnp.concatenate([outer(token_rows, dquery), outer(grad_rows, attended)], axis=1)
        early, late = plain_shares(early), plain_shares(outer(token_rows, dkv))
    dqkv = jnp.concatenate([dquery, dkv], axis=1)
    tokens_grad = nt_dot(dqkv, qkv_weight).astype(jnp.bfloat16)
    return (
        sublayer_out.reshape(tokens.shape),
        tokens_grad.reshape(tokens.shape),
        jnp.concatenate([early[:, :INNER], late], axis=1),
        early[:, INNER:],
    )


def solution(mesh):
    return jax.shard_map(
        local,
        mesh=mesh,
        in_specs=(P("img", "row", "col", None), P(), P(), P("img", "row", "col", None)),
        out_specs=(
            P("img", "row", "col", None),
            P("img", "row", "col", None),
            P(("row", "col"), None),
            P(("row", "col"), None),
        ),
        check_vma=False,
    )
```

```python
import jax
import jax.numpy as jnp
from jax import lax
from jax.experimental import pallas as pl
from jax.experimental.pallas import tpu as pltpu
from jax.sharding import PartitionSpec as P

H = 8
DH = 72
INNER = H * DH
REACH = 8
WINDOW = 17
SIDE = 8
PAIRS = H // 2
SLAB = 256
V_SHIFT = 64
MASKED = -1e30
SCALE = DH ** (-0.5)


def shifted_pairs(count, by):
    return [(i, i + by) for i in range(count) if 0 <= i + by < count]


def dot(a, b):
    return jnp.dot(a, b, preferred_element_type=jnp.float32)


def nt_dot(a, b):
    return lax.dot_general(a, b, (((1,), (1,)), ((), ())), preferred_element_type=jnp.float32)


def attention_kernel(
    start_ref,
    q_ref,
    own_ref,
    g_ref,
    rows_ref,
    cols_ref,
    corner_ref,
    bias_ref,
    o_ref,
    dq_ref,
    grad_ref,
    kv,
    kvt,
    acc,
    qt,
    ot,
    dqt,
):
    strips = bias_ref.shape[0]
    chunk = kv.shape[1]
    chunk_own = own_ref.shape[0] // strips
    chunk_side = chunk - chunk_own
    band = 3 * chunk
    token_count = own_ref.shape[0]
    side_first = token_count + 2 * chunk_own
    last = strips + 1
    own_at = [token_count] + [chunk_own * s for s in range(strips)] + [token_count + chunk_own]
    side_order = [strips] + list(range(strips)) + [strips + 1]
    side_at = [side_first + chunk_side * s for s in side_order]

    def place(slot, first, part):
        count = part.shape[0]
        kv[slot, first : first + count] = part
        if count < 128:
            filler = jnp.zeros((128 - count, 2 * INNER), part.dtype)
            part = jnp.concatenate([part, filler], axis=0)
        kvt[slot, :, first : first + count] = part.T[:, :count]

    qt[...] = q_ref[...].T
    dqt[INNER:, :] = jnp.zeros((64, chunk_own), jnp.float32)
    ot[:64, :] = jnp.zeros((64, chunk_own), jnp.float32)
    for s in range(strips):
        place(s + 1, 0, own_ref[chunk_own * s : chunk_own * (s + 1)])
    for s in range(strips):
        place(s + 1, chunk_own, cols_ref[chunk_side * s : chunk_side * (s + 1)])
    for slot, at in ((0, 0), (last, 1)):
        place(slot, 0, rows_ref[chunk_own * at : chunk_own * (at + 1)])
        place(slot, chunk_own, corner_ref[chunk_side * at : chunk_side * (at + 1)])
    acc[...] = jnp.zeros_like(acc)

    row = lax.broadcasted_iota(jnp.int32, (2 * DH, chunk_own), 0)
    first_head = row < DH
    mask_a = jnp.where(first_head, 1.0, 0.0).astype(jnp.bfloat16)
    mask_b = jnp.where(first_head, 0.0, 1.0).astype(jnp.bfloat16)
    ones = jnp.ones((16, chunk), jnp.bfloat16)

    def pair_block(part, above):
        block = jnp.concatenate([part * mask_a, part * mask_b], axis=1)
        parts = [block]
        if above:
            parts = [jnp.zeros((above, block.shape[1]), block.dtype)] + parts
        below = SLAB - 2 * DH - above
        if below:
            parts = parts + [jnp.zeros((below, block.shape[1]), block.dtype)]
        return jnp.concatenate(parts, axis=0)

    def pick(both):
        return jnp.where(first_head, both[:, :chunk_own], both[:, chunk_own:])

    def strip(s, carry):
        top = start_ref[s]
        rows = pl.ds(pl.multiple_of(s * chunk_own, chunk_own), chunk_own)
        bias = bias_ref[s]
        bias = jnp.concatenate([bias, bias], axis=1)
        heads = [slice(2 * DH * i, 2 * DH * (i + 1)) for i in range(PAIRS)]
        k_lanes = [slice(128 * i, 128 * i + SLAB) for i in range(PAIRS)]
        v_lanes = [slice(512 + 128 * i, 512 + 128 * i + SLAB) for i in range(PAIRS)]

        def band_of(lanes):
            return kv[pl.ds(top, 3), :, lanes].reshape(band, SLAB)

        def from_keys(lines, weights):
            got = jnp.zeros((2 * DH, SLAB), jnp.float32)
            for j in range(3):
                got += dot(kvt[top + j, lines, :], weights[chunk * j : chunk * (j + 1)])
            return got

        q2 = [pair_block(qt[heads[i], rows], 16 * i) for i in range(PAIRS)]
        g2 = [pair_block(g_ref[heads[i], rows], V_SHIFT + 16 * i) for i in range(PAIRS)]
        prob, inv, row_dot, dscore = [], [], [], []
        for i in range(PAIRS):
            scores = dot(band_of(k_lanes[i]), q2[i]) * SCALE + bias
            top_score = jnp.max(scores, axis=0, keepdims=True)
            prob.append(jnp.exp(scores - top_score).astype(jnp.bfloat16))
        for i in range(PAIRS):
            total = jnp.zeros((16, SLAB), jnp.float32)
            for j in range(3):
                total += dot(ones, prob[i][chunk * j : chunk * (j + 1)])
            inv.append(1.0 / total[:1])
            v_rows = slice(INNER + heads[i].start, INNER + heads[i].stop)
            att = pick(from_keys(v_rows, prob[i]) * inv[i])
            ot[64 + heads[i].start : 64 + heads[i].stop, :] = att
            dots = att * g_ref[heads[i], rows].astype(jnp.float32)
            row_dot.append(
                jnp.concatenate(
                    [
                        jnp.sum(dots[:DH], axis=0, keepdims=True),
                        jnp.sum(dots[DH:], axis=0, keepdims=True),
                    ],
                    axis=1,
                )
            )
        for i in range(PAIRS):
            dprob = dot(band_of(v_lanes[i]), g2[i])
            inv_scale = inv[i] * SCALE
            change = dprob * inv_scale - row_dot[i] * inv_scale
            dscore.append((prob[i].astype(jnp.float32) * change).astype(jnp.bfloat16))
        for i in range(PAIRS):
            dv = nt_dot(prob[i], (g2[i].astype(jnp.float32) * inv[i]).astype(jnp.bfloat16))
            acc[pl.ds(top, 3), :, v_lanes[i]] += dv.reshape(3, chunk, SLAB)
        for i in range(PAIRS):
            dqt[heads[i], :] = pick(from_keys(heads[i], dscore[i]))
            dk = nt_dot(dscore[i], q2[i])
            acc[pl.ds(top, 3), :, k_lanes[i]] += dk.reshape(3, chunk, SLAB)
        o_ref[rows, :] = ot[...].T.astype(jnp.bfloat16)
        dq_ref[rows, :] = dqt[...].T.astype(jnp.bfloat16)
        return carry

    lax.fori_loop(0, strips, strip, 0)
    for slot in range(strips + 2):
        grad_ref[own_at[slot] : own_at[slot] + chunk_own, :] = acc[slot, :chunk_own].astype(
            jnp.bfloat16
        )
        grad_ref[side_at[slot] : side_at[slot] + chunk_side, :] = acc[slot, chunk_own:].astype(
            jnp.bfloat16
        )


def attention(start, projected, own, grads, rows, cols, corner, bias):
    strips, band, chunk_own = bias.shape
    chunk = band // 3
    token_count, width = own.shape
    key_count = token_count + rows.shape[0] + cols.shape[0] + corner.shape[0]
    whole = lambda a: pl.BlockSpec(a.shape, lambda _: (0,) * a.ndim)
    outs = (
        jax.ShapeDtypeStruct((token_count, INNER + 64), jnp.bfloat16),
        jax.ShapeDtypeStruct((token_count, INNER + 64), jnp.bfloat16),
        jax.ShapeDtypeStruct((key_count, width), jnp.bfloat16),
    )
    return pl.pallas_call(
        attention_kernel,
        grid=(1,),
        out_shape=outs,
        in_specs=[
            pl.BlockSpec(memory_space=pltpu.SMEM),
            pl.BlockSpec((token_count, 640), lambda _: (0, 0)),
            whole(own),
            whole(grads),
            whole(rows),
            whole(cols),
            whole(corner),
            whole(bias),
        ],
        out_specs=tuple(whole(o) for o in outs),
        scratch_shapes=[
            pltpu.VMEM((strips + 2, chunk, width), jnp.bfloat16),
            pltpu.VMEM((strips + 2, width, chunk), jnp.bfloat16),
            pltpu.VMEM((strips + 2, chunk, width), jnp.float32),
            pltpu.VMEM((640, token_count), jnp.bfloat16),
            pltpu.VMEM((640, chunk_own), jnp.float32),
            pltpu.VMEM((640, chunk_own), jnp.float32),
        ],
        compiler_params=pltpu.CompilerParams(vmem_limit_bytes=52 * 1024 * 1024),
        cost_estimate=pl.CostEstimate(
            flops=12 * token_count * band * 2 * INNER,
            bytes_accessed=16 * 1024 * 1024,
            transcendentals=token_count * band * H,
        ),
        name="window_attention",
    )(start, projected, own, grads, rows, cols, corner, bias)


def outer_kernel(own_ref, *refs):
    pairs = (len(refs) - 3) // 2
    operands, (sent_ref, kept_ref, turned) = refs[: 2 * pairs], refs[2 * pairs :]
    share = sent_ref.shape[0] // 4
    for p in range(pairs):
        turned[p] = operands[2 * p][...].T
    for out_ref, half in ((sent_ref, 1 - own_ref[0]), (kept_ref, own_ref[0])):
        products = []
        for p in range(pairs):
            picked = [
                turned[p, pl.ds(pl.multiple_of((2 * r + half) * share, 16), share), :]
                for r in range(4)
            ]
            products.append(dot(jnp.concatenate(picked, axis=0), operands[2 * p + 1][...]))
        if pairs == 1:
            out_ref[...] = products[0].astype(jnp.bfloat16)
        else:
            first, second = products
            out_ref[:, :512] = first[:, :512].astype(jnp.bfloat16)
            out_ref[:, 512:640] = (first[:, 512:] + second[:, :128]).astype(jnp.bfloat16)
            out_ref[:, 640:] = second[:, 128:].astype(jnp.bfloat16)


def outer_halves(*operands):
    rows, width = operands[0].shape
    whole = lambda a: pl.BlockSpec(a.shape, lambda _: (0,) * a.ndim)
    out = jax.ShapeDtypeStruct((width // 2, 2 * INNER), jnp.bfloat16)
    own = lax.axis_index("col").astype(jnp.int32).reshape(1)
    return pl.pallas_call(
        outer_kernel,
        grid=(1,),
        out_shape=(out, out),
        in_specs=[pl.BlockSpec(memory_space=pltpu.SMEM)] + [whole(a) for a in operands],
        out_specs=(whole(out), whole(out)),
        scratch_shapes=[pltpu.VMEM((len(operands) // 2, width, rows), jnp.bfloat16)],
        compiler_params=pltpu.CompilerParams(vmem_limit_bytes=40 * 1024 * 1024),
        cost_estimate=pl.CostEstimate(
            flops=2 * rows * width * 2 * INNER, bytes_accessed=5 * 1024 * 1024, transcendentals=0
        ),
        name="weight_grad_halves",
    )(own, *operands)


def late_kernel(
    own_ref, first, second, third, tokens_ref, inner_ref, side_ref, above_ref, below_ref,
    sent_ref, kept_ref, grad_ref, turned,
):
    own = own_ref[0]
    count = inner_ref.shape[0]
    share = sent_ref.shape[0] // 4
    edge = above_ref.shape[0]
    width = inner_ref.shape[1]
    side = side_ref[: count // 2].astype(jnp.float32).reshape(-1, REACH, width)
    is_left = (own == 0).astype(jnp.float32)
    side = jnp.concatenate([side * (1.0 - is_left), side * is_left], axis=1)
    total = inner_ref[...].astype(jnp.float32) + side.reshape(count, width)
    grad_ref[:edge] = (total[:edge] + above_ref[...].astype(jnp.float32)).astype(jnp.bfloat16)
    grad_ref[edge : count - edge] = total[edge : count - edge].astype(jnp.bfloat16)
    grad_ref[count - edge :] = (
        total[count - edge :] + below_ref[...].astype(jnp.float32)
    ).astype(jnp.bfloat16)
    turned[...] = tokens_ref[...].T
    for out_ref, half in ((sent_ref, 1 - own), (kept_ref, own)):
        picked = [
            turned[pl.ds(pl.multiple_of((2 * r + half) * share, 16), share), :] for r in range(4)
        ]
        product = dot(jnp.concatenate(picked, axis=0), grad_ref[...])
        out_ref[...] = product.astype(jnp.bfloat16)


def late_halves(earlier, token_rows, ext_grad, side, above, below):
    rows, width = token_rows.shape
    whole = lambda a: pl.BlockSpec(a.shape, lambda _: (0,) * a.ndim)
    out = jax.ShapeDtypeStruct((width // 2, 2 * INNER), jnp.bfloat16)
    grad = jax.ShapeDtypeStruct((rows, 2 * INNER), jnp.bfloat16)
    own = lax.axis_index("col").astype(jnp.int32).reshape(1)
    return pl.pallas_call(
        late_kernel,
        grid=(1,),
        out_shape=(out, out, grad),
        in_specs=[pl.BlockSpec(memory_space=pltpu.SMEM)]
        + [pl.BlockSpec(memory_space=pl.ANY)] * 3
        + [whole(token_rows), whole(grad), whole(side), whole(above), whole(below)],
        out_specs=(whole(out), whole(out), whole(grad)),
        scratch_shapes=[pltpu.VMEM((width, rows), jnp.bfloat16)],
        compiler_params=pltpu.CompilerParams(vmem_limit_bytes=40 * 1024 * 1024),
        cost_estimate=pl.CostEstimate(
            flops=2 * rows * width * 2 * INNER, bytes_accessed=7 * 1024 * 1024, transcendentals=0
        ),
        name="late_weight_grad_halves",
    )(own, *earlier, token_rows, ext_grad, side, above, below)


def window_starts(places, extent):
    return jnp.clip(places - REACH, 0, extent - WINDOW)


def window_bias(tile_rows, tile_cols, two_columns):
    row_id = lax.axis_index("row")
    col_id = lax.axis_index("col")
    frame_rows = tile_rows * lax.axis_size("row")
    frame_cols = tile_cols * lax.axis_size("col")
    strips = tile_rows // SIDE
    col_first = col_id * tile_cols
    strip_id = jnp.arange(strips, dtype=jnp.int32)
    first_chunk = row_id * strips - 1
    band_chunk = jnp.clip(row_id * strips + strip_id - 1, 0, frame_rows // SIDE - 3)
    side = jnp.arange(SIDE, dtype=jnp.int32)
    own_cols = col_first + jnp.arange(tile_cols, dtype=jnp.int32)
    low, high = col_first - REACH + side, col_first + tile_cols + side
    spans = [own_cols, jnp.where(col_id == 0, high, low)] if two_columns else [own_cols, low, high]
    chunk_rows = jnp.concatenate([jnp.repeat(side, span.shape[0]) for span in spans])
    chunk_cols = jnp.concatenate([jnp.tile(span, SIDE) for span in spans])
    in_band = jnp.concatenate([SIDE * j + chunk_rows for j in range(3)])
    key_col = jnp.tile(chunk_cols, 3)
    key_row = SIDE * band_chunk[:, None] + in_band[None, :]
    query_row = row_id * tile_rows + SIDE * strip_id[:, None] + jnp.repeat(side, tile_cols)[None, :]
    row_start = window_starts(query_row, frame_rows)
    col_start = window_starts(jnp.tile(own_cols, SIDE), frame_cols)
    row_off = key_row[:, :, None] - row_start[:, None, :]
    col_off = key_col[:, None] - col_start[None, :]
    row_ok = (row_off >= 0) & (row_off < WINDOW)
    col_ok = (col_off >= 0) & (col_off < WINDOW)
    bias = jnp.where(row_ok & col_ok[None], 0.0, MASKED).astype(jnp.float32)
    return (band_chunk - first_chunk).astype(jnp.int32), bias


def after(value, *earlier):
    return lax.optimization_barrier((value,) + earlier)[0]


def cut(block, axis, take):
    own = lax.axis_index(axis)
    return [take(block, own ^ step) for step in range(lax.axis_size(axis))]


def exchange_sum(parts, axis, *earlier):
    kept, got = parts[0], []
    for step, part in enumerate(parts[1:], 1):
        pairs = [(i, i ^ step) for i in range(lax.axis_size(axis))]
        got.append(lax.ppermute(part, axis, pairs))
    if earlier:
        kept = after(kept, *earlier)
    total = kept.astype(jnp.float32)
    for g in got:
        total += g.astype(jnp.float32)
    return total.astype(jnp.bfloat16)


def gathered(block, axis):
    own = lax.axis_index(axis)
    count = lax.axis_size(axis)
    whole = jnp.zeros((count,) + block.shape, block.dtype)
    whole = lax.dynamic_update_index_in_dim(whole, block, own, 0)
    for step in range(1, count):
        got = lax.ppermute(block, axis, [(i, i ^ step) for i in range(count)])
        whole = lax.dynamic_update_index_in_dim(whole, got, own ^ step, 0)
    return whole


def core_sum(sent, kept):
    rows, images = lax.axis_size("row"), lax.axis_size("img")
    width = sent.shape[1]
    share = sent.shape[0] // rows
    kept = kept.reshape(rows, share, width)
    got = lax.ppermute(sent, "col", [(0, 1), (1, 0)]).reshape(rows, share, width)
    held = (kept.astype(jnp.float32) + got.astype(jnp.float32)).astype(jnp.bfloat16)
    small = -(-share // (8 * images)) * 8
    return jnp.pad(held, ((0, 0), (0, images * small - share), (0, 0)))


def image_parts(held):
    small = held.shape[1] // lax.axis_size("img")
    return cut(held, "img", lambda h, j: lax.dynamic_slice_in_dim(h, small * j, small, 1))


def row_parts(held):
    return cut(held, "row", lambda h, r: lax.dynamic_index_in_dim(h, r, 0, keepdims=False))


def whole_share(held, share):
    whole = gathered(held, "img")
    return whole.reshape(-1, held.shape[1])[:share].astype(jnp.float32)


def plain_shares(part):
    held = lax.psum_scatter(part, ("row", "col"), scatter_dimension=0, tiled=True)
    return lax.psum(held, "img").astype(jnp.float32)


def local(tokens, qkv_weight, out_weight, upstream):
    _, tile_rows, tile_cols, width = tokens.shape
    token_count = tile_rows * tile_cols
    strips = tile_rows // SIDE
    chunk_own = SIDE * tile_cols
    row_count, col_count = lax.axis_size("row"), lax.axis_size("col")
    two_columns = col_count == 2
    col_id = lax.axis_index("col")
    token_rows = tokens.reshape(token_count, width)
    grad_rows = upstream.reshape(token_count, width)
    turns = (0,) if two_columns else (-1, 1)

    def moved(block, down, turn=None):
        pairs = []
        for r in range(row_count):
            for c in range(col_count):
                to_c = c if turn is None else (1 - c if turn == 0 else c + turn)
                if 0 <= r + down < row_count and 0 <= to_c < col_count:
                    pairs.append((r * col_count + c, (r + down) * col_count + to_c))
        return lax.ppermute(block, ("row", "col"), pairs)

    def edge(block, turn):
        if turn == 0:
            return lax.dynamic_slice_in_dim(block, (1 - col_id) * (tile_cols - REACH), REACH, 1)
        return block[:, tile_cols - REACH :] if turn == 1 else block[:, :REACH]

    def side_of(block):
        block = block.reshape(-1, tile_cols, 2 * INNER)
        got = [moved(edge(block, t), 0, t) for t in sorted(turns, reverse=True)]
        got = [g.reshape(-1, SIDE * REACH, 2 * INNER) for g in got]
        got = got[0] if two_columns else jnp.concatenate(got, axis=1)
        return got.reshape(-1, 2 * INNER)

    projected = dot(token_rows, qkv_weight).astype(jnp.bfloat16)
    keyvals = projected[:, INNER:]
    above = moved(keyvals[token_count - chunk_own :], 1)
    below = moved(keyvals[:chunk_own], -1)
    cols = side_of(keyvals)
    rows = jnp.concatenate([above, below], axis=0)
    corner = side_of(rows)
    grad_att = lax.dot_general(
        out_weight, grad_rows, (((0,), (1,)), ((), ())), preferred_element_type=jnp.float32
    ).astype(jnp.bfloat16)
    start, bias = window_bias(tile_rows, tile_cols, two_columns)
    attended, dquery, ext_grad = attention(
        start, projected, keyvals, grad_att, rows, cols, corner, bias
    )

    def outer(a, b):
        return lax.dot_general(
            a, b, (((0,), (0,)), ((), ())), preferred_element_type=jnp.float32
        ).astype(jnp.bfloat16)

    simple = two_columns and row_count == 4 and lax.axis_size("img") == 4
    if simple:
        early = image_parts(core_sum(*outer_halves(token_rows, dquery, grad_rows, attended)))
    dquery, attended = dquery[:, :INNER], attended[:, 64:]
    sublayer_out = nt_dot(attended, out_weight).astype(jnp.bfloat16)

    def spread(side, first):
        side = side.reshape(-1, SIDE, REACH, 2 * INNER).astype(jnp.float32)
        zeros = jnp.zeros((side.shape[0], SIDE, tile_cols - REACH, 2 * INNER), jnp.float32)
        order = [side, zeros] if first else [zeros, side]
        return jnp.concatenate(order, axis=2).reshape(-1, 2 * INNER)

    side_first = token_count + 2 * chunk_own
    side_grad = ext_grad[side_first:]
    if two_columns:
        got = moved(side_grad, 0, 0)
        returned = lambda part: jnp.where(col_id == 0, spread(part, False), spread(part, True))
    else:
        halves = side_grad.reshape(strips + 2, 2, SIDE * REACH, 2 * INNER)
        got = jnp.stack([moved(halves[:, 0], 0, -1), moved(halves[:, 1], 0, 1)], axis=1)
        returned = lambda part: spread(part[:, 0], False) + spread(part[:, 1], True)
    got = got.reshape(strips + 2, -1, SIDE * REACH, 2 * INNER)
    outer_grad = ext_grad[token_count:side_first].astype(jnp.float32) + returned(got[strips:])
    outer_grad = outer_grad.astype(jnp.bfloat16)
    from_below = moved(outer_grad[:chunk_own], -1)
    from_above = moved(outer_grad[chunk_own:], 1)
    if simple:
        side = got.reshape(-1, 2 * INNER)
        sent, kept, dkv = late_halves(early[1:], token_rows, ext_grad, side, from_above, from_below)
    else:
        dkv = ext_grad[:token_count].astype(jnp.float32) + returned(got[:strips])
        rest = jnp.zeros((token_count - chunk_own, 2 * INNER), jnp.float32)
        dkv = dkv + jnp.concatenate([from_above.astype(jnp.float32), rest], axis=0)
        dkv = dkv + jnp.concatenate([rest, from_below.astype(jnp.float32)], axis=0)
        dkv = dkv.astype(jnp.bfloat16)
    if simple:
        late = image_parts(core_sum(sent, kept))
        early = exchange_sum(early, "img")
        late = exchange_sum(late, "img", early)
        early = exchange_sum(row_parts(early), "row")
        late = exchange_sum(row_parts(late), "row", early)
        share = width // (row_count * col_count)
        early, late = whole_share(early, share), whole_share(late, share)
    else:
        early = jnp.concatenate([outer(token_rows, dquery), outer(grad_rows, attended)], axis=1)
        early, late = plain_shares(early), plain_shares(outer(token_rows, dkv))
    dqkv = jnp.concatenate([dquery, dkv], axis=1)
    tokens_grad = nt_dot(dqkv, qkv_weight).astype(jnp.bfloat16)
    return (
        sublayer_out.reshape(tokens.shape),
        tokens_grad.reshape(tokens.shape),
        jnp.concatenate([early[:, :INNER], late], axis=1),
        early[:, INNER:],
    )


def solution(mesh):
    return jax.shard_map(
        local,
        mesh=mesh,
        in_specs=(P("img", "row", "col", None), P(), P(), P("img", "row", "col", None)),
        out_specs=(
            P("img", "row", "col", None),
            P("img", "row", "col", None),
            P(("row", "col"), None),
            P(("row", "col"), None),
        ),
        check_vma=False,
    )
```

```python
import jax
import jax.numpy as jnp
from jax import lax
from jax.experimental import pallas as pl
from jax.experimental.pallas import tpu as pltpu
from jax.sharding import PartitionSpec as P

H = 8
DH = 72
INNER = H * DH
REACH = 8
WINDOW = 17
SIDE = 8
PAIRS = H // 2
SLAB = 256
V_SHIFT = 64
MASKED = -1e30
SCALE = DH ** (-0.5)


def shifted_pairs(count, by):
    return [(i, i + by) for i in range(count) if 0 <= i + by < count]


def dot(a, b):
    return jnp.dot(a, b, preferred_element_type=jnp.float32)


def nt_dot(a, b):
    return lax.dot_general(a, b, (((1,), (1,)), ((), ())), preferred_element_type=jnp.float32)


def project_kernel(
    own_ref, tokens_ref, weight_ref, qt_ref, kv_ref, top_ref, bottom_ref, near_ref, total
):
    step = pl.program_id(0)
    part = dot(tokens_ref[...], weight_ref[...])

    @pl.when(step == 0)
    def _():
        total[...] = part

    @pl.when(step > 0)
    def _():
        total[...] += part

    @pl.when(step == pl.num_programs(0) - 1)
    def _():
        count, edge = kv_ref.shape[0], top_ref.shape[0]
        qt_ref[...] = total[:, : INNER + 64].astype(jnp.bfloat16).T
        keyvals = total[:, INNER - 64 :].astype(jnp.bfloat16)[:, 64:]
        kv_ref[...] = keyvals
        top_ref[...] = keyvals[:edge]
        bottom_ref[...] = keyvals[count - edge :]
        grid = keyvals.astype(jnp.float32).reshape(-1, edge // SIDE, 2 * INNER)
        is_right = own_ref[0].astype(jnp.float32)
        near = grid[:, :REACH] * is_right + grid[:, -REACH:] * (1.0 - is_right)
        near_ref[...] = near.reshape(near_ref.shape).astype(jnp.bfloat16)


def project(token_rows, weight, tile_cols):
    rows, width = token_rows.shape
    steps = 3
    depth = width // steps
    chunk_own = SIDE * tile_cols
    own = lax.axis_index("col").astype(jnp.int32).reshape(1)
    shapes = [
        (INNER + 64, rows),
        (rows, 2 * INNER),
        (chunk_own, 2 * INNER),
        (chunk_own, 2 * INNER),
        (rows // tile_cols * REACH, 2 * INNER),
    ]
    return pl.pallas_call(
        project_kernel,
        grid=(steps,),
        out_shape=[jax.ShapeDtypeStruct(shape, jnp.bfloat16) for shape in shapes],
        in_specs=[
            pl.BlockSpec(memory_space=pltpu.SMEM),
            pl.BlockSpec((rows, depth), lambda k: (0, k)),
            pl.BlockSpec((depth, weight.shape[1]), lambda k: (k, 0)),
        ],
        out_specs=[pl.BlockSpec(shape, lambda k: (0, 0)) for shape in shapes],
        scratch_shapes=[pltpu.VMEM((rows, weight.shape[1]), jnp.float32)],
        compiler_params=pltpu.CompilerParams(vmem_limit_bytes=32 * 1024 * 1024),
        cost_estimate=pl.CostEstimate(
            flops=2 * rows * width * weight.shape[1], bytes_accessed=8 * 1024 * 1024, transcendentals=0
        ),
        name="project",
    )(own, token_rows, weight)


def attention_kernel(
    start_ref,
    qt_ref,
    own_ref,
    g_ref,
    rows_ref,
    cols_ref,
    corner_ref,
    bias_ref,
    o_ref,
    dq_ref,
    inner_ref,
    edge_ref,
    side_ref,
    kv,
    kvt,
    acc,
    ot,
    dqt,
):
    strips = bias_ref.shape[0]
    chunk = kv.shape[1]
    chunk_own = own_ref.shape[0] // strips
    chunk_side = chunk - chunk_own
    band = 3 * chunk
    token_count = own_ref.shape[0]
    last = strips + 1
    side_order = [strips] + list(range(strips)) + [strips + 1]

    def place(slot, first, part):
        count = part.shape[0]
        kv[slot, first : first + count] = part
        if count < 128:
            filler = jnp.zeros((128 - count, 2 * INNER), part.dtype)
            part = jnp.concatenate([part, filler], axis=0)
        kvt[slot, :, first : first + count] = part.T[:, :count]

    dqt[INNER:, :] = jnp.zeros((64, chunk_own), jnp.float32)
    ot[:64, :] = jnp.zeros((64, chunk_own), jnp.float32)
    for s in range(strips):
        place(s + 1, 0, own_ref[chunk_own * s : chunk_own * (s + 1)])
    for s in range(strips):
        place(s + 1, chunk_own, cols_ref[chunk_side * s : chunk_side * (s + 1)])
    for slot, at in ((0, 0), (last, 1)):
        place(slot, 0, rows_ref[chunk_own * at : chunk_own * (at + 1)])
        place(slot, chunk_own, corner_ref[chunk_side * at : chunk_side * (at + 1)])
    acc[...] = jnp.zeros_like(acc)

    row = lax.broadcasted_iota(jnp.int32, (2 * DH, chunk_own), 0)
    first_head = row < DH
    mask_a = jnp.where(first_head, 1.0, 0.0).astype(jnp.bfloat16)
    mask_b = jnp.where(first_head, 0.0, 1.0).astype(jnp.bfloat16)
    ones = jnp.ones((16, chunk), jnp.bfloat16)

    def pair_block(part, above):
        block = jnp.concatenate([part * mask_a, part * mask_b], axis=1)
        parts = [block]
        if above:
            parts = [jnp.zeros((above, block.shape[1]), block.dtype)] + parts
        below = SLAB - 2 * DH - above
        if below:
            parts = parts + [jnp.zeros((below, block.shape[1]), block.dtype)]
        return jnp.concatenate(parts, axis=0)

    def pick(both):
        return jnp.where(first_head, both[:, :chunk_own], both[:, chunk_own:])

    def strip(s, carry):
        top = start_ref[s]
        rows = pl.ds(pl.multiple_of(s * chunk_own, chunk_own), chunk_own)
        bias = bias_ref[s]
        bias = jnp.concatenate([bias, bias], axis=1)
        heads = [slice(2 * DH * i, 2 * DH * (i + 1)) for i in range(PAIRS)]
        k_lanes = [slice(128 * i, 128 * i + SLAB) for i in range(PAIRS)]
        v_lanes = [slice(512 + 128 * i, 512 + 128 * i + SLAB) for i in range(PAIRS)]

        def band_of(lanes):
            return kv[pl.ds(top, 3), :, lanes].reshape(band, SLAB)

        def from_keys(lines, weights):
            got = jnp.zeros((2 * DH, SLAB), jnp.float32)
            for j in range(3):
                got += dot(kvt[top + j, lines, :], weights[chunk * j : chunk * (j + 1)])
            return got

        q2 = [pair_block(qt_ref[heads[i], rows], 16 * i) for i in range(PAIRS)]
        g2 = [pair_block(g_ref[heads[i], rows], V_SHIFT + 16 * i) for i in range(PAIRS)]
        prob, inv, row_dot, dscore = [], [], [], []
        for i in range(PAIRS):
            scores = dot(band_of(k_lanes[i]), q2[i]) * SCALE + bias
            top_score = jnp.max(scores, axis=0, keepdims=True)
            prob.append(jnp.exp(scores - top_score).astype(jnp.bfloat16))
        for i in range(PAIRS):
            total = jnp.zeros((16, SLAB), jnp.float32)
            for j in range(3):
                total += dot(ones, prob[i][chunk * j : chunk * (j + 1)])
            inv.append(1.0 / total[:1])
            v_rows = slice(INNER + heads[i].start, INNER + heads[i].stop)
            att = pick(from_keys(v_rows, prob[i]) * inv[i])
            ot[64 + heads[i].start : 64 + heads[i].stop, :] = att
            dots = att * g_ref[heads[i], rows].astype(jnp.float32)
            row_dot.append(
                jnp.concatenate(
                    [
                        jnp.sum(dots[:DH], axis=0, keepdims=True),
                        jnp.sum(dots[DH:], axis=0, keepdims=True),
                    ],
                    axis=1,
                )
            )
        for i in range(PAIRS):
            dprob = dot(band_of(v_lanes[i]), g2[i])
            inv_scale = inv[i] * SCALE
            change = dprob * inv_scale - row_dot[i] * inv_scale
            dscore.append((prob[i].astype(jnp.float32) * change).astype(jnp.bfloat16))
        for i in range(PAIRS):
            dv = nt_dot(prob[i], (g2[i].astype(jnp.float32) * inv[i]).astype(jnp.bfloat16))
            acc[pl.ds(top, 3), :, v_lanes[i]] += dv.reshape(3, chunk, SLAB)
        for i in range(PAIRS):
            dqt[heads[i], :] = pick(from_keys(heads[i], dscore[i]))
            dk = nt_dot(dscore[i], q2[i])
            acc[pl.ds(top, 3), :, k_lanes[i]] += dk.reshape(3, chunk, SLAB)
        o_ref[rows, :] = ot[...].T.astype(jnp.bfloat16)
        dq_ref[rows, :] = dqt[...].T.astype(jnp.bfloat16)
        return carry

    lax.fori_loop(0, strips, strip, 0)
    for slot, at in enumerate(side_order):
        own_grad = acc[slot, :chunk_own].astype(jnp.bfloat16)
        if at < strips:
            inner_ref[chunk_own * at : chunk_own * (at + 1), :] = own_grad
        else:
            edge_ref[chunk_own * (at - strips) : chunk_own * (at - strips + 1), :] = own_grad
        side_ref[chunk_side * at : chunk_side * (at + 1), :] = acc[slot, chunk_own:].astype(
            jnp.bfloat16
        )


def attention(start, queries, own, grads, rows, cols, corner, bias):
    strips, band, chunk_own = bias.shape
    chunk = band // 3
    token_count, width = own.shape
    whole = lambda a: pl.BlockSpec(a.shape, lambda _: (0,) * a.ndim)
    outs = (
        jax.ShapeDtypeStruct((token_count, INNER + 64), jnp.bfloat16),
        jax.ShapeDtypeStruct((token_count, INNER + 64), jnp.bfloat16),
        jax.ShapeDtypeStruct(own.shape, jnp.bfloat16),
        jax.ShapeDtypeStruct(rows.shape, jnp.bfloat16),
        jax.ShapeDtypeStruct((cols.shape[0] + corner.shape[0], width), jnp.bfloat16),
    )
    return pl.pallas_call(
        attention_kernel,
        grid=(1,),
        out_shape=outs,
        in_specs=[
            pl.BlockSpec(memory_space=pltpu.SMEM),
            whole(queries),
            whole(own),
            whole(grads),
            whole(rows),
            whole(cols),
            whole(corner),
            whole(bias),
        ],
        out_specs=tuple(whole(o) for o in outs),
        scratch_shapes=[
            pltpu.VMEM((strips + 2, chunk, width), jnp.bfloat16),
            pltpu.VMEM((strips + 2, width, chunk), jnp.bfloat16),
            pltpu.VMEM((strips + 2, chunk, width), jnp.float32),
            pltpu.VMEM((640, chunk_own), jnp.float32),
            pltpu.VMEM((640, chunk_own), jnp.float32),
        ],
        compiler_params=pltpu.CompilerParams(vmem_limit_bytes=36 * 1024 * 1024),
        cost_estimate=pl.CostEstimate(
            flops=12 * token_count * band * 2 * INNER,
            bytes_accessed=16 * 1024 * 1024,
            transcendentals=token_count * band * H,
        ),
        name="window_attention",
    )(start, queries, own, grads, rows, cols, corner, bias)


def outer_kernel(own_ref, *refs):
    pairs = (len(refs) - 3) // 2
    operands, (sent_ref, kept_ref, turned) = refs[: 2 * pairs], refs[2 * pairs :]
    share = sent_ref.shape[0] // 4
    for p in range(pairs):
        turned[p] = operands[2 * p][...].T
    for out_ref, half in ((sent_ref, 1 - own_ref[0]), (kept_ref, own_ref[0])):
        products = []
        for p in range(pairs):
            picked = [
                turned[p, pl.ds(pl.multiple_of((2 * r + half) * share, 16), share), :]
                for r in range(4)
            ]
            products.append(dot(jnp.concatenate(picked, axis=0), operands[2 * p + 1][...]))
        if pairs == 1:
            out_ref[...] = products[0].astype(jnp.bfloat16)
        else:
            first, second = products
            out_ref[:, :512] = first[:, :512].astype(jnp.bfloat16)
            out_ref[:, 512:640] = (first[:, 512:] + second[:, :128]).astype(jnp.bfloat16)
            out_ref[:, 640:] = second[:, 128:].astype(jnp.bfloat16)


def outer_halves(*operands):
    rows, width = operands[0].shape
    whole = lambda a: pl.BlockSpec(a.shape, lambda _: (0,) * a.ndim)
    out = jax.ShapeDtypeStruct((width // 2, 2 * INNER), jnp.bfloat16)
    own = lax.axis_index("col").astype(jnp.int32).reshape(1)
    return pl.pallas_call(
        outer_kernel,
        grid=(1,),
        out_shape=(out, out),
        in_specs=[pl.BlockSpec(memory_space=pltpu.SMEM)] + [whole(a) for a in operands],
        out_specs=(whole(out), whole(out)),
        scratch_shapes=[pltpu.VMEM((len(operands) // 2, width, rows), jnp.bfloat16)],
        compiler_params=pltpu.CompilerParams(vmem_limit_bytes=28 * 1024 * 1024),
        cost_estimate=pl.CostEstimate(
            flops=2 * rows * width * 2 * INNER, bytes_accessed=5 * 1024 * 1024, transcendentals=0
        ),
        name="weight_grad_halves",
    )(own, *operands)


def late_kernel(
    own_ref, first, second, third, tokens_ref, inner_ref, side_ref, above_ref, below_ref,
    dq_ref, o_ref, sent_ref, kept_ref, all_ref, att_ref, turned, grad_ref,
):
    own = own_ref[0]
    count = inner_ref.shape[0]
    share = sent_ref.shape[0] // 4
    edge = above_ref.shape[0]
    width = inner_ref.shape[1]
    side = side_ref[: count // 2].astype(jnp.float32).reshape(-1, REACH, width)
    is_left = (own == 0).astype(jnp.float32)
    side = jnp.concatenate([side * (1.0 - is_left), side * is_left], axis=1)
    total = inner_ref[...].astype(jnp.float32) + side.reshape(count, width)
    grad_ref[:edge] = (total[:edge] + above_ref[...].astype(jnp.float32)).astype(jnp.bfloat16)
    grad_ref[edge : count - edge] = total[edge : count - edge].astype(jnp.bfloat16)
    grad_ref[count - edge :] = (
        total[count - edge :] + below_ref[...].astype(jnp.float32)
    ).astype(jnp.bfloat16)
    turned[...] = tokens_ref[...].T
    for out_ref, half in ((sent_ref, 1 - own), (kept_ref, own)):
        picked = [
            turned[pl.ds(pl.multiple_of((2 * r + half) * share, 16), share), :] for r in range(4)
        ]
        product = dot(jnp.concatenate(picked, axis=0), grad_ref[...])
        out_ref[...] = product.astype(jnp.bfloat16)
    all_ref[...] = jnp.concatenate([dq_ref[:, :INNER], grad_ref[...]], axis=1)
    att_ref[...] = o_ref[:, 64:]


def late_halves(earlier, token_rows, inner, side, above, below, dquery, attended):
    rows, width = token_rows.shape
    whole = lambda a: pl.BlockSpec(a.shape, lambda _: (0,) * a.ndim)
    out = jax.ShapeDtypeStruct((width // 2, 2 * INNER), jnp.bfloat16)
    grads = jax.ShapeDtypeStruct((rows, 3 * INNER), jnp.bfloat16)
    att = jax.ShapeDtypeStruct((rows, INNER), jnp.bfloat16)
    operands = (token_rows, inner, side, above, below, dquery, attended)
    own = lax.axis_index("col").astype(jnp.int32).reshape(1)
    return pl.pallas_call(
        late_kernel,
        grid=(1,),
        out_shape=(out, out, grads, att),
        in_specs=[pl.BlockSpec(memory_space=pltpu.SMEM)]
        + [pl.BlockSpec(memory_space=pl.ANY)] * 3
        + [whole(a) for a in operands],
        out_specs=(whole(out), whole(out), whole(grads), whole(att)),
        scratch_shapes=[
            pltpu.VMEM((width, rows), jnp.bfloat16),
            pltpu.VMEM((rows, 2 * INNER), jnp.bfloat16),
        ],
        compiler_params=pltpu.CompilerParams(vmem_limit_bytes=28 * 1024 * 1024),
        cost_estimate=pl.CostEstimate(
            flops=2 * rows * width * 2 * INNER, bytes_accessed=7 * 1024 * 1024, transcendentals=0
        ),
        name="late_weight_grad_halves",
    )(own, *earlier, *operands)


def window_starts(places, extent):
    return jnp.clip(places - REACH, 0, extent - WINDOW)


def window_bias(tile_rows, tile_cols, two_columns):
    row_id = lax.axis_index("row")
    col_id = lax.axis_index("col")
    frame_rows = tile_rows * lax.axis_size("row")
    frame_cols = tile_cols * lax.axis_size("col")
    strips = tile_rows // SIDE
    col_first = col_id * tile_cols
    strip_id = jnp.arange(strips, dtype=jnp.int32)
    first_chunk = row_id * strips - 1
    band_chunk = jnp.clip(row_id * strips + strip_id - 1, 0, frame_rows // SIDE - 3)
    side = jnp.arange(SIDE, dtype=jnp.int32)
    own_cols = col_first + jnp.arange(tile_cols, dtype=jnp.int32)
    low, high = col_first - REACH + side, col_first + tile_cols + side
    spans = [own_cols, jnp.where(col_id == 0, high, low)] if two_columns else [own_cols, low, high]
    chunk_rows = jnp.concatenate([jnp.repeat(side, span.shape[0]) for span in spans])
    chunk_cols = jnp.concatenate([jnp.tile(span, SIDE) for span in spans])
    in_band = jnp.concatenate([SIDE * j + chunk_rows for j in range(3)])
    key_col = jnp.tile(chunk_cols, 3)
    key_row = SIDE * band_chunk[:, None] + in_band[None, :]
    query_row = row_id * tile_rows + SIDE * strip_id[:, None] + jnp.repeat(side, tile_cols)[None, :]
    row_start = window_starts(query_row, frame_rows)
    col_start = window_starts(jnp.tile(own_cols, SIDE), frame_cols)
    row_off = key_row[:, :, None] - row_start[:, None, :]
    col_off = key_col[:, None] - col_start[None, :]
    row_ok = (row_off >= 0) & (row_off < WINDOW)
    col_ok = (col_off >= 0) & (col_off < WINDOW)
    bias = jnp.where(row_ok & col_ok[None], 0.0, MASKED).astype(jnp.float32)
    return (band_chunk - first_chunk).astype(jnp.int32), bias


def after(value, *earlier):
    return lax.optimization_barrier((value,) + earlier)[0]


def cut(block, axis, take):
    own = lax.axis_index(axis)
    return [take(block, own ^ step) for step in range(lax.axis_size(axis))]


def exchange_sum(parts, axis, *earlier):
    kept, got = parts[0], []
    for step, part in enumerate(parts[1:], 1):
        pairs = [(i, i ^ step) for i in range(lax.axis_size(axis))]
        got.append(lax.ppermute(part, axis, pairs))
    if earlier:
        kept = after(kept, *earlier)
    total = kept.astype(jnp.float32)
    for g in got:
        total += g.astype(jnp.float32)
    return total.astype(jnp.bfloat16)


def gathered(block, axis):
    own = lax.axis_index(axis)
    count = lax.axis_size(axis)
    whole = jnp.zeros((count,) + block.shape, block.dtype)
    whole = lax.dynamic_update_index_in_dim(whole, block, own, 0)
    for step in range(1, count):
        got = lax.ppermute(block, axis, [(i, i ^ step) for i in range(count)])
        whole = lax.dynamic_update_index_in_dim(whole, got, own ^ step, 0)
    return whole


def core_sum(sent, kept):
    rows, images = lax.axis_size("row"), lax.axis_size("img")
    width = sent.shape[1]
    share = sent.shape[0] // rows
    kept = kept.reshape(rows, share, width)
    got = lax.ppermute(sent, "col", [(0, 1), (1, 0)]).reshape(rows, share, width)
    held = (kept.astype(jnp.float32) + got.astype(jnp.float32)).astype(jnp.bfloat16)
    small = -(-share // (8 * images)) * 8
    return jnp.pad(held, ((0, 0), (0, images * small - share), (0, 0)))


def image_parts(held):
    small = held.shape[1] // lax.axis_size("img")
    return cut(held, "img", lambda h, j: lax.dynamic_slice_in_dim(h, small * j, small, 1))


def row_parts(held):
    return cut(held, "row", lambda h, r: lax.dynamic_index_in_dim(h, r, 0, keepdims=False))


def whole_share(held, share):
    whole = gathered(held, "img")
    return whole.reshape(-1, held.shape[1])[:share].astype(jnp.float32)


def plain_shares(part):
    held = lax.psum_scatter(part, ("row", "col"), scatter_dimension=0, tiled=True)
    return lax.psum(held, "img").astype(jnp.float32)


def local(tokens, qkv_weight, out_weight, upstream):
    _, tile_rows, tile_cols, width = tokens.shape
    token_count = tile_rows * tile_cols
    strips = tile_rows // SIDE
    chunk_own = SIDE * tile_cols
    row_count, col_count = lax.axis_size("row"), lax.axis_size("col")
    two_columns = col_count == 2
    col_id = lax.axis_index("col")
    token_rows = tokens.reshape(token_count, width)
    grad_rows = upstream.reshape(token_count, width)
    turns = (0,) if two_columns else (-1, 1)

    def moved(block, down, turn=None):
        pairs = []
        for r in range(row_count):
            for c in range(col_count):
                to_c = c if turn is None else (1 - c if turn == 0 else c + turn)
                if 0 <= r + down < row_count and 0 <= to_c < col_count:
                    pairs.append((r * col_count + c, (r + down) * col_count + to_c))
        return lax.ppermute(block, ("row", "col"), pairs)

    def edge(block, turn):
        if turn == 0:
            return lax.dynamic_slice_in_dim(block, (1 - col_id) * (tile_cols - REACH), REACH, 1)
        return block[:, tile_cols - REACH :] if turn == 1 else block[:, :REACH]

    def side_of(block):
        block = block.reshape(-1, tile_cols, 2 * INNER)
        got = [moved(edge(block, t), 0, t) for t in sorted(turns, reverse=True)]
        got = [g.reshape(-1, SIDE * REACH, 2 * INNER) for g in got]
        got = got[0] if two_columns else jnp.concatenate(got, axis=1)
        return got.reshape(-1, 2 * INNER)

    queries, keyvals, top, bottom, near = project(token_rows, qkv_weight, tile_cols)
    above = moved(bottom, 1)
    below = moved(top, -1)
    if two_columns:
        cols = moved(near, 0, 0)
    else:
        cols = side_of(keyvals)
    rows = jnp.concatenate([above, below], axis=0)
    corner = side_of(rows)
    grad_att = lax.dot_general(
        out_weight, grad_rows, (((0,), (1,)), ((), ())), preferred_element_type=jnp.float32
    ).astype(jnp.bfloat16)
    start, bias = window_bias(tile_rows, tile_cols, two_columns)
    attended, dquery, inner_grad, edge_grad, side_grad = attention(
        start, queries, keyvals, grad_att, rows, cols, corner, bias
    )

    def outer(a, b):
        return lax.dot_general(
            a, b, (((0,), (0,)), ((), ())), preferred_element_type=jnp.float32
        ).astype(jnp.bfloat16)

    simple = two_columns and row_count == 4 and lax.axis_size("img") == 4
    if simple:
        early = image_parts(core_sum(*outer_halves(token_rows, dquery, grad_rows, attended)))
    def spread(side, first):
        side = side.reshape(-1, SIDE, REACH, 2 * INNER).astype(jnp.float32)
        zeros = jnp.zeros((side.shape[0], SIDE, tile_cols - REACH, 2 * INNER), jnp.float32)
        order = [side, zeros] if first else [zeros, side]
        return jnp.concatenate(order, axis=2).reshape(-1, 2 * INNER)

    if two_columns:
        got = moved(side_grad, 0, 0)
        returned = lambda part: jnp.where(col_id == 0, spread(part, False), spread(part, True))
    else:
        halves = side_grad.reshape(strips + 2, 2, SIDE * REACH, 2 * INNER)
        got = jnp.stack([moved(halves[:, 0], 0, -1), moved(halves[:, 1], 0, 1)], axis=1)
        returned = lambda part: spread(part[:, 0], False) + spread(part[:, 1], True)
    got = got.reshape(strips + 2, -1, SIDE * REACH, 2 * INNER)
    outer_grad = edge_grad.astype(jnp.float32) + returned(got[strips:])
    outer_grad = outer_grad.astype(jnp.bfloat16)
    from_below = moved(outer_grad[:chunk_own], -1)
    from_above = moved(outer_grad[chunk_own:], 1)
    if simple:
        side = got.reshape(-1, 2 * INNER)
        sent, kept, dqkv, attended = late_halves(
            early[1:], token_rows, inner_grad, side, from_above, from_below, dquery, attended
        )
    else:
        dquery, attended = dquery[:, :INNER], attended[:, 64:]
        dkv = inner_grad.astype(jnp.float32) + returned(got[:strips])
        rest = jnp.zeros((token_count - chunk_own, 2 * INNER), jnp.float32)
        dkv = dkv + jnp.concatenate([from_above.astype(jnp.float32), rest], axis=0)
        dkv = dkv + jnp.concatenate([rest, from_below.astype(jnp.float32)], axis=0)
        dkv = dkv.astype(jnp.bfloat16)
        dqkv = jnp.concatenate([dquery, dkv], axis=1)
    if simple:
        late = image_parts(core_sum(sent, kept))
        early = exchange_sum(early, "img")
        late = exchange_sum(late, "img", early)
        early = exchange_sum(row_parts(early), "row")
        late = exchange_sum(row_parts(late), "row", early)
        share = width // (row_count * col_count)
        early, late = whole_share(early, share), whole_share(late, share)
    else:
        early = jnp.concatenate([outer(token_rows, dquery), outer(grad_rows, attended)], axis=1)
        early, late = plain_shares(early), plain_shares(outer(token_rows, dkv))
    sublayer_out = nt_dot(attended, out_weight).astype(jnp.bfloat16)
    tokens_grad = nt_dot(dqkv, qkv_weight).astype(jnp.bfloat16)
    return (
        sublayer_out.reshape(tokens.shape),
        tokens_grad.reshape(tokens.shape),
        jnp.concatenate([early[:, :INNER], late], axis=1),
        early[:, INNER:],
    )


def solution(mesh):
    return jax.shard_map(
        local,
        mesh=mesh,
        in_specs=(P("img", "row", "col", None), P(), P(), P("img", "row", "col", None)),
        out_specs=(
            P("img", "row", "col", None),
            P("img", "row", "col", None),
            P(("row", "col"), None),
            P(("row", "col"), None),
        ),
        check_vma=False,
    )
```

```python
import jax
import jax.numpy as jnp
from jax import lax
from jax.experimental import pallas as pl
from jax.experimental.pallas import tpu as pltpu
from jax.sharding import PartitionSpec as P

H = 8
DH = 72
INNER = H * DH
REACH = 8
WINDOW = 17
SIDE = 8
PAIRS = H // 2
SLAB = 256
V_SHIFT = 64
MASKED = -1e30
SCALE = DH ** (-0.5)
LIGHT = pl.CostEstimate(flops=1, bytes_accessed=1, transcendentals=0)


def shifted_pairs(count, by):
    return [(i, i + by) for i in range(count) if 0 <= i + by < count]


def dot(a, b):
    return jnp.dot(a, b, preferred_element_type=jnp.float32)


def nt_dot(a, b):
    return lax.dot_general(a, b, (((1,), (1,)), ((), ())), preferred_element_type=jnp.float32)


PIECE = 384


def project_kernel(
    own_ref, tokens_ref, weight_ref, qt_ref, kv_ref, top_ref, bottom_ref, near_ref, tokens, weight, sems
):
    rows = [(INNER + PIECE * p, PIECE) for p in range(2 * INNER // PIECE)] + [(0, INNER)]
    whole = pltpu.make_async_copy(tokens_ref, tokens, sems.at[len(rows)])
    whole.start()
    copies = []
    for n, (first, count) in enumerate(rows):
        part = pl.ds(first, count)
        copies.append(pltpu.make_async_copy(weight_ref.at[part], weight.at[part], sems.at[n]))
        copies[-1].start()
    whole.wait()
    for p in range(2 * INNER // PIECE):
        copies[p].wait()
        lines = weight[INNER + PIECE * p : INNER + PIECE * (p + 1)]
        kv_ref[:, PIECE * p : PIECE * (p + 1)] = nt_dot(tokens[...], lines).astype(jnp.bfloat16)
    count, edge = kv_ref.shape[0], top_ref.shape[0]
    keyvals = kv_ref[...]
    top_ref[...] = keyvals[:edge]
    bottom_ref[...] = keyvals[count - edge :]
    grid = keyvals.astype(jnp.float32).reshape(-1, edge // SIDE, 2 * INNER)
    is_right = own_ref[0].astype(jnp.float32)
    near = grid[:, :REACH] * is_right + grid[:, -REACH:] * (1.0 - is_right)
    near_ref[...] = near.reshape(near_ref.shape).astype(jnp.bfloat16)
    copies[-1].wait()
    qt_ref[...] = nt_dot(weight[:INNER], tokens[...]).astype(jnp.bfloat16)


def project(token_rows, weight, tile_cols):
    rows, width = token_rows.shape
    chunk_own = SIDE * tile_cols
    own = lax.axis_index("col").astype(jnp.int32).reshape(1)
    shapes = [
        (INNER, rows),
        (rows, 2 * INNER),
        (chunk_own, 2 * INNER),
        (chunk_own, 2 * INNER),
        (rows // tile_cols * REACH, 2 * INNER),
    ]
    return pl.pallas_call(
        project_kernel,
        grid=(1,),
        out_shape=[jax.ShapeDtypeStruct(shape, jnp.bfloat16) for shape in shapes],
        in_specs=[
            pl.BlockSpec(memory_space=pltpu.SMEM),
            pl.BlockSpec(memory_space=pl.ANY),
            pl.BlockSpec(memory_space=pl.ANY),
        ],
        out_specs=[pl.BlockSpec(shape, lambda k: (0, 0)) for shape in shapes],
        scratch_shapes=[
            pltpu.VMEM((rows, width), jnp.bfloat16),
            pltpu.VMEM((3 * INNER, width), jnp.bfloat16),
            pltpu.SemaphoreType.DMA((2 * INNER // PIECE + 2,)),
        ],
        compiler_params=pltpu.CompilerParams(vmem_limit_bytes=56 * 1024 * 1024),
        cost_estimate=pl.CostEstimate(
            flops=6 * rows * width * INNER, bytes_accessed=8 * 1024 * 1024, transcendentals=0
        ),
        name="project",
    )(own, token_rows, weight.T)


def attention_kernel(
    start_ref,
    qt_ref,
    own_ref,
    g_ref,
    above_ref,
    below_ref,
    cols_ref,
    corner_ref,
    bias_ref,
    o_ref,
    dq_ref,
    inner_ref,
    edge_ref,
    side_ref,
    kv,
    kvt,
    acc,
    ot,
    dqt,
):
    strips = bias_ref.shape[0]
    chunk = kv.shape[1]
    chunk_own = own_ref.shape[0] // strips
    chunk_side = chunk - chunk_own
    band = 3 * chunk
    token_count = own_ref.shape[0]
    last = strips + 1
    side_order = [strips] + list(range(strips)) + [strips + 1]

    def place(slot, first, part):
        count = part.shape[0]
        kv[slot, first : first + count] = part
        if count < 128:
            filler = jnp.zeros((128 - count, 2 * INNER), part.dtype)
            part = jnp.concatenate([part, filler], axis=0)
        kvt[slot, :, first : first + count] = part.T[:, :count]

    dqt[INNER:, :] = jnp.zeros((64, chunk_own), jnp.float32)
    ot[:64, :] = jnp.zeros((64, chunk_own), jnp.float32)
    for s in range(strips):
        place(s + 1, 0, own_ref[chunk_own * s : chunk_own * (s + 1)])
    for s in range(strips):
        place(s + 1, chunk_own, cols_ref[chunk_side * s : chunk_side * (s + 1)])
    place(0, 0, above_ref[...])
    place(last, 0, below_ref[...])
    for slot, at in ((0, 0), (last, 1)):
        place(slot, chunk_own, corner_ref[chunk_side * at : chunk_side * (at + 1)])
    acc[...] = jnp.zeros_like(acc)

    row = lax.broadcasted_iota(jnp.int32, (2 * DH, chunk_own), 0)
    first_head = row < DH
    mask_a = jnp.where(first_head, 1.0, 0.0).astype(jnp.bfloat16)
    mask_b = jnp.where(first_head, 0.0, 1.0).astype(jnp.bfloat16)
    ones = jnp.ones((16, chunk), jnp.bfloat16)

    def pair_block(part, above):
        block = jnp.concatenate([part * mask_a, part * mask_b], axis=1)
        parts = [block]
        if above:
            parts = [jnp.zeros((above, block.shape[1]), block.dtype)] + parts
        below = SLAB - 2 * DH - above
        if below:
            parts = parts + [jnp.zeros((below, block.shape[1]), block.dtype)]
        return jnp.concatenate(parts, axis=0)

    def pick(both):
        return jnp.where(first_head, both[:, :chunk_own], both[:, chunk_own:])

    def strip(s, carry):
        top = start_ref[s]
        rows = pl.ds(pl.multiple_of(s * chunk_own, chunk_own), chunk_own)
        bias = bias_ref[s]
        bias = jnp.concatenate([bias, bias], axis=1)
        heads = [slice(2 * DH * i, 2 * DH * (i + 1)) for i in range(PAIRS)]
        k_lanes = [slice(128 * i, 128 * i + SLAB) for i in range(PAIRS)]
        v_lanes = [slice(512 + 128 * i, 512 + 128 * i + SLAB) for i in range(PAIRS)]

        def band_of(lanes):
            return kv[pl.ds(top, 3), :, lanes].reshape(band, SLAB)

        def from_keys(lines, weights):
            got = jnp.zeros((2 * DH, SLAB), jnp.float32)
            for j in range(3):
                got += dot(kvt[top + j, lines, :], weights[chunk * j : chunk * (j + 1)])
            return got

        q2 = [pair_block(qt_ref[heads[i], rows], 16 * i) for i in range(PAIRS)]
        g2 = [pair_block(g_ref[heads[i], rows], V_SHIFT + 16 * i) for i in range(PAIRS)]
        prob, inv, row_dot, dscore = [], [], [], []
        for i in range(PAIRS):
            scores = dot(band_of(k_lanes[i]), q2[i]) * SCALE + bias
            top_score = jnp.max(scores, axis=0, keepdims=True)
            prob.append(jnp.exp(scores - top_score).astype(jnp.bfloat16))
        for i in range(PAIRS):
            total = jnp.zeros((16, SLAB), jnp.float32)
            for j in range(3):
                total += dot(ones, prob[i][chunk * j : chunk * (j + 1)])
            inv.append(1.0 / total[:1])
            v_rows = slice(INNER + heads[i].start, INNER + heads[i].stop)
            att = pick(from_keys(v_rows, prob[i]) * inv[i])
            ot[64 + heads[i].start : 64 + heads[i].stop, :] = att
            dots = att * g_ref[heads[i], rows].astype(jnp.float32)
            row_dot.append(
                jnp.concatenate(
                    [
                        jnp.sum(dots[:DH], axis=0, keepdims=True),
                        jnp.sum(dots[DH:], axis=0, keepdims=True),
                    ],
                    axis=1,
                )
            )
        for i in range(PAIRS):
            dprob = dot(band_of(v_lanes[i]), g2[i])
            inv_scale = inv[i] * SCALE
            change = dprob * inv_scale - row_dot[i] * inv_scale
            dscore.append((prob[i].astype(jnp.float32) * change).astype(jnp.bfloat16))
        for i in range(PAIRS):
            dv = nt_dot(prob[i], (g2[i].astype(jnp.float32) * inv[i]).astype(jnp.bfloat16))
            acc[pl.ds(top, 3), :, v_lanes[i]] += dv.reshape(3, chunk, SLAB)
        for i in range(PAIRS):
            dqt[heads[i], :] = pick(from_keys(heads[i], dscore[i]))
            dk = nt_dot(dscore[i], q2[i])
            acc[pl.ds(top, 3), :, k_lanes[i]] += dk.reshape(3, chunk, SLAB)
        o_ref[rows, :] = ot[...].T.astype(jnp.bfloat16)
        dq_ref[rows, :] = dqt[...].T.astype(jnp.bfloat16)
        return carry

    lax.fori_loop(0, strips, strip, 0)
    for slot, at in enumerate(side_order):
        own_grad = acc[slot, :chunk_own].astype(jnp.bfloat16)
        if at < strips:
            inner_ref[chunk_own * at : chunk_own * (at + 1), :] = own_grad
        else:
            edge_ref[chunk_own * (at - strips) : chunk_own * (at - strips + 1), :] = own_grad
        side_ref[chunk_side * at : chunk_side * (at + 1), :] = acc[slot, chunk_own:].astype(
            jnp.bfloat16
        )


def attention(start, queries, own, grads, above, below, cols, corner, bias):
    strips, band, chunk_own = bias.shape
    chunk = band // 3
    token_count, width = own.shape
    whole = lambda a: pl.BlockSpec(a.shape, lambda _: (0,) * a.ndim)
    outs = (
        jax.ShapeDtypeStruct((token_count, INNER + 64), jnp.bfloat16),
        jax.ShapeDtypeStruct((token_count, INNER + 64), jnp.bfloat16),
        jax.ShapeDtypeStruct(own.shape, jnp.bfloat16),
        jax.ShapeDtypeStruct((2 * chunk_own, width), jnp.bfloat16),
        jax.ShapeDtypeStruct((cols.shape[0] + corner.shape[0], width), jnp.bfloat16),
    )
    return pl.pallas_call(
        attention_kernel,
        grid=(1,),
        out_shape=outs,
        in_specs=[
            pl.BlockSpec(memory_space=pltpu.SMEM),
            whole(queries),
            whole(own),
            whole(grads),
            whole(above),
            whole(below),
            whole(cols),
            whole(corner),
            whole(bias),
        ],
        out_specs=tuple(whole(o) for o in outs),
        scratch_shapes=[
            pltpu.VMEM((strips + 2, chunk, width), jnp.bfloat16),
            pltpu.VMEM((strips + 2, width, chunk), jnp.bfloat16),
            pltpu.VMEM((strips + 2, chunk, width), jnp.float32),
            pltpu.VMEM((640, chunk_own), jnp.float32),
            pltpu.VMEM((640, chunk_own), jnp.float32),
        ],
        compiler_params=pltpu.CompilerParams(vmem_limit_bytes=36 * 1024 * 1024),
        cost_estimate=pl.CostEstimate(
            flops=12 * token_count * band * 2 * INNER,
            bytes_accessed=16 * 1024 * 1024,
            transcendentals=token_count * band * H,
        ),
        name="window_attention",
    )(start, queries, own, grads, above, below, cols, corner, bias)


def outer_kernel(own_ref, *refs):
    pairs = (len(refs) - 3) // 2
    operands, (sent_ref, kept_ref, turned) = refs[: 2 * pairs], refs[2 * pairs :]
    share = sent_ref.shape[0] // 4
    for p in range(pairs):
        turned[p] = operands[2 * p][...].T
    for out_ref, half in ((sent_ref, 1 - own_ref[0]), (kept_ref, own_ref[0])):
        products = []
        for p in range(pairs):
            picked = [
                turned[p, pl.ds(pl.multiple_of((2 * r + half) * share, 16), share), :]
                for r in range(4)
            ]
            products.append(dot(jnp.concatenate(picked, axis=0), operands[2 * p + 1][...]))
        if pairs == 1:
            out_ref[...] = products[0].astype(jnp.bfloat16)
        else:
            first, second = products
            out_ref[:, :512] = first[:, :512].astype(jnp.bfloat16)
            out_ref[:, 512:640] = (first[:, 512:] + second[:, :128]).astype(jnp.bfloat16)
            out_ref[:, 640:] = second[:, 128:].astype(jnp.bfloat16)


def outer_halves(*operands):
    rows, width = operands[0].shape
    whole = lambda a: pl.BlockSpec(a.shape, lambda _: (0,) * a.ndim)
    out = jax.ShapeDtypeStruct((width // 2, 2 * INNER), jnp.bfloat16)
    own = lax.axis_index("col").astype(jnp.int32).reshape(1)
    return pl.pallas_call(
        outer_kernel,
        grid=(1,),
        out_shape=(out, out),
        in_specs=[pl.BlockSpec(memory_space=pltpu.SMEM)] + [whole(a) for a in operands],
        out_specs=(whole(out), whole(out)),
        scratch_shapes=[pltpu.VMEM((len(operands) // 2, width, rows), jnp.bfloat16)],
        compiler_params=pltpu.CompilerParams(vmem_limit_bytes=28 * 1024 * 1024),
        cost_estimate=LIGHT,
        name="weight_grad_halves",
    )(own, *operands)


def late_kernel(
    own_ref, first, second, third, tokens_ref, inner_ref, side_ref, above_ref, below_ref,
    dq_ref, o_ref, sent_ref, kept_ref, all_ref, att_ref, turned, grad_ref,
):
    own = own_ref[0]
    count = inner_ref.shape[0]
    share = sent_ref.shape[0] // 4
    edge = above_ref.shape[0]
    width = inner_ref.shape[1]
    side = side_ref[: count // 2].astype(jnp.float32).reshape(-1, REACH, width)
    is_left = (own == 0).astype(jnp.float32)
    side = jnp.concatenate([side * (1.0 - is_left), side * is_left], axis=1)
    total = inner_ref[...].astype(jnp.float32) + side.reshape(count, width)
    grad_ref[:edge] = (total[:edge] + above_ref[...].astype(jnp.float32)).astype(jnp.bfloat16)
    grad_ref[edge : count - edge] = total[edge : count - edge].astype(jnp.bfloat16)
    grad_ref[count - edge :] = (
        total[count - edge :] + below_ref[...].astype(jnp.float32)
    ).astype(jnp.bfloat16)
    turned[...] = tokens_ref[...].T
    for out_ref, half in ((sent_ref, 1 - own), (kept_ref, own)):
        picked = [
            turned[pl.ds(pl.multiple_of((2 * r + half) * share, 16), share), :] for r in range(4)
        ]
        product = dot(jnp.concatenate(picked, axis=0), grad_ref[...])
        out_ref[...] = product.astype(jnp.bfloat16)
    all_ref[...] = jnp.concatenate([dq_ref[:, :INNER], grad_ref[...]], axis=1)
    att_ref[...] = o_ref[:, 64:]


def late_halves(earlier, token_rows, inner, side, above, below, dquery, attended):
    rows, width = token_rows.shape
    whole = lambda a: pl.BlockSpec(a.shape, lambda _: (0,) * a.ndim)
    out = jax.ShapeDtypeStruct((width // 2, 2 * INNER), jnp.bfloat16)
    grads = jax.ShapeDtypeStruct((rows, 3 * INNER), jnp.bfloat16)
    att = jax.ShapeDtypeStruct((rows, INNER), jnp.bfloat16)
    operands = (token_rows, inner, side, above, below, dquery, attended)
    own = lax.axis_index("col").astype(jnp.int32).reshape(1)
    return pl.pallas_call(
        late_kernel,
        grid=(1,),
        out_shape=(out, out, grads, att),
        in_specs=[pl.BlockSpec(memory_space=pltpu.SMEM)]
        + [pl.BlockSpec(memory_space=pl.ANY)] * 3
        + [whole(a) for a in operands],
        out_specs=(whole(out), whole(out), whole(grads), whole(att)),
        scratch_shapes=[
            pltpu.VMEM((width, rows), jnp.bfloat16),
            pltpu.VMEM((rows, 2 * INNER), jnp.bfloat16),
        ],
        compiler_params=pltpu.CompilerParams(vmem_limit_bytes=28 * 1024 * 1024),
        cost_estimate=LIGHT,
        name="late_weight_grad_halves",
    )(own, *earlier, *operands)


def window_starts(places, extent):
    return jnp.clip(places - REACH, 0, extent - WINDOW)


def window_bias(tile_rows, tile_cols, two_columns):
    row_id = lax.axis_index("row")
    col_id = lax.axis_index("col")
    frame_rows = tile_rows * lax.axis_size("row")
    frame_cols = tile_cols * lax.axis_size("col")
    strips = tile_rows // SIDE
    col_first = col_id * tile_cols
    strip_id = jnp.arange(strips, dtype=jnp.int32)
    first_chunk = row_id * strips - 1
    band_chunk = jnp.clip(row_id * strips + strip_id - 1, 0, frame_rows // SIDE - 3)
    side = jnp.arange(SIDE, dtype=jnp.int32)
    own_cols = col_first + jnp.arange(tile_cols, dtype=jnp.int32)
    low, high = col_first - REACH + side, col_first + tile_cols + side
    spans = [own_cols, jnp.where(col_id == 0, high, low)] if two_columns else [own_cols, low, high]
    chunk_rows = jnp.concatenate([jnp.repeat(side, span.shape[0]) for span in spans])
    chunk_cols = jnp.concatenate([jnp.tile(span, SIDE) for span in spans])
    in_band = jnp.concatenate([SIDE * j + chunk_rows for j in range(3)])
    key_col = jnp.tile(chunk_cols, 3)
    key_row = SIDE * band_chunk[:, None] + in_band[None, :]
    query_row = row_id * tile_rows + SIDE * strip_id[:, None] + jnp.repeat(side, tile_cols)[None, :]
    row_start = window_starts(query_row, frame_rows)
    col_start = window_starts(jnp.tile(own_cols, SIDE), frame_cols)
    row_off = key_row[:, :, None] - row_start[:, None, :]
    col_off = key_col[:, None] - col_start[None, :]
    row_ok = (row_off >= 0) & (row_off < WINDOW)
    col_ok = (col_off >= 0) & (col_off < WINDOW)
    bias = jnp.where(row_ok & col_ok[None], 0.0, MASKED).astype(jnp.float32)
    return (band_chunk - first_chunk).astype(jnp.int32), bias


def after(value, *earlier):
    return lax.optimization_barrier((value,) + earlier)[0]


def cut(block, axis, take):
    own = lax.axis_index(axis)
    return [take(block, own ^ step) for step in range(lax.axis_size(axis))]


def exchange_sum(parts, axis, *earlier):
    kept, got = parts[0], []
    for step, part in enumerate(parts[1:], 1):
        pairs = [(i, i ^ step) for i in range(lax.axis_size(axis))]
        got.append(lax.ppermute(part, axis, pairs))
    if earlier:
        kept = after(kept, *earlier)
    total = kept.astype(jnp.float32)
    for g in got:
        total += g.astype(jnp.float32)
    return total.astype(jnp.bfloat16)


def gathered(block, axis):
    own = lax.axis_index(axis)
    count = lax.axis_size(axis)
    whole = jnp.zeros((count,) + block.shape, block.dtype)
    whole = lax.dynamic_update_index_in_dim(whole, block, own, 0)
    for step in range(1, count):
        got = lax.ppermute(block, axis, [(i, i ^ step) for i in range(count)])
        whole = lax.dynamic_update_index_in_dim(whole, got, own ^ step, 0)
    return whole


def core_sum(sent, kept):
    rows, images = lax.axis_size("row"), lax.axis_size("img")
    width = sent.shape[1]
    share = sent.shape[0] // rows
    kept = kept.reshape(rows, share, width)
    got = lax.ppermute(sent, "col", [(0, 1), (1, 0)]).reshape(rows, share, width)
    held = (kept.astype(jnp.float32) + got.astype(jnp.float32)).astype(jnp.bfloat16)
    small = -(-share // (8 * images)) * 8
    return jnp.pad(held, ((0, 0), (0, images * small - share), (0, 0)))


def image_parts(held):
    small = held.shape[1] // lax.axis_size("img")
    return cut(held, "img", lambda h, j: lax.dynamic_slice_in_dim(h, small * j, small, 1))


def row_parts(held):
    return cut(held, "row", lambda h, r: lax.dynamic_index_in_dim(h, r, 0, keepdims=False))


def whole_share(held, share):
    whole = gathered(held, "img")
    return whole.reshape(-1, held.shape[1])[:share].astype(jnp.float32)


def plain_shares(part):
    held = lax.psum_scatter(part, ("row", "col"), scatter_dimension=0, tiled=True)
    return lax.psum(held, "img").astype(jnp.float32)


def local(tokens, qkv_weight, out_weight, upstream):
    _, tile_rows, tile_cols, width = tokens.shape
    token_count = tile_rows * tile_cols
    strips = tile_rows // SIDE
    chunk_own = SIDE * tile_cols
    row_count, col_count = lax.axis_size("row"), lax.axis_size("col")
    two_columns = col_count == 2
    col_id = lax.axis_index("col")
    token_rows = tokens.reshape(token_count, width)
    grad_rows = upstream.reshape(token_count, width)
    turns = (0,) if two_columns else (-1, 1)

    def moved(block, down, turn=None):
        pairs = []
        for r in range(row_count):
            for c in range(col_count):
                to_c = c if turn is None else (1 - c if turn == 0 else c + turn)
                if 0 <= r + down < row_count and 0 <= to_c < col_count:
                    pairs.append((r * col_count + c, (r + down) * col_count + to_c))
        return lax.ppermute(block, ("row", "col"), pairs)

    def edge(block, turn):
        if turn == 0:
            return lax.dynamic_slice_in_dim(block, (1 - col_id) * (tile_cols - REACH), REACH, 1)
        return block[:, tile_cols - REACH :] if turn == 1 else block[:, :REACH]

    def side_of(*blocks):
        got = []
        for turn in sorted(turns, reverse=True):
            near = [edge(block.reshape(-1, tile_cols, 2 * INNER), turn) for block in blocks]
            near = jnp.concatenate(near, axis=0) if len(near) > 1 else near[0]
            got.append(moved(near, 0, turn).reshape(-1, SIDE * REACH, 2 * INNER))
        got = got[0] if two_columns else jnp.concatenate(got, axis=1)
        return got.reshape(-1, 2 * INNER)

    queries, keyvals, top, bottom, near = project(token_rows, qkv_weight, tile_cols)
    above = moved(bottom, 1)
    below = moved(top, -1)
    if two_columns:
        cols = moved(near, 0, 0)
    else:
        cols = side_of(keyvals)
    corner = side_of(above, below)
    grad_att = lax.dot_general(
        out_weight, grad_rows, (((0,), (1,)), ((), ())), preferred_element_type=jnp.float32
    ).astype(jnp.bfloat16)
    start, bias = window_bias(tile_rows, tile_cols, two_columns)
    attended, dquery, inner_grad, edge_grad, side_grad = attention(
        start, queries, keyvals, grad_att, above, below, cols, corner, bias
    )

    def outer(a, b):
        return lax.dot_general(
            a, b, (((0,), (0,)), ((), ())), preferred_element_type=jnp.float32
        ).astype(jnp.bfloat16)

    simple = two_columns and row_count == 4 and lax.axis_size("img") == 4
    if simple:
        early = image_parts(core_sum(*outer_halves(token_rows, dquery, grad_rows, attended)))
    def spread(side, first):
        side = side.reshape(-1, SIDE, REACH, 2 * INNER).astype(jnp.float32)
        zeros = jnp.zeros((side.shape[0], SIDE, tile_cols - REACH, 2 * INNER), jnp.float32)
        order = [side, zeros] if first else [zeros, side]
        return jnp.concatenate(order, axis=2).reshape(-1, 2 * INNER)

    if two_columns:
        got = moved(side_grad, 0, 0)
        returned = lambda part: jnp.where(col_id == 0, spread(part, False), spread(part, True))
    else:
        halves = side_grad.reshape(strips + 2, 2, SIDE * REACH, 2 * INNER)
        got = jnp.stack([moved(halves[:, 0], 0, -1), moved(halves[:, 1], 0, 1)], axis=1)
        returned = lambda part: spread(part[:, 0], False) + spread(part[:, 1], True)
    got = got.reshape(strips + 2, -1, SIDE * REACH, 2 * INNER)
    outer_grad = edge_grad.astype(jnp.float32) + returned(got[strips:])
    outer_grad = outer_grad.astype(jnp.bfloat16)
    from_below = moved(outer_grad[:chunk_own], -1)
    from_above = moved(outer_grad[chunk_own:], 1)
    if simple:
        side = got.reshape(-1, 2 * INNER)
        sent, kept, dqkv, attended = late_halves(
            early[1:], token_rows, inner_grad, side, from_above, from_below, dquery, attended
        )
    else:
        dquery, attended = dquery[:, :INNER], attended[:, 64:]
        dkv = inner_grad.astype(jnp.float32) + returned(got[:strips])
        rest = jnp.zeros((token_count - chunk_own, 2 * INNER), jnp.float32)
        dkv = dkv + jnp.concatenate([from_above.astype(jnp.float32), rest], axis=0)
        dkv = dkv + jnp.concatenate([rest, from_below.astype(jnp.float32)], axis=0)
        dkv = dkv.astype(jnp.bfloat16)
        dqkv = jnp.concatenate([dquery, dkv], axis=1)
    if simple:
        late = image_parts(core_sum(sent, kept))
        early = exchange_sum(early, "img")
        late = exchange_sum(late, "img", early)
        early = exchange_sum(row_parts(early), "row")
        late = exchange_sum(row_parts(late), "row", early)
        share = width // (row_count * col_count)
        early, late = whole_share(early, share), whole_share(late, share)
    else:
        early = jnp.concatenate([outer(token_rows, dquery), outer(grad_rows, attended)], axis=1)
        early, late = plain_shares(early), plain_shares(outer(token_rows, dkv))
    sublayer_out = nt_dot(attended, out_weight).astype(jnp.bfloat16)
    tokens_grad = nt_dot(dqkv, qkv_weight).astype(jnp.bfloat16)
    return (
        sublayer_out.reshape(tokens.shape),
        tokens_grad.reshape(tokens.shape),
        jnp.concatenate([early[:, :INNER], late], axis=1),
        early[:, INNER:],
    )


def solution(mesh):
    return jax.shard_map(
        local,
        mesh=mesh,
        in_specs=(P("img", "row", "col", None), P(), P(), P("img", "row", "col", None)),
        out_specs=(
            P("img", "row", "col", None),
            P("img", "row", "col", None),
            P(("row", "col"), None),
            P(("row", "col"), None),
        ),
        check_vma=False,
    )
```

```python
import jax
import jax.numpy as jnp
from jax import lax
from jax.experimental import pallas as pl
from jax.experimental.pallas import tpu as pltpu
from jax.sharding import PartitionSpec as P

H = 8
DH = 72
INNER = H * DH
REACH = 8
WINDOW = 17
SIDE = 8
PAIRS = H // 2
SLAB = 256
V_SHIFT = 64
MASKED = -1e30
SCALE = DH ** (-0.5)
LIGHT = pl.CostEstimate(flops=1, bytes_accessed=1, transcendentals=0)


def shifted_pairs(count, by):
    return [(i, i + by) for i in range(count) if 0 <= i + by < count]


def dot(a, b):
    return jnp.dot(a, b, preferred_element_type=jnp.float32)


def nt_dot(a, b):
    return lax.dot_general(a, b, (((1,), (1,)), ((), ())), preferred_element_type=jnp.float32)


PIECE = 384
PIECES = 2 * INNER // PIECE


def fetch(pairs, sems):
    copies = [pltpu.make_async_copy(*pair, sems.at[n]) for n, pair in enumerate(pairs)]
    for copy in copies:
        copy.start()
    return copies


def weight_pieces(weight_ref, weight):
    return [
        (weight_ref.at[pl.ds(INNER + PIECE * p, PIECE)], weight.at[pl.ds(PIECE * p, PIECE)])
        for p in range(PIECES)
    ]


def edges_kernel(tokens_ref, weight_ref, top_ref, bottom_ref, tokens, weight, sems):
    edge = top_ref.shape[0]
    ends = [(0, 0), (edge, tokens_ref.shape[0] - edge)]
    token_pairs = [
        (tokens_ref.at[pl.ds(there, edge)], tokens.at[pl.ds(here, edge)]) for here, there in ends
    ]
    copies = fetch(token_pairs + weight_pieces(weight_ref, weight), sems)
    copies[0].wait()
    copies[1].wait()
    for p in range(PIECES):
        copies[2 + p].wait()
        lanes = slice(PIECE * p, PIECE * (p + 1))
        part = nt_dot(tokens[...], weight[lanes]).astype(jnp.bfloat16)
        top_ref[:, lanes] = part[:edge]
        bottom_ref[:, lanes] = part[edge:]


def project_kernel(own_ref, top_ref, tokens_ref, weight_ref, kv_ref, near_ref, tokens, weight, sems):
    copies = fetch([(tokens_ref, tokens)] + weight_pieces(weight_ref, weight), sems)
    copies[0].wait()
    for p in range(PIECES):
        copies[1 + p].wait()
        lanes = slice(PIECE * p, PIECE * (p + 1))
        part = nt_dot(tokens[...], weight[lanes])
        kv_ref[:, lanes] = part.astype(jnp.bfloat16)
        grid = part.reshape(near_ref.shape[0] // REACH, -1, PIECE)
        is_right = own_ref[0].astype(jnp.float32)
        near = grid[:, :REACH] * is_right + grid[:, -REACH:] * (1.0 - is_right)
        near_ref[:, lanes] = near.reshape(-1, PIECE).astype(jnp.bfloat16)


def project(token_rows, weight, tile_cols):
    rows, width = token_rows.shape
    edge = SIDE * tile_cols
    own = lax.axis_index("col").astype(jnp.int32).reshape(1)
    shape = lambda count: jax.ShapeDtypeStruct((count, 2 * INNER), jnp.bfloat16)
    block = lambda count: pl.BlockSpec((count, 2 * INNER), lambda _: (0, 0))
    anywhere = pl.BlockSpec(memory_space=pl.ANY)
    params = pltpu.CompilerParams(vmem_limit_bytes=56 * 1024 * 1024)
    scratch = lambda count, copies: [
        pltpu.VMEM((count, width), jnp.bfloat16),
        pltpu.VMEM((2 * INNER, width), jnp.bfloat16),
        pltpu.SemaphoreType.DMA((copies,)),
    ]
    top, bottom = pl.pallas_call(
        edges_kernel,
        grid=(1,),
        out_shape=[shape(edge)] * 2,
        in_specs=[anywhere] * 2,
        out_specs=[block(edge)] * 2,
        scratch_shapes=scratch(2 * edge, PIECES + 2),
        compiler_params=params,
        cost_estimate=LIGHT,
        name="project_edges",
    )(token_rows, weight.T)
    near = rows // tile_cols * REACH
    keyvals, near = pl.pallas_call(
        project_kernel,
        grid=(1,),
        out_shape=[shape(rows), shape(near)],
        in_specs=[pl.BlockSpec(memory_space=pltpu.SMEM)] + [anywhere] * 3,
        out_specs=[block(rows), block(near)],
        scratch_shapes=scratch(rows, PIECES + 1),
        compiler_params=params,
        cost_estimate=LIGHT,
        name="project",
    )(own, top, token_rows, weight.T)
    return keyvals, top, bottom, near


def attention_kernel(
    start_ref,
    qt_ref,
    own_ref,
    g_ref,
    above_ref,
    below_ref,
    cols_ref,
    corner_ref,
    bias_ref,
    o_ref,
    dq_ref,
    inner_ref,
    edge_ref,
    side_ref,
    kv,
    kvt,
    acc,
    ot,
    dqt,
):
    strips = bias_ref.shape[0]
    chunk = kv.shape[1]
    chunk_own = own_ref.shape[0] // strips
    chunk_side = chunk - chunk_own
    band = 3 * chunk
    token_count = own_ref.shape[0]
    last = strips + 1
    side_order = [strips] + list(range(strips)) + [strips + 1]

    def place(slot, first, part):
        count = part.shape[0]
        kv[slot, first : first + count] = part
        if count < 128:
            filler = jnp.zeros((128 - count, 2 * INNER), part.dtype)
            part = jnp.concatenate([part, filler], axis=0)
        kvt[slot, :, first : first + count] = part.T[:, :count]

    dqt[INNER:, :] = jnp.zeros((64, chunk_own), jnp.float32)
    ot[:64, :] = jnp.zeros((64, chunk_own), jnp.float32)
    for s in range(strips):
        place(s + 1, 0, own_ref[chunk_own * s : chunk_own * (s + 1)])
    for s in range(strips):
        place(s + 1, chunk_own, cols_ref[chunk_side * s : chunk_side * (s + 1)])
    place(0, 0, above_ref[...])
    place(last, 0, below_ref[...])
    for slot, at in ((0, 0), (last, 1)):
        place(slot, chunk_own, corner_ref[chunk_side * at : chunk_side * (at + 1)])
    acc[...] = jnp.zeros_like(acc)

    row = lax.broadcasted_iota(jnp.int32, (2 * DH, chunk_own), 0)
    first_head = row < DH
    mask_a = jnp.where(first_head, 1.0, 0.0).astype(jnp.bfloat16)
    mask_b = jnp.where(first_head, 0.0, 1.0).astype(jnp.bfloat16)
    ones = jnp.ones((16, chunk), jnp.bfloat16)

    def pair_block(part, above):
        block = jnp.concatenate([part * mask_a, part * mask_b], axis=1)
        parts = [block]
        if above:
            parts = [jnp.zeros((above, block.shape[1]), block.dtype)] + parts
        below = SLAB - 2 * DH - above
        if below:
            parts = parts + [jnp.zeros((below, block.shape[1]), block.dtype)]
        return jnp.concatenate(parts, axis=0)

    def pick(both):
        return jnp.where(first_head, both[:, :chunk_own], both[:, chunk_own:])

    def strip(s, carry):
        top = start_ref[s]
        rows = pl.ds(pl.multiple_of(s * chunk_own, chunk_own), chunk_own)
        bias = bias_ref[s]
        bias = jnp.concatenate([bias, bias], axis=1)
        heads = [slice(2 * DH * i, 2 * DH * (i + 1)) for i in range(PAIRS)]
        k_lanes = [slice(128 * i, 128 * i + SLAB) for i in range(PAIRS)]
        v_lanes = [slice(512 + 128 * i, 512 + 128 * i + SLAB) for i in range(PAIRS)]

        def band_of(lanes):
            return kv[pl.ds(top, 3), :, lanes].reshape(band, SLAB)

        def from_keys(lines, weights):
            got = jnp.zeros((2 * DH, SLAB), jnp.float32)
            for j in range(3):
                got += dot(kvt[top + j, lines, :], weights[chunk * j : chunk * (j + 1)])
            return got

        q2 = [pair_block(qt_ref[heads[i], rows], 16 * i) for i in range(PAIRS)]
        g2 = [pair_block(g_ref[heads[i], rows], V_SHIFT + 16 * i) for i in range(PAIRS)]
        prob, inv, row_dot, dscore = [], [], [], []
        for i in range(PAIRS):
            scores = dot(band_of(k_lanes[i]), q2[i]) * SCALE + bias
            top_score = jnp.max(scores, axis=0, keepdims=True)
            prob.append(jnp.exp(scores - top_score).astype(jnp.bfloat16))
        for i in range(PAIRS):
            total = jnp.zeros((16, SLAB), jnp.float32)
            for j in range(3):
                total += dot(ones, prob[i][chunk * j : chunk * (j + 1)])
            inv.append(1.0 / total[:1])
            v_rows = slice(INNER + heads[i].start, INNER + heads[i].stop)
            att = pick(from_keys(v_rows, prob[i]) * inv[i])
            ot[64 + heads[i].start : 64 + heads[i].stop, :] = att
            dots = att * g_ref[heads[i], rows].astype(jnp.float32)
            row_dot.append(
                jnp.concatenate(
                    [
                        jnp.sum(dots[:DH], axis=0, keepdims=True),
                        jnp.sum(dots[DH:], axis=0, keepdims=True),
                    ],
                    axis=1,
                )
            )
        for i in range(PAIRS):
            dprob = dot(band_of(v_lanes[i]), g2[i])
            inv_scale = inv[i] * SCALE
            change = dprob * inv_scale - row_dot[i] * inv_scale
            dscore.append((prob[i].astype(jnp.float32) * change).astype(jnp.bfloat16))
        for i in range(PAIRS):
            dv = nt_dot(prob[i], (g2[i].astype(jnp.float32) * inv[i]).astype(jnp.bfloat16))
            acc[pl.ds(top, 3), :, v_lanes[i]] += dv.reshape(3, chunk, SLAB)
        for i in range(PAIRS):
            dqt[heads[i], :] = pick(from_keys(heads[i], dscore[i]))
            dk = nt_dot(dscore[i], q2[i])
            acc[pl.ds(top, 3), :, k_lanes[i]] += dk.reshape(3, chunk, SLAB)
        o_ref[rows, :] = ot[...].T.astype(jnp.bfloat16)
        dq_ref[rows, :] = dqt[...].T.astype(jnp.bfloat16)
        return carry

    lax.fori_loop(0, strips, strip, 0)
    for slot, at in enumerate(side_order):
        own_grad = acc[slot, :chunk_own].astype(jnp.bfloat16)
        if at < strips:
            inner_ref[chunk_own * at : chunk_own * (at + 1), :] = own_grad
        else:
            edge_ref[chunk_own * (at - strips) : chunk_own * (at - strips + 1), :] = own_grad
        side_ref[chunk_side * at : chunk_side * (at + 1), :] = acc[slot, chunk_own:].astype(
            jnp.bfloat16
        )


def attention(start, queries, own, grads, above, below, cols, corner, bias):
    strips, band, chunk_own = bias.shape
    chunk = band // 3
    token_count, width = own.shape
    whole = lambda a: pl.BlockSpec(a.shape, lambda _: (0,) * a.ndim)
    outs = (
        jax.ShapeDtypeStruct((token_count, INNER + 64), jnp.bfloat16),
        jax.ShapeDtypeStruct((token_count, INNER + 64), jnp.bfloat16),
        jax.ShapeDtypeStruct(own.shape, jnp.bfloat16),
        jax.ShapeDtypeStruct((2 * chunk_own, width), jnp.bfloat16),
        jax.ShapeDtypeStruct((cols.shape[0] + corner.shape[0], width), jnp.bfloat16),
    )
    return pl.pallas_call(
        attention_kernel,
        grid=(1,),
        out_shape=outs,
        in_specs=[
            pl.BlockSpec(memory_space=pltpu.SMEM),
            whole(queries),
            whole(own),
            whole(grads),
            whole(above),
            whole(below),
            whole(cols),
            whole(corner),
            whole(bias),
        ],
        out_specs=tuple(whole(o) for o in outs),
        scratch_shapes=[
            pltpu.VMEM((strips + 2, chunk, width), jnp.bfloat16),
            pltpu.VMEM((strips + 2, width, chunk), jnp.bfloat16),
            pltpu.VMEM((strips + 2, chunk, width), jnp.float32),
            pltpu.VMEM((640, chunk_own), jnp.float32),
            pltpu.VMEM((640, chunk_own), jnp.float32),
        ],
        compiler_params=pltpu.CompilerParams(vmem_limit_bytes=36 * 1024 * 1024),
        cost_estimate=pl.CostEstimate(
            flops=12 * token_count * band * 2 * INNER,
            bytes_accessed=16 * 1024 * 1024,
            transcendentals=token_count * band * H,
        ),
        name="window_attention",
    )(start, queries, own, grads, above, below, cols, corner, bias)


def outer_kernel(own_ref, *refs):
    pairs = (len(refs) - 3) // 2
    operands, (sent_ref, kept_ref, turned) = refs[: 2 * pairs], refs[2 * pairs :]
    share = sent_ref.shape[0] // 4
    for p in range(pairs):
        turned[p] = operands[2 * p][...].T
    for out_ref, half in ((sent_ref, 1 - own_ref[0]), (kept_ref, own_ref[0])):
        products = []
        for p in range(pairs):
            picked = [
                turned[p, pl.ds(pl.multiple_of((2 * r + half) * share, 16), share), :]
                for r in range(4)
            ]
            products.append(dot(jnp.concatenate(picked, axis=0), operands[2 * p + 1][...]))
        if pairs == 1:
            out_ref[...] = products[0].astype(jnp.bfloat16)
        else:
            first, second = products
            out_ref[:, :512] = first[:, :512].astype(jnp.bfloat16)
            out_ref[:, 512:640] = (first[:, 512:] + second[:, :128]).astype(jnp.bfloat16)
            out_ref[:, 640:] = second[:, 128:].astype(jnp.bfloat16)


def outer_halves(*operands):
    rows, width = operands[0].shape
    whole = lambda a: pl.BlockSpec(a.shape, lambda _: (0,) * a.ndim)
    out = jax.ShapeDtypeStruct((width // 2, 2 * INNER), jnp.bfloat16)
    own = lax.axis_index("col").astype(jnp.int32).reshape(1)
    return pl.pallas_call(
        outer_kernel,
        grid=(1,),
        out_shape=(out, out),
        in_specs=[pl.BlockSpec(memory_space=pltpu.SMEM)] + [whole(a) for a in operands],
        out_specs=(whole(out), whole(out)),
        scratch_shapes=[pltpu.VMEM((len(operands) // 2, width, rows), jnp.bfloat16)],
        compiler_params=pltpu.CompilerParams(vmem_limit_bytes=22 * 1024 * 1024),
        cost_estimate=LIGHT,
        name="weight_grad_halves",
    )(own, *operands)


def late_kernel(
    own_ref, earlier_ref, tokens_ref, inner_ref, side_ref, above_ref, below_ref,
    o_ref, sent_ref, kept_ref, grad_ref, att_ref, turned,
):
    own = own_ref[0]
    count = inner_ref.shape[0]
    share = sent_ref.shape[0] // 4
    edge = above_ref.shape[0]
    width = inner_ref.shape[1]
    side = side_ref[: count // 2].astype(jnp.float32).reshape(-1, REACH, width)
    is_left = (own == 0).astype(jnp.float32)
    side = jnp.concatenate([side * (1.0 - is_left), side * is_left], axis=1)
    total = inner_ref[...].astype(jnp.float32) + side.reshape(count, width)
    grad_ref[:edge] = (total[:edge] + above_ref[...].astype(jnp.float32)).astype(jnp.bfloat16)
    grad_ref[edge : count - edge] = total[edge : count - edge].astype(jnp.bfloat16)
    grad_ref[count - edge :] = (
        total[count - edge :] + below_ref[...].astype(jnp.float32)
    ).astype(jnp.bfloat16)
    turned[...] = tokens_ref[...].T
    for out_ref, half in ((sent_ref, 1 - own), (kept_ref, own)):
        picked = [
            turned[pl.ds(pl.multiple_of((2 * r + half) * share, 16), share), :] for r in range(4)
        ]
        product = dot(jnp.concatenate(picked, axis=0), grad_ref[...])
        out_ref[...] = product.astype(jnp.bfloat16)
    att_ref[...] = o_ref[:, 64:]


def late_halves(earlier, token_rows, inner, side, above, below, attended):
    rows, width = token_rows.shape
    whole = lambda a: pl.BlockSpec(a.shape, lambda _: (0,) * a.ndim)
    out = jax.ShapeDtypeStruct((width // 2, 2 * INNER), jnp.bfloat16)
    grads = jax.ShapeDtypeStruct((rows, 2 * INNER), jnp.bfloat16)
    att = jax.ShapeDtypeStruct((rows, INNER), jnp.bfloat16)
    operands = (token_rows, inner, side, above, below, attended)
    own = lax.axis_index("col").astype(jnp.int32).reshape(1)
    return pl.pallas_call(
        late_kernel,
        grid=(1,),
        out_shape=(out, out, grads, att),
        in_specs=[pl.BlockSpec(memory_space=pltpu.SMEM)]
        + [pl.BlockSpec(memory_space=pl.ANY)]
        + [whole(a) for a in operands],
        out_specs=(whole(out), whole(out), whole(grads), whole(att)),
        scratch_shapes=[pltpu.VMEM((width, rows), jnp.bfloat16)],
        compiler_params=pltpu.CompilerParams(vmem_limit_bytes=22 * 1024 * 1024),
        cost_estimate=LIGHT,
        name="late_weight_grad_halves",
    )(own, earlier, *operands)


def row_parts_kernel(own_ref, held, dq_ref, dkv_ref, *refs):
    for step, out in enumerate(refs[-5:-1]):
        out[...] = held[own_ref[0] ^ step]
    refs[-1][...] = jnp.concatenate([dq_ref[:, :INNER], dkv_ref[...]], axis=1)


def row_parts(held, dquery, dkv, *earlier):
    rows, small, width = held.shape
    own = lax.axis_index("row").astype(jnp.int32).reshape(1)
    return pl.pallas_call(
        row_parts_kernel,
        grid=(1,),
        out_shape=[jax.ShapeDtypeStruct((small, width), jnp.bfloat16)] * 4
        + [jax.ShapeDtypeStruct((dkv.shape[0], 3 * INNER), jnp.bfloat16)],
        in_specs=[
            pl.BlockSpec(memory_space=pltpu.SMEM),
            pl.BlockSpec((rows, small, width), lambda _: (0, 0, 0)),
            pl.BlockSpec(dquery.shape, lambda _: (0, 0)),
            pl.BlockSpec(dkv.shape, lambda _: (0, 0)),
        ]
        + [pl.BlockSpec(memory_space=pl.ANY)] * len(earlier),
        out_specs=[pl.BlockSpec((small, width), lambda _: (0, 0))] * 4
        + [pl.BlockSpec((dkv.shape[0], 3 * INNER), lambda _: (0, 0))],
        compiler_params=pltpu.CompilerParams(vmem_limit_bytes=16 * 1024 * 1024),
        cost_estimate=LIGHT,
        name="row_parts",
    )(own, held, dquery, dkv, *earlier)


def window_starts(places, extent):
    return jnp.clip(places - REACH, 0, extent - WINDOW)


def window_bias(tile_rows, tile_cols, two_columns):
    row_id = lax.axis_index("row")
    col_id = lax.axis_index("col")
    frame_rows = tile_rows * lax.axis_size("row")
    frame_cols = tile_cols * lax.axis_size("col")
    strips = tile_rows // SIDE
    col_first = col_id * tile_cols
    strip_id = jnp.arange(strips, dtype=jnp.int32)
    first_chunk = row_id * strips - 1
    band_chunk = jnp.clip(row_id * strips + strip_id - 1, 0, frame_rows // SIDE - 3)
    side = jnp.arange(SIDE, dtype=jnp.int32)
    own_cols = col_first + jnp.arange(tile_cols, dtype=jnp.int32)
    low, high = col_first - REACH + side, col_first + tile_cols + side
    spans = [own_cols, jnp.where(col_id == 0, high, low)] if two_columns else [own_cols, low, high]
    chunk_rows = jnp.concatenate([jnp.repeat(side, span.shape[0]) for span in spans])
    chunk_cols = jnp.concatenate([jnp.tile(span, SIDE) for span in spans])
    in_band = jnp.concatenate([SIDE * j + chunk_rows for j in range(3)])
    key_col = jnp.tile(chunk_cols, 3)
    key_row = SIDE * band_chunk[:, None] + in_band[None, :]
    query_row = row_id * tile_rows + SIDE * strip_id[:, None] + jnp.repeat(side, tile_cols)[None, :]
    row_start = window_starts(query_row, frame_rows)
    col_start = window_starts(jnp.tile(own_cols, SIDE), frame_cols)
    row_off = key_row[:, :, None] - row_start[:, None, :]
    col_off = key_col[:, None] - col_start[None, :]
    row_ok = (row_off >= 0) & (row_off < WINDOW)
    col_ok = (col_off >= 0) & (col_off < WINDOW)
    bias = jnp.where(row_ok & col_ok[None], 0.0, MASKED).astype(jnp.float32)
    return (band_chunk - first_chunk).astype(jnp.int32), bias


def after(value, *earlier):
    return lax.optimization_barrier((value,) + earlier)[0]


def cut(block, axis, take):
    own = lax.axis_index(axis)
    return [take(block, own ^ step) for step in range(lax.axis_size(axis))]


def exchanged(parts, axis):
    got = []
    for step, part in enumerate(parts[1:], 1):
        pairs = [(i, i ^ step) for i in range(lax.axis_size(axis))]
        got.append(lax.ppermute(part, axis, pairs))
    return got


def added(kept, got, *earlier):
    if earlier:
        kept = after(kept, *earlier)
    total = kept.astype(jnp.float32)
    for g in got:
        total += g.astype(jnp.float32)
    return total.astype(jnp.bfloat16)


def gathered(block, axis):
    own = lax.axis_index(axis)
    count = lax.axis_size(axis)
    whole = jnp.zeros((count,) + block.shape, block.dtype)
    whole = lax.dynamic_update_index_in_dim(whole, block, own, 0)
    for step in range(1, count):
        got = lax.ppermute(block, axis, [(i, i ^ step) for i in range(count)])
        whole = lax.dynamic_update_index_in_dim(whole, got, own ^ step, 0)
    return whole


def core_sum(sent, kept):
    rows, images = lax.axis_size("row"), lax.axis_size("img")
    width = sent.shape[1]
    share = sent.shape[0] // rows
    kept = kept.reshape(rows, share, width)
    got = lax.ppermute(sent, "col", [(0, 1), (1, 0)]).reshape(rows, share, width)
    held = (kept.astype(jnp.float32) + got.astype(jnp.float32)).astype(jnp.bfloat16)
    small = -(-share // (8 * images)) * 8
    return jnp.pad(held, ((0, 0), (0, images * small - share), (0, 0)))


def image_parts(held):
    small = held.shape[1] // lax.axis_size("img")
    return cut(held, "img", lambda h, j: lax.dynamic_slice_in_dim(h, small * j, small, 1))


def row_sum_in_steps(held):
    own = lax.axis_index("row")
    count = lax.axis_size("row")
    bit = 1
    while bit < count:
        parts = held.reshape((-1, 2) + held.shape[1:])
        mine = (own // bit) % 2
        kept = lax.dynamic_index_in_dim(parts, mine, 1, keepdims=False)
        sent = lax.dynamic_index_in_dim(parts, 1 - mine, 1, keepdims=False)
        got = lax.ppermute(sent, "row", [(i, i ^ bit) for i in range(count)])
        total = kept.astype(jnp.float32) + got.astype(jnp.float32)
        held = total.astype(jnp.bfloat16)
        bit *= 2
    return held[0]


def whole_share(held, share):
    whole = gathered(held, "img")
    return whole.reshape(-1, held.shape[1])[:share].astype(jnp.float32)


def plain_shares(part):
    held = lax.psum_scatter(part, ("row", "col"), scatter_dimension=0, tiled=True)
    return lax.psum(held, "img").astype(jnp.float32)


def local(tokens, qkv_weight, out_weight, upstream):
    _, tile_rows, tile_cols, width = tokens.shape
    token_count = tile_rows * tile_cols
    strips = tile_rows // SIDE
    chunk_own = SIDE * tile_cols
    row_count, col_count = lax.axis_size("row"), lax.axis_size("col")
    two_columns = col_count == 2
    col_id = lax.axis_index("col")
    token_rows = tokens.reshape(token_count, width)
    grad_rows = upstream.reshape(token_count, width)
    turns = (0,) if two_columns else (-1, 1)

    def moved(block, down, turn=None):
        pairs = []
        for r in range(row_count):
            for c in range(col_count):
                to_c = c if turn is None else (1 - c if turn == 0 else c + turn)
                if 0 <= r + down < row_count and 0 <= to_c < col_count:
                    pairs.append((r * col_count + c, (r + down) * col_count + to_c))
        return lax.ppermute(block, ("row", "col"), pairs)

    def edge(block, turn):
        if turn == 0:
            return lax.dynamic_slice_in_dim(block, (1 - col_id) * (tile_cols - REACH), REACH, 1)
        return block[:, tile_cols - REACH :] if turn == 1 else block[:, :REACH]

    def side_of(*blocks):
        got = []
        for turn in sorted(turns, reverse=True):
            near = [edge(block.reshape(-1, tile_cols, 2 * INNER), turn) for block in blocks]
            near = jnp.concatenate(near, axis=0) if len(near) > 1 else near[0]
            got.append(moved(near, 0, turn).reshape(-1, SIDE * REACH, 2 * INNER))
        got = got[0] if two_columns else jnp.concatenate(got, axis=1)
        return got.reshape(-1, 2 * INNER)

    keyvals, top, bottom, near = project(token_rows, qkv_weight, tile_cols)
    queries = lax.dot_general(
        qkv_weight[:, :INNER], token_rows, (((0,), (1,)), ((), ())), preferred_element_type=jnp.float32
    ).astype(jnp.bfloat16)
    above = moved(bottom, 1)
    below = moved(top, -1)
    if two_columns:
        cols = moved(near, 0, 0)
    else:
        cols = side_of(keyvals)
    corner = side_of(above, below)
    grad_att = lax.dot_general(
        out_weight, grad_rows, (((0,), (1,)), ((), ())), preferred_element_type=jnp.float32
    ).astype(jnp.bfloat16)
    start, bias = window_bias(tile_rows, tile_cols, two_columns)
    attended, dquery, inner_grad, edge_grad, side_grad = attention(
        start, queries, keyvals, grad_att, above, below, cols, corner, bias
    )

    def outer(a, b):
        return lax.dot_general(
            a, b, (((0,), (0,)), ((), ())), preferred_element_type=jnp.float32
        ).astype(jnp.bfloat16)

    simple = two_columns and row_count == 4 and lax.axis_size("img") == 4
    if simple:
        early = image_parts(core_sum(*outer_halves(token_rows, dquery, grad_rows, attended)))
        early_got = exchanged(early, "img")
    def spread(side, first):
        side = side.reshape(-1, SIDE, REACH, 2 * INNER).astype(jnp.float32)
        zeros = jnp.zeros((side.shape[0], SIDE, tile_cols - REACH, 2 * INNER), jnp.float32)
        order = [side, zeros] if first else [zeros, side]
        return jnp.concatenate(order, axis=2).reshape(-1, 2 * INNER)

    if two_columns:
        got = moved(side_grad, 0, 0)
        returned = lambda part: jnp.where(col_id == 0, spread(part, False), spread(part, True))
    else:
        halves = side_grad.reshape(strips + 2, 2, SIDE * REACH, 2 * INNER)
        got = jnp.stack([moved(halves[:, 0], 0, -1), moved(halves[:, 1], 0, 1)], axis=1)
        returned = lambda part: spread(part[:, 0], False) + spread(part[:, 1], True)
    got = got.reshape(strips + 2, -1, SIDE * REACH, 2 * INNER)
    outer_grad = edge_grad.astype(jnp.float32) + returned(got[strips:])
    outer_grad = outer_grad.astype(jnp.bfloat16)
    from_below = moved(outer_grad[:chunk_own], -1)
    from_above = moved(outer_grad[chunk_own:], 1)
    if simple:
        side = got.reshape(-1, 2 * INNER)
        sent, kept, dkv, attended = late_halves(
            early_got[-1], token_rows, inner_grad, side, from_above, from_below, attended
        )
    else:
        dquery, attended = dquery[:, :INNER], attended[:, 64:]
        dkv = inner_grad.astype(jnp.float32) + returned(got[:strips])
        rest = jnp.zeros((token_count - chunk_own, 2 * INNER), jnp.float32)
        dkv = dkv + jnp.concatenate([from_above.astype(jnp.float32), rest], axis=0)
        dkv = dkv + jnp.concatenate([rest, from_below.astype(jnp.float32)], axis=0)
        dkv = dkv.astype(jnp.bfloat16)
        dqkv = jnp.concatenate([dquery, dkv], axis=1)
        sublayer_out = nt_dot(attended, out_weight).astype(jnp.bfloat16)
    if simple:
        late = image_parts(core_sum(sent, kept))
        late_got = exchanged(late, "img")
        early = added(early[0], early_got)
        late = added(late[0], late_got, early)
        sublayer_out = nt_dot(attended, out_weight).astype(jnp.bfloat16)
        *early, dqkv = row_parts(early, dquery, dkv, late_got[-1])
        early = added(early[0], exchanged(early, "row"))
        late = row_sum_in_steps(late)
        share = width // (row_count * col_count)
        early, late = whole_share(early, share), whole_share(late, share)
    else:
        early = jnp.concatenate([outer(token_rows, dquery), outer(grad_rows, attended)], axis=1)
        early, late = plain_shares(early), plain_shares(outer(token_rows, dkv))
    tokens_grad = nt_dot(dqkv, qkv_weight).astype(jnp.bfloat16)
    return (
        sublayer_out.reshape(tokens.shape),
        tokens_grad.reshape(tokens.shape),
        jnp.concatenate([early[:, :INNER], late], axis=1),
        early[:, INNER:],
    )


def solution(mesh):
    return jax.shard_map(
        local,
        mesh=mesh,
        in_specs=(P("img", "row", "col", None), P(), P(), P("img", "row", "col", None)),
        out_specs=(
            P("img", "row", "col", None),
            P("img", "row", "col", None),
            P(("row", "col"), None),
            P(("row", "col"), None),
        ),
        check_vma=False,
    )
```

```python
import jax
import jax.numpy as jnp
from jax import lax
from jax.experimental import pallas as pl
from jax.experimental.pallas import tpu as pltpu
from jax.sharding import PartitionSpec as P

H = 8
DH = 72
INNER = H * DH
REACH = 8
WINDOW = 17
SIDE = 8
PAIRS = H // 2
SLAB = 256
V_SHIFT = 64
MASKED = -1e30
SCALE = DH ** (-0.5)
LIGHT = pl.CostEstimate(flops=1, bytes_accessed=1, transcendentals=0)


def shifted_pairs(count, by):
    return [(i, i + by) for i in range(count) if 0 <= i + by < count]


def dot(a, b):
    return jnp.dot(a, b, preferred_element_type=jnp.float32)


def nt_dot(a, b):
    return lax.dot_general(a, b, (((1,), (1,)), ((), ())), preferred_element_type=jnp.float32)


PIECE = 384
PIECES = 2 * INNER // PIECE


def fetch(pairs, sems):
    copies = [pltpu.make_async_copy(*pair, sems.at[n]) for n, pair in enumerate(pairs)]
    for copy in copies:
        copy.start()
    return copies


def weight_pieces(weight_ref, weight):
    return [
        (weight_ref.at[pl.ds(INNER + PIECE * p, PIECE)], weight.at[pl.ds(PIECE * p, PIECE)])
        for p in range(PIECES)
    ]


def edges_kernel(tokens_ref, weight_ref, top_ref, bottom_ref, tokens, weight, sems):
    edge = top_ref.shape[0]
    ends = [(0, 0), (edge, tokens_ref.shape[0] - edge)]
    token_pairs = [
        (tokens_ref.at[pl.ds(there, edge)], tokens.at[pl.ds(here, edge)]) for here, there in ends
    ]
    copies = fetch(token_pairs + weight_pieces(weight_ref, weight), sems)
    copies[0].wait()
    copies[1].wait()
    for p in range(PIECES):
        copies[2 + p].wait()
        lanes = slice(PIECE * p, PIECE * (p + 1))
        part = nt_dot(tokens[...], weight[lanes]).astype(jnp.bfloat16)
        top_ref[:, lanes] = part[:edge]
        bottom_ref[:, lanes] = part[edge:]


def project_kernel(
    own_ref, top_ref, tokens_ref, weight_ref, qt_ref, kv_ref, near_ref, tokens, weight, q_weight, sems
):
    pairs = [(tokens_ref, tokens)] + weight_pieces(weight_ref, weight)
    copies = fetch(pairs + [(weight_ref.at[pl.ds(0, INNER)], q_weight)], sems)
    copies[0].wait()
    for p in range(PIECES):
        copies[1 + p].wait()
        lanes = slice(PIECE * p, PIECE * (p + 1))
        part = nt_dot(tokens[...], weight[lanes])
        kv_ref[:, lanes] = part.astype(jnp.bfloat16)
        grid = part.reshape(near_ref.shape[0] // REACH, -1, PIECE)
        is_right = own_ref[0].astype(jnp.float32)
        near = grid[:, :REACH] * is_right + grid[:, -REACH:] * (1.0 - is_right)
        near_ref[:, lanes] = near.reshape(-1, PIECE).astype(jnp.bfloat16)
    copies[1 + PIECES].wait()
    qt_ref[...] = nt_dot(q_weight[...], tokens[...]).astype(jnp.bfloat16)


def project(token_rows, weight, tile_cols):
    rows, width = token_rows.shape
    edge = SIDE * tile_cols
    own = lax.axis_index("col").astype(jnp.int32).reshape(1)
    shape = lambda count: jax.ShapeDtypeStruct((count, 2 * INNER), jnp.bfloat16)
    block = lambda count: pl.BlockSpec((count, 2 * INNER), lambda _: (0, 0))
    anywhere = pl.BlockSpec(memory_space=pl.ANY)
    top, bottom = pl.pallas_call(
        edges_kernel,
        grid=(1,),
        out_shape=[shape(edge)] * 2,
        in_specs=[anywhere] * 2,
        out_specs=[block(edge)] * 2,
        scratch_shapes=[
            pltpu.VMEM((2 * edge, width), jnp.bfloat16),
            pltpu.VMEM((2 * INNER, width), jnp.bfloat16),
            pltpu.SemaphoreType.DMA((PIECES + 2,)),
        ],
        compiler_params=pltpu.CompilerParams(vmem_limit_bytes=56 * 1024 * 1024),
        cost_estimate=LIGHT,
        name="project_edges",
    )(token_rows, weight.T)
    near = rows // tile_cols * REACH
    queries, keyvals, near = pl.pallas_call(
        project_kernel,
        grid=(1,),
        out_shape=[jax.ShapeDtypeStruct((INNER, rows), jnp.bfloat16), shape(rows), shape(near)],
        in_specs=[pl.BlockSpec(memory_space=pltpu.SMEM)] + [anywhere] * 3,
        out_specs=[pl.BlockSpec((INNER, rows), lambda _: (0, 0)), block(rows), block(near)],
        scratch_shapes=[
            pltpu.VMEM((rows, width), jnp.bfloat16),
            pltpu.VMEM((2 * INNER, width), jnp.bfloat16),
            pltpu.VMEM((INNER, width), jnp.bfloat16),
            pltpu.SemaphoreType.DMA((PIECES + 2,)),
        ],
        compiler_params=pltpu.CompilerParams(vmem_limit_bytes=24 * 1024 * 1024),
        cost_estimate=LIGHT,
        name="project",
    )(own, top, token_rows, weight.T)
    return queries, keyvals, top, bottom, near


def attention_kernel(
    start_ref,
    qt_ref,
    own_ref,
    g_ref,
    above_ref,
    below_ref,
    cols_ref,
    corner_ref,
    bias_ref,
    o_ref,
    dq_ref,
    inner_ref,
    edge_ref,
    side_ref,
    corner_grad_ref,
    kv,
    kvt,
    acc,
    ot,
    dqt,
):
    strips = bias_ref.shape[0]
    chunk = kv.shape[1]
    chunk_own = own_ref.shape[0] // strips
    chunk_side = chunk - chunk_own
    band = 3 * chunk
    token_count = own_ref.shape[0]
    last = strips + 1
    side_order = [strips] + list(range(strips)) + [strips + 1]

    def place(slot, first, part):
        count = part.shape[0]
        kv[slot, first : first + count] = part
        if count < 128:
            filler = jnp.zeros((128 - count, 2 * INNER), part.dtype)
            part = jnp.concatenate([part, filler], axis=0)
        kvt[slot, :, first : first + count] = part.T[:, :count]

    dqt[INNER:, :] = jnp.zeros((64, chunk_own), jnp.float32)
    ot[:64, :] = jnp.zeros((64, chunk_own), jnp.float32)
    for s in range(strips):
        place(s + 1, 0, own_ref[chunk_own * s : chunk_own * (s + 1)])
    for s in range(strips):
        place(s + 1, chunk_own, cols_ref[chunk_side * s : chunk_side * (s + 1)])
    place(0, 0, above_ref[...])
    place(last, 0, below_ref[...])
    for slot, at in ((0, 0), (last, 1)):
        place(slot, chunk_own, corner_ref[chunk_side * at : chunk_side * (at + 1)])
    acc[...] = jnp.zeros_like(acc)

    row = lax.broadcasted_iota(jnp.int32, (2 * DH, chunk_own), 0)
    first_head = row < DH
    mask_a = jnp.where(first_head, 1.0, 0.0).astype(jnp.bfloat16)
    mask_b = jnp.where(first_head, 0.0, 1.0).astype(jnp.bfloat16)
    ones = jnp.ones((16, chunk), jnp.bfloat16)

    def pair_block(part, above):
        block = jnp.concatenate([part * mask_a, part * mask_b], axis=1)
        parts = [block]
        if above:
            parts = [jnp.zeros((above, block.shape[1]), block.dtype)] + parts
        below = SLAB - 2 * DH - above
        if below:
            parts = parts + [jnp.zeros((below, block.shape[1]), block.dtype)]
        return jnp.concatenate(parts, axis=0)

    def pick(both):
        return jnp.where(first_head, both[:, :chunk_own], both[:, chunk_own:])

    def strip(s, carry):
        top = start_ref[s]
        rows = pl.ds(pl.multiple_of(s * chunk_own, chunk_own), chunk_own)
        bias = bias_ref[s]
        bias = jnp.concatenate([bias, bias], axis=1)
        heads = [slice(2 * DH * i, 2 * DH * (i + 1)) for i in range(PAIRS)]
        k_lanes = [slice(128 * i, 128 * i + SLAB) for i in range(PAIRS)]
        v_lanes = [slice(512 + 128 * i, 512 + 128 * i + SLAB) for i in range(PAIRS)]

        def band_of(lanes):
            return kv[pl.ds(top, 3), :, lanes].reshape(band, SLAB)

        def from_keys(lines, weights):
            got = jnp.zeros((2 * DH, SLAB), jnp.float32)
            for j in range(3):
                got += dot(kvt[top + j, lines, :], weights[chunk * j : chunk * (j + 1)])
            return got

        q2 = [pair_block(qt_ref[heads[i], rows], 16 * i) for i in range(PAIRS)]
        g2 = [pair_block(g_ref[heads[i], rows], V_SHIFT + 16 * i) for i in range(PAIRS)]
        prob, inv, row_dot, dscore = [], [], [], []
        for i in range(PAIRS):
            scores = dot(band_of(k_lanes[i]), q2[i]) * SCALE + bias
            top_score = jnp.max(scores, axis=0, keepdims=True)
            prob.append(jnp.exp(scores - top_score).astype(jnp.bfloat16))
        for i in range(PAIRS):
            total = jnp.zeros((16, SLAB), jnp.float32)
            for j in range(3):
                total += dot(ones, prob[i][chunk * j : chunk * (j + 1)])
            inv.append(1.0 / total[:1])
            v_rows = slice(INNER + heads[i].start, INNER + heads[i].stop)
            att = pick(from_keys(v_rows, prob[i]) * inv[i])
            ot[64 + heads[i].start : 64 + heads[i].stop, :] = att
            dots = att * g_ref[heads[i], rows].astype(jnp.float32)
            row_dot.append(
                jnp.concatenate(
                    [
                        jnp.sum(dots[:DH], axis=0, keepdims=True),
                        jnp.sum(dots[DH:], axis=0, keepdims=True),
                    ],
                    axis=1,
                )
            )
        for i in range(PAIRS):
            dprob = dot(band_of(v_lanes[i]), g2[i])
            inv_scale = inv[i] * SCALE
            change = dprob * inv_scale - row_dot[i] * inv_scale
            dscore.append((prob[i].astype(jnp.float32) * change).astype(jnp.bfloat16))
        for i in range(PAIRS):
            dv = nt_dot(prob[i], (g2[i].astype(jnp.float32) * inv[i]).astype(jnp.bfloat16))
            acc[pl.ds(top, 3), :, v_lanes[i]] += dv.reshape(3, chunk, SLAB)
        for i in range(PAIRS):
            dqt[heads[i], :] = pick(from_keys(heads[i], dscore[i]))
            dk = nt_dot(dscore[i], q2[i])
            acc[pl.ds(top, 3), :, k_lanes[i]] += dk.reshape(3, chunk, SLAB)
        o_ref[rows, :] = ot[...].T.astype(jnp.bfloat16)
        dq_ref[rows, :] = dqt[...].T.astype(jnp.bfloat16)
        return carry

    lax.fori_loop(0, strips, strip, 0)
    for slot, at in enumerate(side_order):
        own_grad = acc[slot, :chunk_own].astype(jnp.bfloat16)
        if at < strips:
            inner_ref[chunk_own * at : chunk_own * (at + 1), :] = own_grad
        else:
            edge_ref[chunk_own * (at - strips) : chunk_own * (at - strips + 1), :] = own_grad
        side_grad = acc[slot, chunk_own:].astype(jnp.bfloat16)
        if at < strips:
            side_ref[chunk_side * at : chunk_side * (at + 1), :] = side_grad
        else:
            at -= strips
            corner_grad_ref[chunk_side * at : chunk_side * (at + 1), :] = side_grad


def attention(start, queries, own, grads, above, below, cols, corner, bias):
    strips, band, chunk_own = bias.shape
    chunk = band // 3
    token_count, width = own.shape
    whole = lambda a: pl.BlockSpec(a.shape, lambda _: (0,) * a.ndim)
    outs = (
        jax.ShapeDtypeStruct((token_count, INNER + 64), jnp.bfloat16),
        jax.ShapeDtypeStruct((token_count, INNER + 64), jnp.bfloat16),
        jax.ShapeDtypeStruct(own.shape, jnp.bfloat16),
        jax.ShapeDtypeStruct((2 * chunk_own, width), jnp.bfloat16),
        jax.ShapeDtypeStruct(cols.shape, jnp.bfloat16),
        jax.ShapeDtypeStruct(corner.shape, jnp.bfloat16),
    )
    return pl.pallas_call(
        attention_kernel,
        grid=(1,),
        out_shape=outs,
        in_specs=[
            pl.BlockSpec(memory_space=pltpu.SMEM),
            whole(queries),
            whole(own),
            whole(grads),
            whole(above),
            whole(below),
            whole(cols),
            whole(corner),
            whole(bias),
        ],
        out_specs=tuple(whole(o) for o in outs),
        scratch_shapes=[
            pltpu.VMEM((strips + 2, chunk, width), jnp.bfloat16),
            pltpu.VMEM((strips + 2, width, chunk), jnp.bfloat16),
            pltpu.VMEM((strips + 2, chunk, width), jnp.float32),
            pltpu.VMEM((640, chunk_own), jnp.float32),
            pltpu.VMEM((640, chunk_own), jnp.float32),
        ],
        compiler_params=pltpu.CompilerParams(vmem_limit_bytes=36 * 1024 * 1024),
        cost_estimate=pl.CostEstimate(
            flops=12 * token_count * band * 2 * INNER,
            bytes_accessed=16 * 1024 * 1024,
            transcendentals=token_count * band * H,
        ),
        name="window_attention",
    )(start, queries, own, grads, above, below, cols, corner, bias)


def outer_kernel(own_ref, *refs):
    pairs = (len(refs) - 3) // 2
    operands, (sent_ref, kept_ref, turned) = refs[: 2 * pairs], refs[2 * pairs :]
    share = sent_ref.shape[0] // 4
    for p in range(pairs):
        turned[p] = operands[2 * p][...].T
    for out_ref, half in ((sent_ref, 1 - own_ref[0]), (kept_ref, own_ref[0])):
        products = []
        for p in range(pairs):
            picked = [
                turned[p, pl.ds(pl.multiple_of((2 * r + half) * share, 16), share), :]
                for r in range(4)
            ]
            products.append(dot(jnp.concatenate(picked, axis=0), operands[2 * p + 1][...]))
        if pairs == 1:
            out_ref[...] = products[0].astype(jnp.bfloat16)
        else:
            first, second = products
            out_ref[:, :512] = first[:, :512].astype(jnp.bfloat16)
            out_ref[:, 512:640] = (first[:, 512:] + second[:, :128]).astype(jnp.bfloat16)
            out_ref[:, 640:] = second[:, 128:].astype(jnp.bfloat16)


def outer_halves(*operands):
    rows, width = operands[0].shape
    whole = lambda a: pl.BlockSpec(a.shape, lambda _: (0,) * a.ndim)
    out = jax.ShapeDtypeStruct((width // 2, 2 * INNER), jnp.bfloat16)
    own = lax.axis_index("col").astype(jnp.int32).reshape(1)
    return pl.pallas_call(
        outer_kernel,
        grid=(1,),
        out_shape=(out, out),
        in_specs=[pl.BlockSpec(memory_space=pltpu.SMEM)] + [whole(a) for a in operands],
        out_specs=(whole(out), whole(out)),
        scratch_shapes=[pltpu.VMEM((len(operands) // 2, width, rows), jnp.bfloat16)],
        compiler_params=pltpu.CompilerParams(vmem_limit_bytes=22 * 1024 * 1024),
        cost_estimate=LIGHT,
        name="weight_grad_halves",
    )(own, *operands)


def late_kernel(
    own_ref, first, second, third, tokens_ref, inner_ref, side_ref, above_ref, below_ref,
    dq_ref, o_ref, sent_ref, kept_ref, all_ref, att_ref, turned, grad_ref,
):
    own = own_ref[0]
    count = inner_ref.shape[0]
    share = sent_ref.shape[0] // 4
    edge = above_ref.shape[0]
    width = inner_ref.shape[1]
    side = side_ref[: count // 2].astype(jnp.float32).reshape(-1, REACH, width)
    is_left = (own == 0).astype(jnp.float32)
    side = jnp.concatenate([side * (1.0 - is_left), side * is_left], axis=1)
    total = inner_ref[...].astype(jnp.float32) + side.reshape(count, width)
    grad_ref[:edge] = (total[:edge] + above_ref[...].astype(jnp.float32)).astype(jnp.bfloat16)
    grad_ref[edge : count - edge] = total[edge : count - edge].astype(jnp.bfloat16)
    grad_ref[count - edge :] = (
        total[count - edge :] + below_ref[...].astype(jnp.float32)
    ).astype(jnp.bfloat16)
    turned[...] = tokens_ref[...].T
    for out_ref, half in ((sent_ref, 1 - own), (kept_ref, own)):
        picked = [
            turned[pl.ds(pl.multiple_of((2 * r + half) * share, 16), share), :] for r in range(4)
        ]
        product = dot(jnp.concatenate(picked, axis=0), grad_ref[...])
        out_ref[...] = product.astype(jnp.bfloat16)
    all_ref[...] = jnp.concatenate([dq_ref[:, :INNER], grad_ref[...]], axis=1)
    att_ref[...] = o_ref[:, 64:]


def late_halves(earlier, token_rows, inner, side, above, below, dquery, attended):
    rows, width = token_rows.shape
    whole = lambda a: pl.BlockSpec(a.shape, lambda _: (0,) * a.ndim)
    out = jax.ShapeDtypeStruct((width // 2, 2 * INNER), jnp.bfloat16)
    grads = jax.ShapeDtypeStruct((rows, 3 * INNER), jnp.bfloat16)
    att = jax.ShapeDtypeStruct((rows, INNER), jnp.bfloat16)
    operands = (token_rows, inner, side, above, below, dquery, attended)
    own = lax.axis_index("col").astype(jnp.int32).reshape(1)
    return pl.pallas_call(
        late_kernel,
        grid=(1,),
        out_shape=(out, out, grads, att),
        in_specs=[pl.BlockSpec(memory_space=pltpu.SMEM)]
        + [pl.BlockSpec(memory_space=pl.ANY)] * 3
        + [whole(a) for a in operands],
        out_specs=(whole(out), whole(out), whole(grads), whole(att)),
        scratch_shapes=[
            pltpu.VMEM((width, rows), jnp.bfloat16),
            pltpu.VMEM((rows, 2 * INNER), jnp.bfloat16),
        ],
        compiler_params=pltpu.CompilerParams(vmem_limit_bytes=22 * 1024 * 1024),
        cost_estimate=LIGHT,
        name="late_weight_grad_halves",
    )(own, *earlier, *operands)


def core_parts_kernel(own_ref, kept_ref, got_ref, *refs):
    outs, total = refs[-5:-1], refs[-1]
    rows, padded, _ = total.shape
    share, small = kept_ref.shape[0] // rows, padded // 4
    for r in range(rows):
        part = slice(share * r, share * (r + 1))
        total[r, :share] = kept_ref[part].astype(jnp.float32) + got_ref[part].astype(jnp.float32)
        total[r, share:] = jnp.zeros((padded - share, total.shape[2]), jnp.float32)
    for step, out in enumerate(outs):
        first = pl.multiple_of((own_ref[0] ^ step) * small, 8)
        out[...] = total[:, pl.ds(first, small), :].astype(jnp.bfloat16)


def core_parts(sent, kept, *earlier):
    got = lax.ppermute(sent, "col", [(0, 1), (1, 0)])
    rows, images = lax.axis_size("row"), lax.axis_size("img")
    width = kept.shape[1]
    small = -(-kept.shape[0] // rows // (8 * images)) * 8
    own = lax.axis_index("img").astype(jnp.int32).reshape(1)
    return pl.pallas_call(
        core_parts_kernel,
        grid=(1,),
        out_shape=[jax.ShapeDtypeStruct((rows, small, width), jnp.bfloat16)] * images,
        in_specs=[pl.BlockSpec(memory_space=pltpu.SMEM)]
        + [pl.BlockSpec(kept.shape, lambda _: (0, 0))] * 2
        + [pl.BlockSpec(memory_space=pl.ANY)] * len(earlier),
        out_specs=[pl.BlockSpec((rows, small, width), lambda _: (0, 0, 0))] * images,
        scratch_shapes=[pltpu.VMEM((rows, images * small, width), jnp.float32)],
        compiler_params=pltpu.CompilerParams(vmem_limit_bytes=20 * 1024 * 1024),
        cost_estimate=LIGHT,
        name="core_parts",
    )(own, kept, got, *earlier)


def row_sum_kernel(kept, first, second, third, *refs):
    total = kept[...].astype(jnp.float32) + first[...].astype(jnp.float32)
    total += second[...].astype(jnp.float32)
    refs[-1][...] = (total + third[...].astype(jnp.float32)).astype(jnp.bfloat16)


def row_sum_after(parts, earlier):
    parts = [parts[0]] + exchanged(parts, "row")
    shape = parts[0].shape
    return pl.pallas_call(
        row_sum_kernel,
        grid=(1,),
        out_shape=jax.ShapeDtypeStruct(shape, jnp.bfloat16),
        in_specs=[pl.BlockSpec(shape, lambda _: (0, 0))] * 4 + [pl.BlockSpec(memory_space=pl.ANY)],
        out_specs=pl.BlockSpec(shape, lambda _: (0, 0)),
        compiler_params=pltpu.CompilerParams(vmem_limit_bytes=8 * 1024 * 1024),
        cost_estimate=LIGHT,
        name="row_sum",
    )(*parts, earlier)


def window_starts(places, extent):
    return jnp.clip(places - REACH, 0, extent - WINDOW)


def window_bias(tile_rows, tile_cols, two_columns):
    row_id = lax.axis_index("row")
    col_id = lax.axis_index("col")
    frame_rows = tile_rows * lax.axis_size("row")
    frame_cols = tile_cols * lax.axis_size("col")
    strips = tile_rows // SIDE
    col_first = col_id * tile_cols
    strip_id = jnp.arange(strips, dtype=jnp.int32)
    first_chunk = row_id * strips - 1
    band_chunk = jnp.clip(row_id * strips + strip_id - 1, 0, frame_rows // SIDE - 3)
    side = jnp.arange(SIDE, dtype=jnp.int32)
    own_cols = col_first + jnp.arange(tile_cols, dtype=jnp.int32)
    low, high = col_first - REACH + side, col_first + tile_cols + side
    spans = [own_cols, jnp.where(col_id == 0, high, low)] if two_columns else [own_cols, low, high]
    chunk_rows = jnp.concatenate([jnp.repeat(side, span.shape[0]) for span in spans])
    chunk_cols = jnp.concatenate([jnp.tile(span, SIDE) for span in spans])
    in_band = jnp.concatenate([SIDE * j + chunk_rows for j in range(3)])
    key_col = jnp.tile(chunk_cols, 3)
    key_row = SIDE * band_chunk[:, None] + in_band[None, :]
    query_row = row_id * tile_rows + SIDE * strip_id[:, None] + jnp.repeat(side, tile_cols)[None, :]
    row_start = window_starts(query_row, frame_rows)
    col_start = window_starts(jnp.tile(own_cols, SIDE), frame_cols)
    row_off = key_row[:, :, None] - row_start[:, None, :]
    col_off = key_col[:, None] - col_start[None, :]
    row_ok = (row_off >= 0) & (row_off < WINDOW)
    col_ok = (col_off >= 0) & (col_off < WINDOW)
    bias = jnp.where(row_ok & col_ok[None], 0.0, MASKED).astype(jnp.float32)
    return (band_chunk - first_chunk).astype(jnp.int32), bias


def after(value, *earlier):
    return lax.optimization_barrier((value,) + earlier)[0]


def cut(block, axis, take):
    own = lax.axis_index(axis)
    return [take(block, own ^ step) for step in range(lax.axis_size(axis))]


def exchanged(parts, axis):
    got = []
    for step, part in enumerate(parts[1:], 1):
        pairs = [(i, i ^ step) for i in range(lax.axis_size(axis))]
        got.append(lax.ppermute(part, axis, pairs))
    return got


def added(kept, got, *earlier):
    if earlier:
        kept = after(kept, *earlier)
    total = kept.astype(jnp.float32)
    for g in got:
        total += g.astype(jnp.float32)
    return total.astype(jnp.bfloat16)


def gathered(block, axis):
    own = lax.axis_index(axis)
    count = lax.axis_size(axis)
    whole = jnp.zeros((count,) + block.shape, block.dtype)
    whole = lax.dynamic_update_index_in_dim(whole, block, own, 0)
    for step in range(1, count):
        got = lax.ppermute(block, axis, [(i, i ^ step) for i in range(count)])
        whole = lax.dynamic_update_index_in_dim(whole, got, own ^ step, 0)
    return whole


def row_parts(held):
    return cut(held, "row", lambda h, r: lax.dynamic_index_in_dim(h, r, 0, keepdims=False))


def whole_share(held, share):
    whole = gathered(held, "img")
    return whole.reshape(-1, held.shape[1])[:share].astype(jnp.float32)


def plain_shares(part):
    held = lax.psum_scatter(part, ("row", "col"), scatter_dimension=0, tiled=True)
    return lax.psum(held, "img").astype(jnp.float32)


def local(tokens, qkv_weight, out_weight, upstream):
    _, tile_rows, tile_cols, width = tokens.shape
    token_count = tile_rows * tile_cols
    strips = tile_rows // SIDE
    chunk_own = SIDE * tile_cols
    row_count, col_count = lax.axis_size("row"), lax.axis_size("col")
    two_columns = col_count == 2
    col_id = lax.axis_index("col")
    token_rows = tokens.reshape(token_count, width)
    grad_rows = upstream.reshape(token_count, width)
    turns = (0,) if two_columns else (-1, 1)

    def moved(block, down, turn=None):
        pairs = []
        for r in range(row_count):
            for c in range(col_count):
                to_c = c if turn is None else (1 - c if turn == 0 else c + turn)
                if 0 <= r + down < row_count and 0 <= to_c < col_count:
                    pairs.append((r * col_count + c, (r + down) * col_count + to_c))
        return lax.ppermute(block, ("row", "col"), pairs)

    def edge(block, turn):
        if turn == 0:
            return lax.dynamic_slice_in_dim(block, (1 - col_id) * (tile_cols - REACH), REACH, 1)
        return block[:, tile_cols - REACH :] if turn == 1 else block[:, :REACH]

    def side_of(*blocks):
        got = []
        for turn in sorted(turns, reverse=True):
            near = [edge(block.reshape(-1, tile_cols, 2 * INNER), turn) for block in blocks]
            near = jnp.concatenate(near, axis=0) if len(near) > 1 else near[0]
            got.append(moved(near, 0, turn).reshape(-1, SIDE * REACH, 2 * INNER))
        got = got[0] if two_columns else jnp.concatenate(got, axis=1)
        return got.reshape(-1, 2 * INNER)

    queries, keyvals, top, bottom, near = project(token_rows, qkv_weight, tile_cols)
    above = moved(bottom, 1)
    below = moved(top, -1)
    if two_columns:
        cols = moved(near, 0, 0)
    else:
        cols = side_of(keyvals)
    corner = side_of(above, below)
    grad_att = lax.dot_general(
        out_weight, grad_rows, (((0,), (1,)), ((), ())), preferred_element_type=jnp.float32
    ).astype(jnp.bfloat16)
    start, bias = window_bias(tile_rows, tile_cols, two_columns)
    attended, dquery, inner_grad, edge_grad, side_grad, corner_grad = attention(
        start, queries, keyvals, grad_att, above, below, cols, corner, bias
    )

    def outer(a, b):
        return lax.dot_general(
            a, b, (((0,), (0,)), ((), ())), preferred_element_type=jnp.float32
        ).astype(jnp.bfloat16)

    simple = two_columns and row_count == 4 and lax.axis_size("img") == 4
    if simple:
        early = core_parts(*outer_halves(token_rows, dquery, grad_rows, attended))
    def outputs(attended, dqkv):
        sublayer_out = nt_dot(attended, out_weight).astype(jnp.bfloat16)
        return sublayer_out, nt_dot(dqkv, qkv_weight).astype(jnp.bfloat16)

    def spread(side, first):
        side = side.reshape(-1, SIDE, REACH, 2 * INNER).astype(jnp.float32)
        zeros = jnp.zeros((side.shape[0], SIDE, tile_cols - REACH, 2 * INNER), jnp.float32)
        order = [side, zeros] if first else [zeros, side]
        return jnp.concatenate(order, axis=2).reshape(-1, 2 * INNER)

    def sides_back(part):
        if two_columns:
            return moved(part, 0, 0).reshape(-1, SIDE * REACH, 2 * INNER)
        halves = part.reshape(-1, 2, SIDE * REACH, 2 * INNER)
        return jnp.stack([moved(halves[:, 0], 0, -1), moved(halves[:, 1], 0, 1)], axis=1)

    def returned(part):
        if two_columns:
            return jnp.where(col_id == 0, spread(part, False), spread(part, True))
        return spread(part[:, 0], False) + spread(part[:, 1], True)

    side, corner = sides_back(side_grad), sides_back(corner_grad)
    outer_grad = edge_grad.astype(jnp.float32) + returned(corner)
    outer_grad = outer_grad.astype(jnp.bfloat16)
    from_below = moved(outer_grad[:chunk_own], -1)
    from_above = moved(outer_grad[chunk_own:], 1)
    if simple:
        side = side.reshape(-1, 2 * INNER)
        sent, kept, dqkv, attended = late_halves(
            early[1:], token_rows, inner_grad, side, from_above, from_below, dquery, attended
        )
    else:
        dquery, attended = dquery[:, :INNER], attended[:, 64:]
        dkv = inner_grad.astype(jnp.float32) + returned(side)
        rest = jnp.zeros((token_count - chunk_own, 2 * INNER), jnp.float32)
        dkv = dkv + jnp.concatenate([from_above.astype(jnp.float32), rest], axis=0)
        dkv = dkv + jnp.concatenate([rest, from_below.astype(jnp.float32)], axis=0)
        dkv = dkv.astype(jnp.bfloat16)
        dqkv = jnp.concatenate([dquery, dkv], axis=1)
        sublayer_out, tokens_grad = outputs(attended, dqkv)
    if simple:
        early = added(early[0], exchanged(early, "img"))
        sublayer_out, tokens_grad = outputs(attended, dqkv)
        late = core_parts(sent, kept, early, sublayer_out, tokens_grad)
        late = added(late[0], exchanged(late, "img"), early)
        early = row_sum_after(row_parts(early), late)
        late = row_parts(late)
        late = added(late[0], exchanged(late, "row"), early)
        share = width // (row_count * col_count)
        early, late = whole_share(early, share), whole_share(late, share)
    else:
        early = jnp.concatenate([outer(token_rows, dquery), outer(grad_rows, attended)], axis=1)
        early, late = plain_shares(early), plain_shares(outer(token_rows, dkv))
    return (
        sublayer_out.reshape(tokens.shape),
        tokens_grad.reshape(tokens.shape),
        jnp.concatenate([early[:, :INNER], late], axis=1),
        early[:, INNER:],
    )


def solution(mesh):
    return jax.shard_map(
        local,
        mesh=mesh,
        in_specs=(P("img", "row", "col", None), P(), P(), P("img", "row", "col", None)),
        out_specs=(
            P("img", "row", "col", None),
            P("img", "row", "col", None),
            P(("row", "col"), None),
            P(("row", "col"), None),
        ),
        check_vma=False,
    )
```

```python
import jax
import jax.numpy as jnp
from jax import lax
from jax.experimental import pallas as pl
from jax.experimental.pallas import tpu as pltpu
from jax.sharding import PartitionSpec as P

H = 8
DH = 72
INNER = H * DH
REACH = 8
WINDOW = 17
SIDE = 8
PAIRS = H // 2
SLAB = 256
V_SHIFT = 64
MASKED = -1e30
SCALE = DH ** (-0.5)
LIGHT = pl.CostEstimate(flops=1, bytes_accessed=1, transcendentals=0)


def shifted_pairs(count, by):
    return [(i, i + by) for i in range(count) if 0 <= i + by < count]


def dot(a, b):
    return jnp.dot(a, b, preferred_element_type=jnp.float32)


def nt_dot(a, b):
    return lax.dot_general(a, b, (((1,), (1,)), ((), ())), preferred_element_type=jnp.float32)


PIECE = 384
PIECES = 2 * INNER // PIECE
CUTS = 3


def fetch(pairs, sems):
    copies = [pltpu.make_async_copy(*pair, sems.at[n]) for n, pair in enumerate(pairs)]
    for copy in copies:
        copy.start()
    return copies


def weight_pieces(weight_ref, weight):
    part = PIECE // CUTS
    return [
        (weight_ref.at[pl.ds(INNER + part * p, part)], weight.at[pl.ds(part * p, part)])
        for p in range(PIECES * CUTS)
    ]


def edges_kernel(tokens_ref, weight_ref, top_ref, bottom_ref, tokens, weight, sems):
    edge = top_ref.shape[0]
    ends = [(0, 0), (edge, tokens_ref.shape[0] - edge)]
    token_pairs = [
        (tokens_ref.at[pl.ds(there, edge)], tokens.at[pl.ds(here, edge)]) for here, there in ends
    ]
    copies = fetch(token_pairs + weight_pieces(weight_ref, weight), sems)
    copies[0].wait()
    copies[1].wait()
    for p in range(PIECES):
        for copy in copies[2 + CUTS * p : 2 + CUTS * (p + 1)]:
            copy.wait()
        lanes = slice(PIECE * p, PIECE * (p + 1))
        part = nt_dot(tokens[...], weight[lanes]).astype(jnp.bfloat16)
        top_ref[:, lanes] = part[:edge]
        bottom_ref[:, lanes] = part[edge:]


def project_kernel(
    own_ref, top_ref, tokens_ref, weight_ref, qt_ref, kv_ref, near_ref, tokens, weight, q_weight, sems
):
    pairs = [(tokens_ref, tokens)] + weight_pieces(weight_ref, weight)
    copies = fetch(pairs + [(weight_ref.at[pl.ds(0, INNER)], q_weight)], sems)
    copies[0].wait()
    for p in range(PIECES):
        for copy in copies[1 + CUTS * p : 1 + CUTS * (p + 1)]:
            copy.wait()
        lanes = slice(PIECE * p, PIECE * (p + 1))
        part = nt_dot(tokens[...], weight[lanes])
        kv_ref[:, lanes] = part.astype(jnp.bfloat16)
        grid = part.reshape(near_ref.shape[0] // REACH, -1, PIECE)
        is_right = own_ref[0].astype(jnp.float32)
        near = grid[:, :REACH] * is_right + grid[:, -REACH:] * (1.0 - is_right)
        near_ref[:, lanes] = near.reshape(-1, PIECE).astype(jnp.bfloat16)
    copies[-1].wait()
    qt_ref[...] = nt_dot(q_weight[...], tokens[...]).astype(jnp.bfloat16)


def project(token_rows, weight, tile_cols):
    rows, width = token_rows.shape
    edge = SIDE * tile_cols
    own = lax.axis_index("col").astype(jnp.int32).reshape(1)
    shape = lambda count: jax.ShapeDtypeStruct((count, 2 * INNER), jnp.bfloat16)
    block = lambda count: pl.BlockSpec((count, 2 * INNER), lambda _: (0, 0))
    anywhere = pl.BlockSpec(memory_space=pl.ANY)
    top, bottom = pl.pallas_call(
        edges_kernel,
        grid=(1,),
        out_shape=[shape(edge)] * 2,
        in_specs=[anywhere] * 2,
        out_specs=[block(edge)] * 2,
        scratch_shapes=[
            pltpu.VMEM((2 * edge, width), jnp.bfloat16),
            pltpu.VMEM((2 * INNER, width), jnp.bfloat16),
            pltpu.SemaphoreType.DMA((PIECES * CUTS + 2,)),
        ],
        compiler_params=pltpu.CompilerParams(vmem_limit_bytes=56 * 1024 * 1024),
        cost_estimate=LIGHT,
        name="project_edges",
    )(token_rows, weight.T)
    near = rows // tile_cols * REACH
    queries, keyvals, near = pl.pallas_call(
        project_kernel,
        grid=(1,),
        out_shape=[jax.ShapeDtypeStruct((INNER, rows), jnp.bfloat16), shape(rows), shape(near)],
        in_specs=[pl.BlockSpec(memory_space=pltpu.SMEM)] + [anywhere] * 3,
        out_specs=[pl.BlockSpec((INNER, rows), lambda _: (0, 0)), block(rows), block(near)],
        scratch_shapes=[
            pltpu.VMEM((rows, width), jnp.bfloat16),
            pltpu.VMEM((2 * INNER, width), jnp.bfloat16),
            pltpu.VMEM((INNER, width), jnp.bfloat16),
            pltpu.SemaphoreType.DMA((PIECES * CUTS + 2,)),
        ],
        compiler_params=pltpu.CompilerParams(vmem_limit_bytes=56 * 1024 * 1024),
        cost_estimate=LIGHT,
        name="project",
    )(own, top, token_rows, weight.T)
    return queries, keyvals, top, bottom, near


def attention_kernel(
    start_ref,
    core_ref,
    tokens_ref,
    upstream_ref,
    qt_ref,
    own_ref,
    g_ref,
    above_ref,
    below_ref,
    cols_ref,
    corner_ref,
    bias_ref,
    o_ref,
    dq_ref,
    inner_ref,
    edge_ref,
    side_ref,
    corner_grad_ref,
    sent_ref,
    kept_ref,
    kv,
    kvt,
    acc,
    ot,
    dqt,
    left,
    turned,
    sems,
):
    strips = bias_ref.shape[0]
    chunk = kv.shape[1]
    chunk_own = own_ref.shape[0] // strips
    chunk_side = chunk - chunk_own
    band = 3 * chunk
    token_count = own_ref.shape[0]
    last = strips + 1
    side_order = [strips] + list(range(strips)) + [strips + 1]

    def place(slot, first, part):
        count = part.shape[0]
        kv[slot, first : first + count] = part
        if count < 128:
            filler = jnp.zeros((128 - count, 2 * INNER), part.dtype)
            part = jnp.concatenate([part, filler], axis=0)
        kvt[slot, :, first : first + count] = part.T[:, :count]

    copies = fetch([(tokens_ref, left.at[0]), (upstream_ref, left.at[1])], sems)
    dqt[INNER:, :] = jnp.zeros((64, chunk_own), jnp.float32)
    ot[:64, :] = jnp.zeros((64, chunk_own), jnp.float32)
    for s in range(strips):
        place(s + 1, 0, own_ref[chunk_own * s : chunk_own * (s + 1)])
    for s in range(strips):
        place(s + 1, chunk_own, cols_ref[chunk_side * s : chunk_side * (s + 1)])
    place(0, 0, above_ref[...])
    place(last, 0, below_ref[...])
    for slot, at in ((0, 0), (last, 1)):
        place(slot, chunk_own, corner_ref[chunk_side * at : chunk_side * (at + 1)])
    acc[...] = jnp.zeros_like(acc)

    row = lax.broadcasted_iota(jnp.int32, (2 * DH, chunk_own), 0)
    first_head = row < DH
    mask_a = jnp.where(first_head, 1.0, 0.0).astype(jnp.bfloat16)
    mask_b = jnp.where(first_head, 0.0, 1.0).astype(jnp.bfloat16)
    ones = jnp.ones((16, chunk), jnp.bfloat16)

    def pair_block(part, above):
        block = jnp.concatenate([part * mask_a, part * mask_b], axis=1)
        parts = [block]
        if above:
            parts = [jnp.zeros((above, block.shape[1]), block.dtype)] + parts
        below = SLAB - 2 * DH - above
        if below:
            parts = parts + [jnp.zeros((below, block.shape[1]), block.dtype)]
        return jnp.concatenate(parts, axis=0)

    def pick(both):
        return jnp.where(first_head, both[:, :chunk_own], both[:, chunk_own:])

    def strip(s, carry):
        top = start_ref[s]
        rows = pl.ds(pl.multiple_of(s * chunk_own, chunk_own), chunk_own)
        bias = bias_ref[s]
        bias = jnp.concatenate([bias, bias], axis=1)
        heads = [slice(2 * DH * i, 2 * DH * (i + 1)) for i in range(PAIRS)]
        k_lanes = [slice(128 * i, 128 * i + SLAB) for i in range(PAIRS)]
        v_lanes = [slice(512 + 128 * i, 512 + 128 * i + SLAB) for i in range(PAIRS)]

        def band_of(lanes):
            return kv[pl.ds(top, 3), :, lanes].reshape(band, SLAB)

        def from_keys(lines, weights):
            got = jnp.zeros((2 * DH, SLAB), jnp.float32)
            for j in range(3):
                got += dot(kvt[top + j, lines, :], weights[chunk * j : chunk * (j + 1)])
            return got

        q2 = [pair_block(qt_ref[heads[i], rows], 16 * i) for i in range(PAIRS)]
        g2 = [pair_block(g_ref[heads[i], rows], V_SHIFT + 16 * i) for i in range(PAIRS)]
        prob, inv, row_dot, dscore = [], [], [], []
        for i in range(PAIRS):
            scores = dot(band_of(k_lanes[i]), q2[i]) * SCALE + bias
            top_score = jnp.max(scores, axis=0, keepdims=True)
            prob.append(jnp.exp(scores - top_score).astype(jnp.bfloat16))
        for i in range(PAIRS):
            total = jnp.zeros((16, SLAB), jnp.float32)
            for j in range(3):
                total += dot(ones, prob[i][chunk * j : chunk * (j + 1)])
            inv.append(1.0 / total[:1])
            v_rows = slice(INNER + heads[i].start, INNER + heads[i].stop)
            att = pick(from_keys(v_rows, prob[i]) * inv[i])
            ot[64 + heads[i].start : 64 + heads[i].stop, :] = att
            dots = att * g_ref[heads[i], rows].astype(jnp.float32)
            row_dot.append(
                jnp.concatenate(
                    [
                        jnp.sum(dots[:DH], axis=0, keepdims=True),
                        jnp.sum(dots[DH:], axis=0, keepdims=True),
                    ],
                    axis=1,
                )
            )
        for i in range(PAIRS):
            dprob = dot(band_of(v_lanes[i]), g2[i])
            inv_scale = inv[i] * SCALE
            change = dprob * inv_scale - row_dot[i] * inv_scale
            dscore.append((prob[i].astype(jnp.float32) * change).astype(jnp.bfloat16))
        for i in range(PAIRS):
            dv = nt_dot(prob[i], (g2[i].astype(jnp.float32) * inv[i]).astype(jnp.bfloat16))
            acc[pl.ds(top, 3), :, v_lanes[i]] += dv.reshape(3, chunk, SLAB)
        for i in range(PAIRS):
            dqt[heads[i], :] = pick(from_keys(heads[i], dscore[i]))
            dk = nt_dot(dscore[i], q2[i])
            acc[pl.ds(top, 3), :, k_lanes[i]] += dk.reshape(3, chunk, SLAB)
        o_ref[rows, :] = ot[...].T.astype(jnp.bfloat16)
        dq_ref[rows, :] = dqt[...].T.astype(jnp.bfloat16)
        for side in range(2):
            turned[side, :, rows] = left[side, rows, :].T
        return carry

    for copy in copies:
        copy.wait()
    lax.fori_loop(0, strips, strip, 0)
    share = sent_ref.shape[0] // 4
    for out_ref, half in ((sent_ref, 1 - core_ref[0]), (kept_ref, core_ref[0])):
        products = []
        for side, right in enumerate((dq_ref, o_ref)):
            picked = [
                turned[side, pl.ds(pl.multiple_of((2 * r + half) * share, 16), share), :]
                for r in range(4)
            ]
            products.append(dot(jnp.concatenate(picked, axis=0), right[...]))
        first, second = products
        out_ref[:, :512] = first[:, :512].astype(jnp.bfloat16)
        out_ref[:, 512:640] = (first[:, 512:] + second[:, :128]).astype(jnp.bfloat16)
        out_ref[:, 640:] = second[:, 128:].astype(jnp.bfloat16)
    for slot, at in enumerate(side_order):
        own_grad = acc[slot, :chunk_own].astype(jnp.bfloat16)
        if at < strips:
            inner_ref[chunk_own * at : chunk_own * (at + 1), :] = own_grad
        else:
            edge_ref[chunk_own * (at - strips) : chunk_own * (at - strips + 1), :] = own_grad
        side_grad = acc[slot, chunk_own:].astype(jnp.bfloat16)
        if at < strips:
            side_ref[chunk_side * at : chunk_side * (at + 1), :] = side_grad
        else:
            at -= strips
            corner_grad_ref[chunk_side * at : chunk_side * (at + 1), :] = side_grad


def attention(start, token_rows, grad_rows, queries, own, grads, above, below, cols, corner, bias):
    strips, band, chunk_own = bias.shape
    chunk = band // 3
    token_count, width = own.shape
    whole = lambda a: pl.BlockSpec(
        a.shape, lambda _: (0,) * a.ndim, pipeline_mode=pl.Buffered(1)
    )
    outs = (
        jax.ShapeDtypeStruct((token_count, INNER + 64), jnp.bfloat16),
        jax.ShapeDtypeStruct((token_count, INNER + 64), jnp.bfloat16),
        jax.ShapeDtypeStruct(own.shape, jnp.bfloat16),
        jax.ShapeDtypeStruct((2 * chunk_own, width), jnp.bfloat16),
        jax.ShapeDtypeStruct(cols.shape, jnp.bfloat16),
        jax.ShapeDtypeStruct(corner.shape, jnp.bfloat16),
        jax.ShapeDtypeStruct((token_rows.shape[1] // 2, width), jnp.bfloat16),
        jax.ShapeDtypeStruct((token_rows.shape[1] // 2, width), jnp.bfloat16),
    )
    core = lax.axis_index("col").astype(jnp.int32).reshape(1) % 2
    return pl.pallas_call(
        attention_kernel,
        grid=(1,),
        out_shape=outs,
        in_specs=[
            pl.BlockSpec(memory_space=pltpu.SMEM),
            pl.BlockSpec(memory_space=pltpu.SMEM),
            pl.BlockSpec(memory_space=pl.ANY),
            pl.BlockSpec(memory_space=pl.ANY),
            whole(queries),
            whole(own),
            whole(grads),
            whole(above),
            whole(below),
            whole(cols),
            whole(corner),
            whole(bias),
        ],
        out_specs=tuple(whole(o) for o in outs),
        scratch_shapes=[
            pltpu.VMEM((strips + 2, chunk, width), jnp.bfloat16),
            pltpu.VMEM((strips + 2, width, chunk), jnp.bfloat16),
            pltpu.VMEM((strips + 2, chunk, width), jnp.float32),
            pltpu.VMEM((640, chunk_own), jnp.float32),
            pltpu.VMEM((640, chunk_own), jnp.float32),
            pltpu.VMEM((2,) + token_rows.shape, jnp.bfloat16),
            pltpu.VMEM((2,) + token_rows.shape[::-1], jnp.bfloat16),
            pltpu.SemaphoreType.DMA((2,)),
        ],
        compiler_params=pltpu.CompilerParams(vmem_limit_bytes=34 * 1024 * 1024),
        cost_estimate=pl.CostEstimate(
            flops=12 * token_count * band * 2 * INNER,
            bytes_accessed=16 * 1024 * 1024,
            transcendentals=token_count * band * H,
        ),
        name="window_attention",
    )(start, core, token_rows, grad_rows, queries, own, grads, above, below, cols, corner, bias)


def late_kernel(
    own_ref, first, second, third, tokens_ref, inner_ref, side_ref, above_ref, below_ref,
    dq_ref, o_ref, sent_ref, kept_ref, all_ref, att_ref, turned, grad_ref,
):
    own = own_ref[0]
    count = inner_ref.shape[0]
    share = sent_ref.shape[0] // 4
    edge = above_ref.shape[0]
    width = inner_ref.shape[1]
    side = side_ref[: count // 2].astype(jnp.float32).reshape(-1, REACH, width)
    is_left = (own == 0).astype(jnp.float32)
    side = jnp.concatenate([side * (1.0 - is_left), side * is_left], axis=1)
    total = inner_ref[...].astype(jnp.float32) + side.reshape(count, width)
    grad_ref[:edge] = (total[:edge] + above_ref[...].astype(jnp.float32)).astype(jnp.bfloat16)
    grad_ref[edge : count - edge] = total[edge : count - edge].astype(jnp.bfloat16)
    grad_ref[count - edge :] = (
        total[count - edge :] + below_ref[...].astype(jnp.float32)
    ).astype(jnp.bfloat16)
    turned[...] = tokens_ref[...].T
    for out_ref, half in ((sent_ref, 1 - own), (kept_ref, own)):
        picked = [
            turned[pl.ds(pl.multiple_of((2 * r + half) * share, 16), share), :] for r in range(4)
        ]
        product = dot(jnp.concatenate(picked, axis=0), grad_ref[...])
        out_ref[...] = product.astype(jnp.bfloat16)
    all_ref[...] = jnp.concatenate([dq_ref[:, :INNER], grad_ref[...]], axis=1)
    att_ref[...] = o_ref[:, 64:]


def late_halves(earlier, token_rows, inner, side, above, below, dquery, attended):
    rows, width = token_rows.shape
    whole = lambda a: pl.BlockSpec(a.shape, lambda _: (0,) * a.ndim)
    out = jax.ShapeDtypeStruct((width // 2, 2 * INNER), jnp.bfloat16)
    grads = jax.ShapeDtypeStruct((rows, 3 * INNER), jnp.bfloat16)
    att = jax.ShapeDtypeStruct((rows, INNER), jnp.bfloat16)
    operands = (token_rows, inner, side, above, below, dquery, attended)
    own = lax.axis_index("col").astype(jnp.int32).reshape(1)
    return pl.pallas_call(
        late_kernel,
        grid=(1,),
        out_shape=(out, out, grads, att),
        in_specs=[pl.BlockSpec(memory_space=pltpu.SMEM)]
        + [pl.BlockSpec(memory_space=pl.ANY)] * 3
        + [whole(a) for a in operands],
        out_specs=(whole(out), whole(out), whole(grads), whole(att)),
        scratch_shapes=[
            pltpu.VMEM((width, rows), jnp.bfloat16),
            pltpu.VMEM((rows, 2 * INNER), jnp.bfloat16),
        ],
        compiler_params=pltpu.CompilerParams(vmem_limit_bytes=22 * 1024 * 1024),
        cost_estimate=LIGHT,
        name="late_weight_grad_halves",
    )(own, *earlier, *operands)


def core_parts_kernel(own_ref, kept_ref, got_ref, *refs):
    outs, total = refs[-5:-1], refs[-1]
    rows, padded, _ = total.shape
    share, small = kept_ref.shape[0] // rows, padded // 4
    for r in range(rows):
        part = slice(share * r, share * (r + 1))
        total[r, :share] = kept_ref[part].astype(jnp.float32) + got_ref[part].astype(jnp.float32)
        total[r, share:] = jnp.zeros((padded - share, total.shape[2]), jnp.float32)
    for step, out in enumerate(outs):
        first = pl.multiple_of((own_ref[0] ^ step) * small, 8)
        out[...] = total[:, pl.ds(first, small), :].astype(jnp.bfloat16)


def core_parts(sent, kept, *earlier):
    got = lax.ppermute(sent, "col", [(0, 1), (1, 0)])
    rows, images = lax.axis_size("row"), lax.axis_size("img")
    width = kept.shape[1]
    small = -(-kept.shape[0] // rows // (8 * images)) * 8
    own = lax.axis_index("img").astype(jnp.int32).reshape(1)
    return pl.pallas_call(
        core_parts_kernel,
        grid=(1,),
        out_shape=[jax.ShapeDtypeStruct((rows, small, width), jnp.bfloat16)] * images,
        in_specs=[pl.BlockSpec(memory_space=pltpu.SMEM)]
        + [pl.BlockSpec(kept.shape, lambda _: (0, 0))] * 2
        + [pl.BlockSpec(memory_space=pl.ANY)] * len(earlier),
        out_specs=[pl.BlockSpec((rows, small, width), lambda _: (0, 0, 0))] * images,
        scratch_shapes=[pltpu.VMEM((rows, images * small, width), jnp.float32)],
        compiler_params=pltpu.CompilerParams(vmem_limit_bytes=20 * 1024 * 1024),
        cost_estimate=LIGHT,
        name="core_parts",
    )(own, kept, got, *earlier)


def row_sum_kernel(kept, first, second, third, *refs):
    total = kept[...].astype(jnp.float32) + first[...].astype(jnp.float32)
    total += second[...].astype(jnp.float32)
    refs[-1][...] = (total + third[...].astype(jnp.float32)).astype(jnp.bfloat16)


def row_sum_after(parts, earlier):
    parts = [parts[0]] + exchanged(parts, "row")
    shape = parts[0].shape
    return pl.pallas_call(
        row_sum_kernel,
        grid=(1,),
        out_shape=jax.ShapeDtypeStruct(shape, jnp.bfloat16),
        in_specs=[pl.BlockSpec(shape, lambda _: (0, 0))] * 4 + [pl.BlockSpec(memory_space=pl.ANY)],
        out_specs=pl.BlockSpec(shape, lambda _: (0, 0)),
        compiler_params=pltpu.CompilerParams(vmem_limit_bytes=8 * 1024 * 1024),
        cost_estimate=LIGHT,
        name="row_sum",
    )(*parts, earlier)


def outputs_kernel(own_ref, *refs):
    parts, (qkv_ref, out_ref, early, late) = refs[:8], refs[8:]
    share = qkv_ref.shape[0]
    small = parts[0].shape[0]
    for step in range(4):
        first = pl.multiple_of((own_ref[0] ^ step) * small, 8)
        early[pl.ds(first, small), :] = parts[step][...].astype(jnp.float32)
        late[pl.ds(first, small), :] = parts[4 + step][...].astype(jnp.float32)
    qkv_ref[...] = jnp.concatenate([early[:share, :INNER], late[:share]], axis=1)
    out_ref[...] = early[:share, INNER:]


def written_outputs(early, late, share):
    small, width = early[0].shape
    parts = early + late
    own = lax.axis_index("img").astype(jnp.int32).reshape(1)
    shapes = [(share, 3 * INNER), (share, INNER)]
    return pl.pallas_call(
        outputs_kernel,
        grid=(1,),
        out_shape=[jax.ShapeDtypeStruct(shape, jnp.float32) for shape in shapes],
        in_specs=[pl.BlockSpec(memory_space=pltpu.SMEM)]
        + [pl.BlockSpec((small, width), lambda _: (0, 0))] * len(parts),
        out_specs=[pl.BlockSpec(shape, lambda _: (0, 0)) for shape in shapes],
        scratch_shapes=[pltpu.VMEM((len(early) * small, width), jnp.float32)] * 2,
        compiler_params=pltpu.CompilerParams(vmem_limit_bytes=16 * 1024 * 1024),
        cost_estimate=LIGHT,
        name="weight_grads",
    )(own, *parts)


def window_starts(places, extent):
    return jnp.clip(places - REACH, 0, extent - WINDOW)


def window_bias(tile_rows, tile_cols, two_columns):
    row_id = lax.axis_index("row")
    col_id = lax.axis_index("col")
    frame_rows = tile_rows * lax.axis_size("row")
    frame_cols = tile_cols * lax.axis_size("col")
    strips = tile_rows // SIDE
    col_first = col_id * tile_cols
    strip_id = jnp.arange(strips, dtype=jnp.int32)
    first_chunk = row_id * strips - 1
    band_chunk = jnp.clip(row_id * strips + strip_id - 1, 0, frame_rows // SIDE - 3)
    side = jnp.arange(SIDE, dtype=jnp.int32)
    own_cols = col_first + jnp.arange(tile_cols, dtype=jnp.int32)
    low, high = col_first - REACH + side, col_first + tile_cols + side
    spans = [own_cols, jnp.where(col_id == 0, high, low)] if two_columns else [own_cols, low, high]
    chunk_rows = jnp.concatenate([jnp.repeat(side, span.shape[0]) for span in spans])
    chunk_cols = jnp.concatenate([jnp.tile(span, SIDE) for span in spans])
    in_band = jnp.concatenate([SIDE * j + chunk_rows for j in range(3)])
    key_col = jnp.tile(chunk_cols, 3)
    key_row = SIDE * band_chunk[:, None] + in_band[None, :]
    query_row = row_id * tile_rows + SIDE * strip_id[:, None] + jnp.repeat(side, tile_cols)[None, :]
    row_start = window_starts(query_row, frame_rows)
    col_start = window_starts(jnp.tile(own_cols, SIDE), frame_cols)
    row_off = key_row[:, :, None] - row_start[:, None, :]
    col_off = key_col[:, None] - col_start[None, :]
    row_ok = (row_off >= 0) & (row_off < WINDOW)
    col_ok = (col_off >= 0) & (col_off < WINDOW)
    bias = jnp.where(row_ok & col_ok[None], 0.0, MASKED).astype(jnp.float32)
    return (band_chunk - first_chunk).astype(jnp.int32), bias


def after(value, *earlier):
    return lax.optimization_barrier((value,) + earlier)[0]


def cut(block, axis, take):
    own = lax.axis_index(axis)
    return [take(block, own ^ step) for step in range(lax.axis_size(axis))]


def exchanged(parts, axis):
    got = []
    for step, part in enumerate(parts[1:], 1):
        pairs = [(i, i ^ step) for i in range(lax.axis_size(axis))]
        got.append(lax.ppermute(part, axis, pairs))
    return got


def added(kept, got, *earlier):
    if earlier:
        kept = after(kept, *earlier)
    total = kept.astype(jnp.float32)
    for g in got:
        total += g.astype(jnp.float32)
    return total.astype(jnp.bfloat16)


def row_parts(held):
    return cut(held, "row", lambda h, r: lax.dynamic_index_in_dim(h, r, 0, keepdims=False))


def plain_shares(part):
    held = lax.psum_scatter(part, ("row", "col"), scatter_dimension=0, tiled=True)
    return lax.psum(held, "img").astype(jnp.float32)


def local(tokens, qkv_weight, out_weight, upstream):
    _, tile_rows, tile_cols, width = tokens.shape
    token_count = tile_rows * tile_cols
    strips = tile_rows // SIDE
    chunk_own = SIDE * tile_cols
    row_count, col_count = lax.axis_size("row"), lax.axis_size("col")
    two_columns = col_count == 2
    col_id = lax.axis_index("col")
    token_rows = tokens.reshape(token_count, width)
    grad_rows = upstream.reshape(token_count, width)
    turns = (0,) if two_columns else (-1, 1)

    def moved(block, down, turn=None):
        pairs = []
        for r in range(row_count):
            for c in range(col_count):
                to_c = c if turn is None else (1 - c if turn == 0 else c + turn)
                if 0 <= r + down < row_count and 0 <= to_c < col_count:
                    pairs.append((r * col_count + c, (r + down) * col_count + to_c))
        return lax.ppermute(block, ("row", "col"), pairs)

    def edge(block, turn):
        if turn == 0:
            return lax.dynamic_slice_in_dim(block, (1 - col_id) * (tile_cols - REACH), REACH, 1)
        return block[:, tile_cols - REACH :] if turn == 1 else block[:, :REACH]

    def side_of(*blocks):
        got = []
        for turn in sorted(turns, reverse=True):
            near = [edge(block.reshape(-1, tile_cols, 2 * INNER), turn) for block in blocks]
            near = jnp.concatenate(near, axis=0) if len(near) > 1 else near[0]
            got.append(moved(near, 0, turn).reshape(-1, SIDE * REACH, 2 * INNER))
        got = got[0] if two_columns else jnp.concatenate(got, axis=1)
        return got.reshape(-1, 2 * INNER)

    queries, keyvals, top, bottom, near = project(token_rows, qkv_weight, tile_cols)
    above = moved(bottom, 1)
    below = moved(top, -1)
    if two_columns:
        cols = moved(near, 0, 0)
    else:
        cols = side_of(keyvals)
    corner = side_of(above, below)
    grad_att = lax.dot_general(
        out_weight, grad_rows, (((0,), (1,)), ((), ())), preferred_element_type=jnp.float32
    ).astype(jnp.bfloat16)
    start, bias = window_bias(tile_rows, tile_cols, two_columns)
    attended, dquery, inner_grad, edge_grad, side_grad, corner_grad, sent, kept = attention(
        start, token_rows, grad_rows, queries, keyvals, grad_att, above, below, cols, corner, bias
    )

    def outer(a, b):
        return lax.dot_general(
            a, b, (((0,), (0,)), ((), ())), preferred_element_type=jnp.float32
        ).astype(jnp.bfloat16)

    simple = two_columns and row_count == 4 and lax.axis_size("img") == 4
    if simple:
        early = core_parts(sent, kept)
    def outputs(attended, dqkv):
        sublayer_out = nt_dot(attended, out_weight).astype(jnp.bfloat16)
        return sublayer_out, nt_dot(dqkv, qkv_weight).astype(jnp.bfloat16)

    def spread(side, first):
        side = side.reshape(-1, SIDE, REACH, 2 * INNER).astype(jnp.float32)
        zeros = jnp.zeros((side.shape[0], SIDE, tile_cols - REACH, 2 * INNER), jnp.float32)
        order = [side, zeros] if first else [zeros, side]
        return jnp.concatenate(order, axis=2).reshape(-1, 2 * INNER)

    def sides_back(part):
        if two_columns:
            return moved(part, 0, 0).reshape(-1, SIDE * REACH, 2 * INNER)
        halves = part.reshape(-1, 2, SIDE * REACH, 2 * INNER)
        return jnp.stack([moved(halves[:, 0], 0, -1), moved(halves[:, 1], 0, 1)], axis=1)

    def returned(part):
        if two_columns:
            return jnp.where(col_id == 0, spread(part, False), spread(part, True))
        return spread(part[:, 0], False) + spread(part[:, 1], True)

    side, corner = sides_back(side_grad), sides_back(corner_grad)
    outer_grad = edge_grad.astype(jnp.float32) + returned(corner)
    outer_grad = outer_grad.astype(jnp.bfloat16)
    from_below = moved(outer_grad[:chunk_own], -1)
    from_above = moved(outer_grad[chunk_own:], 1)
    if simple:
        side = side.reshape(-1, 2 * INNER)
        sent, kept, dqkv, attended = late_halves(
            early[1:], token_rows, inner_grad, side, from_above, from_below, dquery, attended
        )
    else:
        dquery, attended = dquery[:, :INNER], attended[:, 64:]
        dkv = inner_grad.astype(jnp.float32) + returned(side)
        rest = jnp.zeros((token_count - chunk_own, 2 * INNER), jnp.float32)
        dkv = dkv + jnp.concatenate([from_above.astype(jnp.float32), rest], axis=0)
        dkv = dkv + jnp.concatenate([rest, from_below.astype(jnp.float32)], axis=0)
        dkv = dkv.astype(jnp.bfloat16)
        dqkv = jnp.concatenate([dquery, dkv], axis=1)
        sublayer_out, tokens_grad = outputs(attended, dqkv)
    if simple:
        early = added(early[0], exchanged(early, "img"))
        sublayer_out, tokens_grad = outputs(attended, dqkv)
        late = core_parts(sent, kept, early, sublayer_out, tokens_grad)
        late_got = exchanged(late, "img")
        late = added(late[0], late_got, early)
        early = row_sum_after(row_parts(early), late_got[0])
        late = row_parts(late)
        late = added(late[0], exchanged(late, "row"), early)
        share = width // (row_count * col_count)
        early = [early] + exchanged([early] * 4, "img")
        late = [late] + exchanged([late] * 4, "img")
        qkv_grad, out_grad = written_outputs(early, late, share)
    else:
        early = jnp.concatenate([outer(token_rows, dquery), outer(grad_rows, attended)], axis=1)
        early, late = plain_shares(early), plain_shares(outer(token_rows, dkv))
        qkv_grad = jnp.concatenate([early[:, :INNER], late], axis=1)
        out_grad = early[:, INNER:]
    return (
        sublayer_out.reshape(tokens.shape),
        tokens_grad.reshape(tokens.shape),
        qkv_grad,
        out_grad,
    )


def solution(mesh):
    return jax.shard_map(
        local,
        mesh=mesh,
        in_specs=(P("img", "row", "col", None), P(), P(), P("img", "row", "col", None)),
        out_specs=(
            P("img", "row", "col", None),
            P("img", "row", "col", None),
            P(("row", "col"), None),
            P(("row", "col"), None),
        ),
        check_vma=False,
    )
```

```python
import jax
import jax.numpy as jnp
from jax import lax
from jax.experimental import pallas as pl
from jax.experimental.pallas import tpu as pltpu
from jax.sharding import PartitionSpec as P

H = 8
DH = 72
INNER = H * DH
REACH = 8
WINDOW = 17
SIDE = 8
PAIRS = H // 2
SLAB = 256
V_SHIFT = 64
MASKED = -1e30
SCALE = DH ** (-0.5)
LIGHT = pl.CostEstimate(flops=1, bytes_accessed=1, transcendentals=0)


def shifted_pairs(count, by):
    return [(i, i + by) for i in range(count) if 0 <= i + by < count]


def dot(a, b):
    return jnp.dot(a, b, preferred_element_type=jnp.float32)


def nt_dot(a, b):
    return lax.dot_general(a, b, (((1,), (1,)), ((), ())), preferred_element_type=jnp.float32)


PIECE = 384
PIECES = 2 * INNER // PIECE
CUTS = 3


def fetch(pairs, sems):
    copies = [pltpu.make_async_copy(*pair, sems.at[n]) for n, pair in enumerate(pairs)]
    for copy in copies:
        copy.start()
    return copies


def weight_pieces(weight_ref, weight):
    part = PIECE // CUTS
    return [
        (weight_ref.at[pl.ds(INNER + part * p, part)], weight.at[pl.ds(part * p, part)])
        for p in range(PIECES * CUTS)
    ]


def edges_kernel(tokens_ref, weight_ref, top_ref, bottom_ref, tokens, weight, sems):
    edge = top_ref.shape[0]
    ends = [(0, 0), (edge, tokens_ref.shape[0] - edge)]
    token_pairs = [
        (tokens_ref.at[pl.ds(there, edge)], tokens.at[pl.ds(here, edge)]) for here, there in ends
    ]
    copies = fetch(token_pairs + weight_pieces(weight_ref, weight), sems)
    copies[0].wait()
    copies[1].wait()
    for p in range(PIECES):
        for copy in copies[2 + CUTS * p : 2 + CUTS * (p + 1)]:
            copy.wait()
        lanes = slice(PIECE * p, PIECE * (p + 1))
        part = nt_dot(tokens[...], weight[lanes]).astype(jnp.bfloat16)
        top_ref[:, lanes] = part[:edge]
        bottom_ref[:, lanes] = part[edge:]


def project_kernel(
    own_ref, top_ref, tokens_ref, weight_ref, qt_ref, kv_ref, near_ref, tokens, weight, q_weight, sems
):
    pairs = [(tokens_ref, tokens)] + weight_pieces(weight_ref, weight)
    copies = fetch(pairs + [(weight_ref.at[pl.ds(0, INNER)], q_weight)], sems)
    copies[0].wait()
    for p in range(PIECES):
        for copy in copies[1 + CUTS * p : 1 + CUTS * (p + 1)]:
            copy.wait()
        lanes = slice(PIECE * p, PIECE * (p + 1))
        part = nt_dot(tokens[...], weight[lanes])
        kv_ref[:, lanes] = part.astype(jnp.bfloat16)
        grid = part.reshape(near_ref.shape[0] // REACH, -1, PIECE)
        is_right = own_ref[0].astype(jnp.float32)
        near = grid[:, :REACH] * is_right + grid[:, -REACH:] * (1.0 - is_right)
        near_ref[:, lanes] = near.reshape(-1, PIECE).astype(jnp.bfloat16)
    copies[-1].wait()
    qt_ref[...] = nt_dot(q_weight[...], tokens[...]).astype(jnp.bfloat16)


def project(token_rows, weight, tile_cols):
    rows, width = token_rows.shape
    edge = SIDE * tile_cols
    own = lax.axis_index("col").astype(jnp.int32).reshape(1)
    shape = lambda count: jax.ShapeDtypeStruct((count, 2 * INNER), jnp.bfloat16)
    block = lambda count: pl.BlockSpec((count, 2 * INNER), lambda _: (0, 0))
    anywhere = pl.BlockSpec(memory_space=pl.ANY)
    top, bottom = pl.pallas_call(
        edges_kernel,
        grid=(1,),
        out_shape=[shape(edge)] * 2,
        in_specs=[anywhere] * 2,
        out_specs=[block(edge)] * 2,
        scratch_shapes=[
            pltpu.VMEM((2 * edge, width), jnp.bfloat16),
            pltpu.VMEM((2 * INNER, width), jnp.bfloat16),
            pltpu.SemaphoreType.DMA((PIECES * CUTS + 2,)),
        ],
        compiler_params=pltpu.CompilerParams(vmem_limit_bytes=56 * 1024 * 1024),
        cost_estimate=LIGHT,
        name="project_edges",
    )(token_rows, weight.T)
    near = rows // tile_cols * REACH
    queries, keyvals, near = pl.pallas_call(
        project_kernel,
        grid=(1,),
        out_shape=[jax.ShapeDtypeStruct((INNER, rows), jnp.bfloat16), shape(rows), shape(near)],
        in_specs=[pl.BlockSpec(memory_space=pltpu.SMEM)] + [anywhere] * 3,
        out_specs=[pl.BlockSpec((INNER, rows), lambda _: (0, 0)), block(rows), block(near)],
        scratch_shapes=[
            pltpu.VMEM((rows, width), jnp.bfloat16),
            pltpu.VMEM((2 * INNER, width), jnp.bfloat16),
            pltpu.VMEM((INNER, width), jnp.bfloat16),
            pltpu.SemaphoreType.DMA((PIECES * CUTS + 2,)),
        ],
        compiler_params=pltpu.CompilerParams(vmem_limit_bytes=50 * 1024 * 1024),
        cost_estimate=LIGHT,
        name="project",
    )(own, top[:16, :128], token_rows, weight.T)
    return queries, keyvals, top, bottom, near


def attention_kernel(
    start_ref,
    core_ref,
    tokens_ref,
    upstream_ref,
    qt_ref,
    own_ref,
    g_ref,
    above_ref,
    below_ref,
    cols_ref,
    corner_ref,
    bias_ref,
    o_ref,
    dq_ref,
    inner_ref,
    edge_ref,
    side_ref,
    corner_grad_ref,
    sent_ref,
    kept_ref,
    kv,
    kvt,
    acc,
    ot,
    dqt,
    left,
    turned,
    sems,
):
    strips = bias_ref.shape[0]
    chunk = kv.shape[1]
    chunk_own = own_ref.shape[0] // strips
    chunk_side = chunk - chunk_own
    band = 3 * chunk
    token_count = own_ref.shape[0]
    last = strips + 1
    side_order = [strips] + list(range(strips)) + [strips + 1]

    def place(slot, first, part):
        count = part.shape[0]
        kv[slot, first : first + count] = part
        if count < 128:
            filler = jnp.zeros((128 - count, 2 * INNER), part.dtype)
            part = jnp.concatenate([part, filler], axis=0)
        kvt[slot, :, first : first + count] = part.T[:, :count]

    copies = fetch([(tokens_ref, left.at[0]), (upstream_ref, left.at[1])], sems)
    dqt[INNER:, :] = jnp.zeros((64, chunk_own), jnp.float32)
    ot[:64, :] = jnp.zeros((64, chunk_own), jnp.float32)
    for s in range(strips):
        place(s + 1, 0, own_ref[chunk_own * s : chunk_own * (s + 1)])
    for s in range(strips):
        place(s + 1, chunk_own, cols_ref[chunk_side * s : chunk_side * (s + 1)])
    place(0, 0, above_ref[...])
    place(last, 0, below_ref[...])
    for slot, at in ((0, 0), (last, 1)):
        place(slot, chunk_own, corner_ref[chunk_side * at : chunk_side * (at + 1)])
    acc[...] = jnp.zeros_like(acc)

    row = lax.broadcasted_iota(jnp.int32, (2 * DH, chunk_own), 0)
    first_head = row < DH
    mask_a = jnp.where(first_head, 1.0, 0.0).astype(jnp.bfloat16)
    mask_b = jnp.where(first_head, 0.0, 1.0).astype(jnp.bfloat16)
    ones = jnp.ones((16, chunk), jnp.bfloat16)

    def pair_block(part, above):
        block = jnp.concatenate([part * mask_a, part * mask_b], axis=1)
        parts = [block]
        if above:
            parts = [jnp.zeros((above, block.shape[1]), block.dtype)] + parts
        below = SLAB - 2 * DH - above
        if below:
            parts = parts + [jnp.zeros((below, block.shape[1]), block.dtype)]
        return jnp.concatenate(parts, axis=0)

    def pick(both):
        return jnp.where(first_head, both[:, :chunk_own], both[:, chunk_own:])

    def strip(s, carry):
        top = start_ref[s]
        rows = pl.ds(pl.multiple_of(s * chunk_own, chunk_own), chunk_own)
        bias = bias_ref[s]
        bias = jnp.concatenate([bias, bias], axis=1)
        heads = [slice(2 * DH * i, 2 * DH * (i + 1)) for i in range(PAIRS)]
        k_lanes = [slice(128 * i, 128 * i + SLAB) for i in range(PAIRS)]
        v_lanes = [slice(512 + 128 * i, 512 + 128 * i + SLAB) for i in range(PAIRS)]

        def band_of(lanes):
            return kv[pl.ds(top, 3), :, lanes].reshape(band, SLAB)

        def from_keys(lines, weights):
            got = jnp.zeros((2 * DH, SLAB), jnp.float32)
            for j in range(3):
                got += dot(kvt[top + j, lines, :], weights[chunk * j : chunk * (j + 1)])
            return got

        q2 = [pair_block(qt_ref[heads[i], rows], 16 * i) for i in range(PAIRS)]
        g2 = [pair_block(g_ref[heads[i], rows], V_SHIFT + 16 * i) for i in range(PAIRS)]
        prob, inv, row_dot, dscore = [], [], [], []
        for i in range(PAIRS):
            scores = dot(band_of(k_lanes[i]), q2[i]) * SCALE + bias
            top_score = jnp.max(scores, axis=0, keepdims=True)
            prob.append(jnp.exp(scores - top_score).astype(jnp.bfloat16))
        for i in range(PAIRS):
            total = jnp.zeros((16, SLAB), jnp.float32)
            for j in range(3):
                total += dot(ones, prob[i][chunk * j : chunk * (j + 1)])
            inv.append(1.0 / total[:1])
            v_rows = slice(INNER + heads[i].start, INNER + heads[i].stop)
            att = pick(from_keys(v_rows, prob[i]) * inv[i])
            ot[64 + heads[i].start : 64 + heads[i].stop, :] = att
            dots = att * g_ref[heads[i], rows].astype(jnp.float32)
            row_dot.append(
                jnp.concatenate(
                    [
                        jnp.sum(dots[:DH], axis=0, keepdims=True),
                        jnp.sum(dots[DH:], axis=0, keepdims=True),
                    ],
                    axis=1,
                )
            )
        for i in range(PAIRS):
            dprob = dot(band_of(v_lanes[i]), g2[i])
            inv_scale = inv[i] * SCALE
            change = dprob * inv_scale - row_dot[i] * inv_scale
            dscore.append((prob[i].astype(jnp.float32) * change).astype(jnp.bfloat16))
        for i in range(PAIRS):
            dv = nt_dot(prob[i], (g2[i].astype(jnp.float32) * inv[i]).astype(jnp.bfloat16))
            acc[pl.ds(top, 3), :, v_lanes[i]] += dv.reshape(3, chunk, SLAB)
        for i in range(PAIRS):
            dqt[heads[i], :] = pick(from_keys(heads[i], dscore[i]))
            dk = nt_dot(dscore[i], q2[i])
            acc[pl.ds(top, 3), :, k_lanes[i]] += dk.reshape(3, chunk, SLAB)
        o_ref[rows, :] = ot[...].T.astype(jnp.bfloat16)
        dq_ref[rows, :] = dqt[...].T.astype(jnp.bfloat16)
        for side in range(2):
            turned[side, :, rows] = left[side, rows, :].T
        return carry

    for copy in copies:
        copy.wait()
    lax.fori_loop(0, strips, strip, 0, unroll=2)
    share = sent_ref.shape[0] // 4
    for out_ref, half in ((sent_ref, 1 - core_ref[0]), (kept_ref, core_ref[0])):
        products = []
        for side, right in enumerate((dq_ref, o_ref)):
            picked = [
                turned[side, pl.ds(pl.multiple_of((2 * r + half) * share, 16), share), :]
                for r in range(4)
            ]
            products.append(dot(jnp.concatenate(picked, axis=0), right[...]))
        first, second = products
        out_ref[:, :512] = first[:, :512].astype(jnp.bfloat16)
        out_ref[:, 512:640] = (first[:, 512:] + second[:, :128]).astype(jnp.bfloat16)
        out_ref[:, 640:] = second[:, 128:].astype(jnp.bfloat16)
    for slot, at in enumerate(side_order):
        own_grad = acc[slot, :chunk_own].astype(jnp.bfloat16)
        if at < strips:
            inner_ref[chunk_own * at : chunk_own * (at + 1), :] = own_grad
        else:
            edge_ref[chunk_own * (at - strips) : chunk_own * (at - strips + 1), :] = own_grad
        side_grad = acc[slot, chunk_own:].astype(jnp.bfloat16)
        if at < strips:
            side_ref[chunk_side * at : chunk_side * (at + 1), :] = side_grad
        else:
            at -= strips
            corner_grad_ref[chunk_side * at : chunk_side * (at + 1), :] = side_grad


def attention(start, token_rows, grad_rows, queries, own, grads, above, below, cols, corner, bias):
    strips, band, chunk_own = bias.shape
    chunk = band // 3
    token_count, width = own.shape
    whole = lambda a: pl.BlockSpec(
        a.shape, lambda _: (0,) * a.ndim, pipeline_mode=pl.Buffered(1)
    )
    outs = (
        jax.ShapeDtypeStruct((token_count, INNER + 64), jnp.bfloat16),
        jax.ShapeDtypeStruct((token_count, INNER + 64), jnp.bfloat16),
        jax.ShapeDtypeStruct(own.shape, jnp.bfloat16),
        jax.ShapeDtypeStruct((2 * chunk_own, width), jnp.bfloat16),
        jax.ShapeDtypeStruct(cols.shape, jnp.bfloat16),
        jax.ShapeDtypeStruct(corner.shape, jnp.bfloat16),
        jax.ShapeDtypeStruct((token_rows.shape[1] // 2, width), jnp.bfloat16),
        jax.ShapeDtypeStruct((token_rows.shape[1] // 2, width), jnp.bfloat16),
    )
    core = lax.axis_index("col").astype(jnp.int32).reshape(1) % 2
    return pl.pallas_call(
        attention_kernel,
        grid=(1,),
        out_shape=outs,
        in_specs=[
            pl.BlockSpec(memory_space=pltpu.SMEM),
            pl.BlockSpec(memory_space=pltpu.SMEM),
            pl.BlockSpec(memory_space=pl.ANY),
            pl.BlockSpec(memory_space=pl.ANY),
            whole(queries),
            whole(own),
            whole(grads),
            whole(above),
            whole(below),
            whole(cols),
            whole(corner),
            whole(bias),
        ],
        out_specs=tuple(whole(o) for o in outs),
        scratch_shapes=[
            pltpu.VMEM((strips + 2, chunk, width), jnp.bfloat16),
            pltpu.VMEM((strips + 2, width, chunk), jnp.bfloat16),
            pltpu.VMEM((strips + 2, chunk, width), jnp.float32),
            pltpu.VMEM((640, chunk_own), jnp.float32),
            pltpu.VMEM((640, chunk_own), jnp.float32),
            pltpu.VMEM((2,) + token_rows.shape, jnp.bfloat16),
            pltpu.VMEM((2,) + token_rows.shape[::-1], jnp.bfloat16),
            pltpu.SemaphoreType.DMA((2,)),
        ],
        compiler_params=pltpu.CompilerParams(vmem_limit_bytes=30 * 1024 * 1024),
        cost_estimate=pl.CostEstimate(
            flops=12 * token_count * band * 2 * INNER,
            bytes_accessed=16 * 1024 * 1024,
            transcendentals=token_count * band * H,
        ),
        name="window_attention",
    )(start, core, token_rows, grad_rows, queries, own, grads, above, below, cols, corner, bias)


def late_kernel(
    own_ref, first, second, third, tokens_ref, inner_ref, side_ref, above_ref, below_ref,
    dq_ref, o_ref, sent_ref, kept_ref, all_ref, att_ref, turned, grad_ref,
):
    own = own_ref[0]
    count = inner_ref.shape[0]
    share = sent_ref.shape[0] // 4
    edge = above_ref.shape[0]
    width = inner_ref.shape[1]
    side = side_ref[: count // 2].astype(jnp.float32).reshape(-1, REACH, width)
    is_left = (own == 0).astype(jnp.float32)
    side = jnp.concatenate([side * (1.0 - is_left), side * is_left], axis=1)
    total = inner_ref[...].astype(jnp.float32) + side.reshape(count, width)
    grad_ref[:edge] = (total[:edge] + above_ref[...].astype(jnp.float32)).astype(jnp.bfloat16)
    grad_ref[edge : count - edge] = total[edge : count - edge].astype(jnp.bfloat16)
    grad_ref[count - edge :] = (
        total[count - edge :] + below_ref[...].astype(jnp.float32)
    ).astype(jnp.bfloat16)
    turned[...] = tokens_ref[...].T
    for out_ref, half in ((sent_ref, 1 - own), (kept_ref, own)):
        picked = [
            turned[pl.ds(pl.multiple_of((2 * r + half) * share, 16), share), :] for r in range(4)
        ]
        product = dot(jnp.concatenate(picked, axis=0), grad_ref[...])
        out_ref[...] = product.astype(jnp.bfloat16)
    all_ref[...] = jnp.concatenate([dq_ref[:, :INNER], grad_ref[...]], axis=1)
    att_ref[...] = o_ref[:, 64:]


def late_halves(earlier, token_rows, inner, side, above, below, dquery, attended):
    rows, width = token_rows.shape
    whole = lambda a: pl.BlockSpec(a.shape, lambda _: (0,) * a.ndim)
    out = jax.ShapeDtypeStruct((width // 2, 2 * INNER), jnp.bfloat16)
    grads = jax.ShapeDtypeStruct((rows, 3 * INNER), jnp.bfloat16)
    att = jax.ShapeDtypeStruct((rows, INNER), jnp.bfloat16)
    operands = (token_rows, inner, side, above, below, dquery, attended)
    own = lax.axis_index("col").astype(jnp.int32).reshape(1)
    return pl.pallas_call(
        late_kernel,
        grid=(1,),
        out_shape=(out, out, grads, att),
        in_specs=[pl.BlockSpec(memory_space=pltpu.SMEM)]
        + [pl.BlockSpec(memory_space=pl.ANY)] * 3
        + [whole(a) for a in operands],
        out_specs=(whole(out), whole(out), whole(grads), whole(att)),
        scratch_shapes=[
            pltpu.VMEM((width, rows), jnp.bfloat16),
            pltpu.VMEM((rows, 2 * INNER), jnp.bfloat16),
        ],
        compiler_params=pltpu.CompilerParams(vmem_limit_bytes=22 * 1024 * 1024),
        cost_estimate=LIGHT,
        name="late_weight_grad_halves",
    )(own, *earlier, *operands)


def core_parts_kernel(own_ref, kept_ref, got_ref, *refs):
    outs, total = refs[-5:-1], refs[-1]
    rows, padded, _ = total.shape
    share, small = kept_ref.shape[0] // rows, padded // 4
    for r in range(rows):
        part = slice(share * r, share * (r + 1))
        total[r, :share] = kept_ref[part].astype(jnp.float32) + got_ref[part].astype(jnp.float32)
        total[r, share:] = jnp.zeros((padded - share, total.shape[2]), jnp.float32)
    for step, out in enumerate(outs):
        first = pl.multiple_of((own_ref[0] ^ step) * small, 8)
        out[...] = total[:, pl.ds(first, small), :].astype(jnp.bfloat16)


def core_parts(sent, kept, *earlier):
    got = lax.ppermute(sent, "col", [(0, 1), (1, 0)])
    rows, images = lax.axis_size("row"), lax.axis_size("img")
    width = kept.shape[1]
    small = -(-kept.shape[0] // rows // (8 * images)) * 8
    own = lax.axis_index("img").astype(jnp.int32).reshape(1)
    return pl.pallas_call(
        core_parts_kernel,
        grid=(1,),
        out_shape=[jax.ShapeDtypeStruct((rows, small, width), jnp.bfloat16)] * images,
        in_specs=[pl.BlockSpec(memory_space=pltpu.SMEM)]
        + [pl.BlockSpec(kept.shape, lambda _: (0, 0))] * 2
        + [pl.BlockSpec(memory_space=pl.ANY)] * len(earlier),
        out_specs=[pl.BlockSpec((rows, small, width), lambda _: (0, 0, 0))] * images,
        scratch_shapes=[pltpu.VMEM((rows, images * small, width), jnp.float32)],
        compiler_params=pltpu.CompilerParams(vmem_limit_bytes=20 * 1024 * 1024),
        cost_estimate=LIGHT,
        name="core_parts",
    )(own, kept, got, *earlier)


def row_sum_kernel(kept, first, second, third, *refs):
    total = kept[...].astype(jnp.float32) + first[...].astype(jnp.float32)
    total += second[...].astype(jnp.float32)
    refs[-1][...] = (total + third[...].astype(jnp.float32)).astype(jnp.bfloat16)


def row_sum_after(parts, earlier):
    parts = [parts[0]] + exchanged(parts, "row")
    shape = parts[0].shape
    return pl.pallas_call(
        row_sum_kernel,
        grid=(1,),
        out_shape=jax.ShapeDtypeStruct(shape, jnp.bfloat16),
        in_specs=[pl.BlockSpec(shape, lambda _: (0, 0))] * 4 + [pl.BlockSpec(memory_space=pl.ANY)],
        out_specs=pl.BlockSpec(shape, lambda _: (0, 0)),
        compiler_params=pltpu.CompilerParams(vmem_limit_bytes=8 * 1024 * 1024),
        cost_estimate=LIGHT,
        name="row_sum",
    )(*parts, earlier)


def outputs_kernel(own_ref, *refs):
    parts, (qkv_ref, out_ref, early, late) = refs[:8], refs[8:]
    share = qkv_ref.shape[0]
    small = parts[0].shape[0]
    for step in range(4):
        first = pl.multiple_of((own_ref[0] ^ step) * small, 8)
        early[pl.ds(first, small), :] = parts[step][...].astype(jnp.float32)
        late[pl.ds(first, small), :] = parts[4 + step][...].astype(jnp.float32)
    qkv_ref[...] = jnp.concatenate([early[:share, :INNER], late[:share]], axis=1)
    out_ref[...] = early[:share, INNER:]


def written_outputs(early, late, share):
    small, width = early[0].shape
    parts = early + late
    own = lax.axis_index("img").astype(jnp.int32).reshape(1)
    shapes = [(share, 3 * INNER), (share, INNER)]
    return pl.pallas_call(
        outputs_kernel,
        grid=(1,),
        out_shape=[jax.ShapeDtypeStruct(shape, jnp.float32) for shape in shapes],
        in_specs=[pl.BlockSpec(memory_space=pltpu.SMEM)]
        + [pl.BlockSpec((small, width), lambda _: (0, 0))] * len(parts),
        out_specs=[pl.BlockSpec(shape, lambda _: (0, 0)) for shape in shapes],
        scratch_shapes=[pltpu.VMEM((len(early) * small, width), jnp.float32)] * 2,
        compiler_params=pltpu.CompilerParams(vmem_limit_bytes=16 * 1024 * 1024),
        cost_estimate=LIGHT,
        name="weight_grads",
    )(own, *parts)


def window_starts(places, extent):
    return jnp.clip(places - REACH, 0, extent - WINDOW)


def window_bias(tile_rows, tile_cols, two_columns):
    row_id = lax.axis_index("row")
    col_id = lax.axis_index("col")
    frame_rows = tile_rows * lax.axis_size("row")
    frame_cols = tile_cols * lax.axis_size("col")
    strips = tile_rows // SIDE
    col_first = col_id * tile_cols
    strip_id = jnp.arange(strips, dtype=jnp.int32)
    first_chunk = row_id * strips - 1
    band_chunk = jnp.clip(row_id * strips + strip_id - 1, 0, frame_rows // SIDE - 3)
    side = jnp.arange(SIDE, dtype=jnp.int32)
    own_cols = col_first + jnp.arange(tile_cols, dtype=jnp.int32)
    low, high = col_first - REACH + side, col_first + tile_cols + side
    spans = [own_cols, jnp.where(col_id == 0, high, low)] if two_columns else [own_cols, low, high]
    chunk_rows = jnp.concatenate([jnp.repeat(side, span.shape[0]) for span in spans])
    chunk_cols = jnp.concatenate([jnp.tile(span, SIDE) for span in spans])
    in_band = jnp.concatenate([SIDE * j + chunk_rows for j in range(3)])
    key_col = jnp.tile(chunk_cols, 3)
    key_row = SIDE * band_chunk[:, None] + in_band[None, :]
    query_row = row_id * tile_rows + SIDE * strip_id[:, None] + jnp.repeat(side, tile_cols)[None, :]
    row_start = window_starts(query_row, frame_rows)
    col_start = window_starts(jnp.tile(own_cols, SIDE), frame_cols)
    row_off = key_row[:, :, None] - row_start[:, None, :]
    col_off = key_col[:, None] - col_start[None, :]
    row_ok = (row_off >= 0) & (row_off < WINDOW)
    col_ok = (col_off >= 0) & (col_off < WINDOW)
    bias = jnp.where(row_ok & col_ok[None], 0.0, MASKED).astype(jnp.float32)
    return (band_chunk - first_chunk).astype(jnp.int32), bias


def after(value, *earlier):
    return lax.optimization_barrier((value,) + earlier)[0]


def cut(block, axis, take):
    own = lax.axis_index(axis)
    return [take(block, own ^ step) for step in range(lax.axis_size(axis))]


def exchanged(parts, axis):
    got = []
    for step, part in enumerate(parts[1:], 1):
        pairs = [(i, i ^ step) for i in range(lax.axis_size(axis))]
        got.append(lax.ppermute(part, axis, pairs))
    return got


def added(kept, got, *earlier):
    if earlier:
        kept = after(kept, *earlier)
    total = kept.astype(jnp.float32)
    for g in got:
        total += g.astype(jnp.float32)
    return total.astype(jnp.bfloat16)


def row_parts(held):
    return cut(held, "row", lambda h, r: lax.dynamic_index_in_dim(h, r, 0, keepdims=False))


def plain_shares(part):
    held = lax.psum_scatter(part, ("row", "col"), scatter_dimension=0, tiled=True)
    return lax.psum(held, "img").astype(jnp.float32)


def local(tokens, qkv_weight, out_weight, upstream):
    _, tile_rows, tile_cols, width = tokens.shape
    token_count = tile_rows * tile_cols
    strips = tile_rows // SIDE
    chunk_own = SIDE * tile_cols
    row_count, col_count = lax.axis_size("row"), lax.axis_size("col")
    two_columns = col_count == 2
    col_id = lax.axis_index("col")
    token_rows = tokens.reshape(token_count, width)
    grad_rows = upstream.reshape(token_count, width)
    turns = (0,) if two_columns else (-1, 1)

    def moved(block, down, turn=None):
        pairs = []
        for r in range(row_count):
            for c in range(col_count):
                to_c = c if turn is None else (1 - c if turn == 0 else c + turn)
                if 0 <= r + down < row_count and 0 <= to_c < col_count:
                    pairs.append((r * col_count + c, (r + down) * col_count + to_c))
        return lax.ppermute(block, ("row", "col"), pairs)

    def edge(block, turn):
        if turn == 0:
            return lax.dynamic_slice_in_dim(block, (1 - col_id) * (tile_cols - REACH), REACH, 1)
        return block[:, tile_cols - REACH :] if turn == 1 else block[:, :REACH]

    def side_of(*blocks):
        got = []
        for turn in sorted(turns, reverse=True):
            near = [edge(block.reshape(-1, tile_cols, 2 * INNER), turn) for block in blocks]
            near = jnp.concatenate(near, axis=0) if len(near) > 1 else near[0]
            got.append(moved(near, 0, turn).reshape(-1, SIDE * REACH, 2 * INNER))
        got = got[0] if two_columns else jnp.concatenate(got, axis=1)
        return got.reshape(-1, 2 * INNER)

    queries, keyvals, top, bottom, near = project(token_rows, qkv_weight, tile_cols)
    above = moved(bottom, 1)
    below = moved(top, -1)
    if two_columns:
        cols = moved(near, 0, 0)
    else:
        cols = side_of(keyvals)
    corner = side_of(above, below)
    grad_att = lax.dot_general(
        out_weight, grad_rows, (((0,), (1,)), ((), ())), preferred_element_type=jnp.float32
    ).astype(jnp.bfloat16)
    start, bias = window_bias(tile_rows, tile_cols, two_columns)
    attended, dquery, inner_grad, edge_grad, side_grad, corner_grad, sent, kept = attention(
        start, token_rows, grad_rows, queries, keyvals, grad_att, above, below, cols, corner, bias
    )

    def outer(a, b):
        return lax.dot_general(
            a, b, (((0,), (0,)), ((), ())), preferred_element_type=jnp.float32
        ).astype(jnp.bfloat16)

    simple = two_columns and row_count == 4 and lax.axis_size("img") == 4
    if simple:
        early = core_parts(sent, kept)
    def outputs(attended, dqkv):
        sublayer_out = nt_dot(attended, out_weight).astype(jnp.bfloat16)
        return sublayer_out, nt_dot(dqkv, qkv_weight).astype(jnp.bfloat16)

    def spread(side, first):
        side = side.reshape(-1, SIDE, REACH, 2 * INNER).astype(jnp.float32)
        zeros = jnp.zeros((side.shape[0], SIDE, tile_cols - REACH, 2 * INNER), jnp.float32)
        order = [side, zeros] if first else [zeros, side]
        return jnp.concatenate(order, axis=2).reshape(-1, 2 * INNER)

    def sides_back(part):
        if two_columns:
            return moved(part, 0, 0).reshape(-1, SIDE * REACH, 2 * INNER)
        halves = part.reshape(-1, 2, SIDE * REACH, 2 * INNER)
        return jnp.stack([moved(halves[:, 0], 0, -1), moved(halves[:, 1], 0, 1)], axis=1)

    def returned(part):
        if two_columns:
            return jnp.where(col_id == 0, spread(part, False), spread(part, True))
        return spread(part[:, 0], False) + spread(part[:, 1], True)

    side, corner = sides_back(side_grad), sides_back(corner_grad)
    outer_grad = edge_grad.astype(jnp.float32) + returned(corner)
    outer_grad = outer_grad.astype(jnp.bfloat16)
    from_below = moved(outer_grad[:chunk_own], -1)
    from_above = moved(outer_grad[chunk_own:], 1)
    if simple:
        side = side.reshape(-1, 2 * INNER)
        sent, kept, dqkv, attended = late_halves(
            early[1:], token_rows, inner_grad, side, from_above, from_below, dquery, attended
        )
    else:
        dquery, attended = dquery[:, :INNER], attended[:, 64:]
        dkv = inner_grad.astype(jnp.float32) + returned(side)
        rest = jnp.zeros((token_count - chunk_own, 2 * INNER), jnp.float32)
        dkv = dkv + jnp.concatenate([from_above.astype(jnp.float32), rest], axis=0)
        dkv = dkv + jnp.concatenate([rest, from_below.astype(jnp.float32)], axis=0)
        dkv = dkv.astype(jnp.bfloat16)
        dqkv = jnp.concatenate([dquery, dkv], axis=1)
        sublayer_out, tokens_grad = outputs(attended, dqkv)
    if simple:
        early = added(early[0], exchanged(early, "img"))
        sublayer_out, tokens_grad = outputs(attended, dqkv)
        late = core_parts(sent, kept, early, sublayer_out, tokens_grad)
        late_got = exchanged(late, "img")
        late = added(late[0], late_got, early)
        early = row_sum_after(row_parts(early), late_got[0])
        late = row_parts(late)
        late = added(late[0], exchanged(late, "row"), early)
        share = width // (row_count * col_count)
        early = [early] + exchanged([early] * 4, "img")
        late = [late] + exchanged([late] * 4, "img")
        qkv_grad, out_grad = written_outputs(early, late, share)
    else:
        early = jnp.concatenate([outer(token_rows, dquery), outer(grad_rows, attended)], axis=1)
        early, late = plain_shares(early), plain_shares(outer(token_rows, dkv))
        qkv_grad = jnp.concatenate([early[:, :INNER], late], axis=1)
        out_grad = early[:, INNER:]
    return (
        sublayer_out.reshape(tokens.shape),
        tokens_grad.reshape(tokens.shape),
        qkv_grad,
        out_grad,
    )


def solution(mesh):
    return jax.shard_map(
        local,
        mesh=mesh,
        in_specs=(P("img", "row", "col", None), P(), P(), P("img", "row", "col", None)),
        out_specs=(
            P("img", "row", "col", None),
            P("img", "row", "col", None),
            P(("row", "col"), None),
            P(("row", "col"), None),
        ),
        check_vma=False,
    )
```

```python
import functools

import jax
import jax.numpy as jnp
from jax import lax
from jax.experimental import pallas as pl
from jax.experimental.pallas import tpu as pltpu
from jax.sharding import PartitionSpec as P

H = 8
DH = 72
INNER = H * DH
REACH = 8
WINDOW = 17
SIDE = 8
PAIRS = H // 2
SLAB = 256
V_SHIFT = 64
MASKED = -1e30
SCALE = DH ** (-0.5)
LIGHT = pl.CostEstimate(flops=1, bytes_accessed=1, transcendentals=0)


def shifted_pairs(count, by):
    return [(i, i + by) for i in range(count) if 0 <= i + by < count]


def dot(a, b):
    return jnp.dot(a, b, preferred_element_type=jnp.float32)


def nt_dot(a, b):
    return lax.dot_general(a, b, (((1,), (1,)), ((), ())), preferred_element_type=jnp.float32)


PIECE = 384
PIECES = 2 * INNER // PIECE
CUTS = 3


def fetch(pairs, sems):
    copies = [pltpu.make_async_copy(*pair, sems.at[n]) for n, pair in enumerate(pairs)]
    for copy in copies:
        copy.start()
    return copies


def weight_pieces(weight_ref, weight):
    part = PIECE // CUTS
    return [
        (weight_ref.at[pl.ds(INNER + part * p, part)], weight.at[pl.ds(part * p, part)])
        for p in range(PIECES * CUTS)
    ]


def edges_kernel(tokens_ref, weight_ref, top_ref, bottom_ref, tokens, weight, sems):
    edge = top_ref.shape[0]
    ends = [(0, 0), (edge, tokens_ref.shape[0] - edge)]
    token_pairs = [
        (tokens_ref.at[pl.ds(there, edge)], tokens.at[pl.ds(here, edge)]) for here, there in ends
    ]
    copies = fetch(token_pairs + weight_pieces(weight_ref, weight), sems)
    copies[0].wait()
    copies[1].wait()
    for p in range(PIECES):
        for copy in copies[2 + CUTS * p : 2 + CUTS * (p + 1)]:
            copy.wait()
        lanes = slice(PIECE * p, PIECE * (p + 1))
        part = nt_dot(tokens[...], weight[lanes]).astype(jnp.bfloat16)
        top_ref[:, lanes] = part[:edge]
        bottom_ref[:, lanes] = part[edge:]


def project_kernel(
    own_ref, top_ref, tokens_ref, weight_ref, qt_ref, kv_ref, near_ref, tokens, weight, q_weight, sems
):
    pairs = [(tokens_ref, tokens)] + weight_pieces(weight_ref, weight)
    copies = fetch(pairs + [(weight_ref.at[pl.ds(0, INNER)], q_weight)], sems)
    copies[0].wait()
    for p in range(PIECES):
        for copy in copies[1 + CUTS * p : 1 + CUTS * (p + 1)]:
            copy.wait()
        lanes = slice(PIECE * p, PIECE * (p + 1))
        part = nt_dot(tokens[...], weight[lanes])
        kv_ref[:, lanes] = part.astype(jnp.bfloat16)
        grid = part.reshape(near_ref.shape[0] // REACH, -1, PIECE)
        is_right = own_ref[0].astype(jnp.float32)
        near = grid[:, :REACH] * is_right + grid[:, -REACH:] * (1.0 - is_right)
        near_ref[:, lanes] = near.reshape(-1, PIECE).astype(jnp.bfloat16)
    copies[-1].wait()
    qt_ref[...] = nt_dot(q_weight[...], tokens[...]).astype(jnp.bfloat16)


def project(token_rows, weight, tile_cols):
    rows, width = token_rows.shape
    edge = SIDE * tile_cols
    own = lax.axis_index("col").astype(jnp.int32).reshape(1)
    shape = lambda count: jax.ShapeDtypeStruct((count, 2 * INNER), jnp.bfloat16)
    block = lambda count: pl.BlockSpec((count, 2 * INNER), lambda _: (0, 0))
    anywhere = pl.BlockSpec(memory_space=pl.ANY)
    top, bottom = pl.pallas_call(
        edges_kernel,
        grid=(1,),
        out_shape=[shape(edge)] * 2,
        in_specs=[anywhere] * 2,
        out_specs=[block(edge)] * 2,
        scratch_shapes=[
            pltpu.VMEM((2 * edge, width), jnp.bfloat16),
            pltpu.VMEM((2 * INNER, width), jnp.bfloat16),
            pltpu.SemaphoreType.DMA((PIECES * CUTS + 2,)),
        ],
        compiler_params=pltpu.CompilerParams(vmem_limit_bytes=56 * 1024 * 1024),
        cost_estimate=LIGHT,
        name="project_edges",
    )(token_rows, weight.T)
    near = rows // tile_cols * REACH
    queries, keyvals, near = pl.pallas_call(
        project_kernel,
        grid=(1,),
        out_shape=[jax.ShapeDtypeStruct((INNER, rows), jnp.bfloat16), shape(rows), shape(near)],
        in_specs=[pl.BlockSpec(memory_space=pltpu.SMEM)] + [anywhere] * 3,
        out_specs=[pl.BlockSpec((INNER, rows), lambda _: (0, 0)), block(rows), block(near)],
        scratch_shapes=[
            pltpu.VMEM((rows, width), jnp.bfloat16),
            pltpu.VMEM((2 * INNER, width), jnp.bfloat16),
            pltpu.VMEM((INNER, width), jnp.bfloat16),
            pltpu.SemaphoreType.DMA((PIECES * CUTS + 2,)),
        ],
        compiler_params=pltpu.CompilerParams(vmem_limit_bytes=56 * 1024 * 1024),
        cost_estimate=LIGHT,
        name="project",
    )(own, top, token_rows, weight.T)
    return queries, keyvals, top, bottom, near


def attention_kernel(
    counts,
    tile_ref,
    tokens_ref,
    upstream_ref,
    qt_ref,
    own_ref,
    g_ref,
    above_ref,
    below_ref,
    cols_ref,
    corner_ref,
    o_ref,
    dq_ref,
    inner_ref,
    edge_ref,
    side_ref,
    corner_grad_ref,
    sent_ref,
    kept_ref,
    kv,
    kvt,
    acc,
    ot,
    dqt,
    left,
    turned,
    key_row,
    col_bias,
    sems,
):
    strips, row_tiles, col_tiles = counts
    chunk = kv.shape[1]
    chunk_own = own_ref.shape[0] // strips
    chunk_side = chunk - chunk_own
    band = 3 * chunk
    token_count = own_ref.shape[0]
    last = strips + 1
    side_order = [strips] + list(range(strips)) + [strips + 1]

    def place(slot, first, part):
        count = part.shape[0]
        kv[slot, first : first + count] = part
        if count < 128:
            filler = jnp.zeros((128 - count, 2 * INNER), part.dtype)
            part = jnp.concatenate([part, filler], axis=0)
        kvt[slot, :, first : first + count] = part.T[:, :count]

    copies = fetch([(tokens_ref, left.at[0]), (upstream_ref, left.at[1])], sems)
    dqt[INNER:, :] = jnp.zeros((64, chunk_own), jnp.float32)
    ot[:64, :] = jnp.zeros((64, chunk_own), jnp.float32)
    for s in range(strips):
        place(s + 1, 0, own_ref[chunk_own * s : chunk_own * (s + 1)])
    for s in range(strips):
        place(s + 1, chunk_own, cols_ref[chunk_side * s : chunk_side * (s + 1)])
    place(0, 0, above_ref[...])
    place(last, 0, below_ref[...])
    for slot, at in ((0, 0), (last, 1)):
        place(slot, chunk_own, corner_ref[chunk_side * at : chunk_side * (at + 1)])
    acc[...] = jnp.zeros_like(acc)

    row = lax.broadcasted_iota(jnp.int32, (2 * DH, chunk_own), 0)
    first_head = row < DH
    mask_a = jnp.where(first_head, 1.0, 0.0).astype(jnp.bfloat16)
    mask_b = jnp.where(first_head, 0.0, 1.0).astype(jnp.bfloat16)
    ones = jnp.ones((16, chunk), jnp.bfloat16)

    def pair_block(part, above):
        block = jnp.concatenate([part * mask_a, part * mask_b], axis=1)
        parts = [block]
        if above:
            parts = [jnp.zeros((above, block.shape[1]), block.dtype)] + parts
        below = SLAB - 2 * DH - above
        if below:
            parts = parts + [jnp.zeros((below, block.shape[1]), block.dtype)]
        return jnp.concatenate(parts, axis=0)

    def pick(both):
        return jnp.where(first_head, both[:, :chunk_own], both[:, chunk_own:])

    tile_cols = chunk_own // SIDE
    log_cols = tile_cols.bit_length() - 1
    row_id, col_id = tile_ref[0], tile_ref[1]
    col_first = col_id * tile_cols
    left_first, right_first = col_first - REACH, col_first + tile_cols
    if col_tiles == 2:
        left_first = jnp.where(col_id == 0, right_first, left_first)
    key = lax.broadcasted_iota(jnp.int32, (band, chunk_own), 0)
    query = lax.broadcasted_iota(jnp.int32, (band, chunk_own), 1)
    query_row = query >> log_cols
    part = jnp.where(key >= 2 * chunk, 2, jnp.where(key >= chunk, 1, 0))
    within = key - chunk * part
    is_own = within < chunk_own
    beside = within - chunk_own
    is_right = beside >= SIDE * REACH
    beside = jnp.where(is_right, beside - SIDE * REACH, beside)
    side_col = jnp.where(is_right, right_first, left_first) + (beside & (REACH - 1))
    key_col = jnp.where(is_own, col_first + (within & (tile_cols - 1)), side_col)
    key_row[...] = SIDE * part + jnp.where(is_own, within >> log_cols, beside >> 3)
    query_col = col_first + (query & (tile_cols - 1))
    col_off = key_col - jnp.clip(query_col - REACH, 0, tile_cols * col_tiles - WINDOW)
    col_bias[...] = jnp.where((col_off >= 0) & (col_off < WINDOW), 0.0, MASKED)

    def strip(s, carry):
        here = row_id * strips + s
        first = jnp.clip(here - 1, 0, strips * row_tiles - 3)
        top = first - (row_id * strips - 1)
        rows = pl.ds(pl.multiple_of(s * chunk_own, chunk_own), chunk_own)
        row_start = jnp.clip(
            SIDE * here + query_row - REACH, 0, SIDE * strips * row_tiles - WINDOW
        )
        row_off = key_row[...] + SIDE * first - row_start
        bias = jnp.where((row_off >= 0) & (row_off < WINDOW), col_bias[...], MASKED)
        bias = jnp.concatenate([bias, bias], axis=1)
        heads = [slice(2 * DH * i, 2 * DH * (i + 1)) for i in range(PAIRS)]
        k_lanes = [slice(128 * i, 128 * i + SLAB) for i in range(PAIRS)]
        v_lanes = [slice(512 + 128 * i, 512 + 128 * i + SLAB) for i in range(PAIRS)]

        def band_of(lanes):
            return kv[pl.ds(top, 3), :, lanes].reshape(band, SLAB)

        def from_keys(lines, weights):
            got = jnp.zeros((2 * DH, SLAB), jnp.float32)
            for j in range(3):
                got += dot(kvt[top + j, lines, :], weights[chunk * j : chunk * (j + 1)])
            return got

        q2 = [pair_block(qt_ref[heads[i], rows], 16 * i) for i in range(PAIRS)]
        g2 = [pair_block(g_ref[heads[i], rows], V_SHIFT + 16 * i) for i in range(PAIRS)]
        prob, inv, row_dot, dscore = [], [], [], []
        for i in range(PAIRS):
            scores = dot(band_of(k_lanes[i]), q2[i]) * SCALE + bias
            top_score = jnp.max(scores, axis=0, keepdims=True)
            prob.append(jnp.exp(scores - top_score).astype(jnp.bfloat16))
        for i in range(PAIRS):
            total = jnp.zeros((16, SLAB), jnp.float32)
            for j in range(3):
                total += dot(ones, prob[i][chunk * j : chunk * (j + 1)])
            inv.append(1.0 / total[:1])
            v_rows = slice(INNER + heads[i].start, INNER + heads[i].stop)
            att = pick(from_keys(v_rows, prob[i]) * inv[i])
            ot[64 + heads[i].start : 64 + heads[i].stop, :] = att
            dots = att * g_ref[heads[i], rows].astype(jnp.float32)
            row_dot.append(
                jnp.concatenate(
                    [
                        jnp.sum(dots[:DH], axis=0, keepdims=True),
                        jnp.sum(dots[DH:], axis=0, keepdims=True),
                    ],
                    axis=1,
                )
            )
        for i in range(PAIRS):
            dprob = dot(band_of(v_lanes[i]), g2[i])
            inv_scale = inv[i] * SCALE
            change = dprob * inv_scale - row_dot[i] * inv_scale
            dscore.append((prob[i].astype(jnp.float32) * change).astype(jnp.bfloat16))
        for i in range(PAIRS):
            dv = nt_dot(prob[i], (g2[i].astype(jnp.float32) * inv[i]).astype(jnp.bfloat16))
            acc[pl.ds(top, 3), :, v_lanes[i]] += dv.reshape(3, chunk, SLAB)
        for i in range(PAIRS):
            dqt[heads[i], :] = pick(from_keys(heads[i], dscore[i]))
            dk = nt_dot(dscore[i], q2[i])
            acc[pl.ds(top, 3), :, k_lanes[i]] += dk.reshape(3, chunk, SLAB)
        o_ref[rows, :] = ot[...].T.astype(jnp.bfloat16)
        dq_ref[rows, :] = dqt[...].T.astype(jnp.bfloat16)
        for side in range(2):
            turned[side, :, rows] = left[side, rows, :].T
        return carry

    for copy in copies:
        copy.wait()
    lax.fori_loop(0, strips, strip, 0)
    share = sent_ref.shape[0] // 4
    for out_ref, half in ((sent_ref, 1 - tile_ref[1] % 2), (kept_ref, tile_ref[1] % 2)):
        products = []
        for side, right in enumerate((dq_ref, o_ref)):
            picked = [
                turned[side, pl.ds(pl.multiple_of((2 * r + half) * share, 16), share), :]
                for r in range(4)
            ]
            products.append(dot(jnp.concatenate(picked, axis=0), right[...]))
        first, second = products
        out_ref[:, :512] = first[:, :512].astype(jnp.bfloat16)
        out_ref[:, 512:640] = (first[:, 512:] + second[:, :128]).astype(jnp.bfloat16)
        out_ref[:, 640:] = second[:, 128:].astype(jnp.bfloat16)
    for slot, at in enumerate(side_order):
        own_grad = acc[slot, :chunk_own].astype(jnp.bfloat16)
        if at < strips:
            inner_ref[chunk_own * at : chunk_own * (at + 1), :] = own_grad
        else:
            edge_ref[chunk_own * (at - strips) : chunk_own * (at - strips + 1), :] = own_grad
        side_grad = acc[slot, chunk_own:].astype(jnp.bfloat16)
        if at < strips:
            side_ref[chunk_side * at : chunk_side * (at + 1), :] = side_grad
        else:
            at -= strips
            corner_grad_ref[chunk_side * at : chunk_side * (at + 1), :] = side_grad


def attention(token_rows, grad_rows, queries, own, grads, above, below, cols, corner):
    chunk_own = above.shape[0]
    strips = own.shape[0] // chunk_own
    chunk = chunk_own + cols.shape[0] // strips
    band = 3 * chunk
    counts = (strips, lax.axis_size("row"), lax.axis_size("col"))
    tile = jnp.stack([lax.axis_index("row"), lax.axis_index("col")]).astype(jnp.int32)
    token_count, width = own.shape
    whole = lambda a: pl.BlockSpec(
        a.shape, lambda _: (0,) * a.ndim, pipeline_mode=pl.Buffered(1)
    )
    outs = (
        jax.ShapeDtypeStruct((token_count, INNER + 64), jnp.bfloat16),
        jax.ShapeDtypeStruct((token_count, INNER + 64), jnp.bfloat16),
        jax.ShapeDtypeStruct(own.shape, jnp.bfloat16),
        jax.ShapeDtypeStruct((2 * chunk_own, width), jnp.bfloat16),
        jax.ShapeDtypeStruct(cols.shape, jnp.bfloat16),
        jax.ShapeDtypeStruct(corner.shape, jnp.bfloat16),
        jax.ShapeDtypeStruct((token_rows.shape[1] // 2, width), jnp.bfloat16),
        jax.ShapeDtypeStruct((token_rows.shape[1] // 2, width), jnp.bfloat16),
    )
    return pl.pallas_call(
        functools.partial(attention_kernel, counts),
        grid=(1,),
        out_shape=outs,
        in_specs=[
            pl.BlockSpec(memory_space=pltpu.SMEM),
            pl.BlockSpec(memory_space=pl.ANY),
            pl.BlockSpec(memory_space=pl.ANY),
            whole(queries),
            whole(own),
            whole(grads),
            whole(above),
            whole(below),
            whole(cols),
            whole(corner),
        ],
        out_specs=tuple(whole(o) for o in outs),
        scratch_shapes=[
            pltpu.VMEM((strips + 2, chunk, width), jnp.bfloat16),
            pltpu.VMEM((strips + 2, width, chunk), jnp.bfloat16),
            pltpu.VMEM((strips + 2, chunk, width), jnp.float32),
            pltpu.VMEM((640, chunk_own), jnp.float32),
            pltpu.VMEM((640, chunk_own), jnp.float32),
            pltpu.VMEM((2,) + token_rows.shape, jnp.bfloat16),
            pltpu.VMEM((2,) + token_rows.shape[::-1], jnp.bfloat16),
            pltpu.VMEM((band, chunk_own), jnp.int32),
            pltpu.VMEM((band, chunk_own), jnp.float32),
            pltpu.SemaphoreType.DMA((2,)),
        ],
        compiler_params=pltpu.CompilerParams(vmem_limit_bytes=34 * 1024 * 1024),
        cost_estimate=pl.CostEstimate(
            flops=12 * token_count * band * 2 * INNER,
            bytes_accessed=16 * 1024 * 1024,
            transcendentals=token_count * band * H,
        ),
        name="window_attention",
    )(tile, token_rows, grad_rows, queries, own, grads, above, below, cols, corner)


def late_kernel(
    own_ref, first, second, third, tokens_ref, inner_ref, side_ref, above_ref, below_ref,
    dq_ref, o_ref, sent_ref, kept_ref, all_ref, att_ref, turned, grad_ref,
):
    own = own_ref[0]
    count = inner_ref.shape[0]
    share = sent_ref.shape[0] // 4
    edge = above_ref.shape[0]
    width = inner_ref.shape[1]
    side = side_ref[: count // 2].astype(jnp.float32).reshape(-1, REACH, width)
    is_left = (own == 0).astype(jnp.float32)
    side = jnp.concatenate([side * (1.0 - is_left), side * is_left], axis=1)
    total = inner_ref[...].astype(jnp.float32) + side.reshape(count, width)
    grad_ref[:edge] = (total[:edge] + above_ref[...].astype(jnp.float32)).astype(jnp.bfloat16)
    grad_ref[edge : count - edge] = total[edge : count - edge].astype(jnp.bfloat16)
    grad_ref[count - edge :] = (
        total[count - edge :] + below_ref[...].astype(jnp.float32)
    ).astype(jnp.bfloat16)
    turned[...] = tokens_ref[...].T
    for out_ref, half in ((sent_ref, 1 - own), (kept_ref, own)):
        picked = [
            turned[pl.ds(pl.multiple_of((2 * r + half) * share, 16), share), :] for r in range(4)
        ]
        product = dot(jnp.concatenate(picked, axis=0), grad_ref[...])
        out_ref[...] = product.astype(jnp.bfloat16)
    all_ref[...] = jnp.concatenate([dq_ref[:, :INNER], grad_ref[...]], axis=1)
    att_ref[...] = o_ref[:, 64:]


def late_halves(earlier, token_rows, inner, side, above, below, dquery, attended):
    rows, width = token_rows.shape
    whole = lambda a: pl.BlockSpec(a.shape, lambda _: (0,) * a.ndim)
    out = jax.ShapeDtypeStruct((width // 2, 2 * INNER), jnp.bfloat16)
    grads = jax.ShapeDtypeStruct((rows, 3 * INNER), jnp.bfloat16)
    att = jax.ShapeDtypeStruct((rows, INNER), jnp.bfloat16)
    operands = (token_rows, inner, side, above, below, dquery, attended)
    own = lax.axis_index("col").astype(jnp.int32).reshape(1)
    return pl.pallas_call(
        late_kernel,
        grid=(1,),
        out_shape=(out, out, grads, att),
        in_specs=[pl.BlockSpec(memory_space=pltpu.SMEM)]
        + [pl.BlockSpec(memory_space=pl.ANY)] * 3
        + [whole(a) for a in operands],
        out_specs=(whole(out), whole(out), whole(grads), whole(att)),
        scratch_shapes=[
            pltpu.VMEM((width, rows), jnp.bfloat16),
            pltpu.VMEM((rows, 2 * INNER), jnp.bfloat16),
        ],
        compiler_params=pltpu.CompilerParams(vmem_limit_bytes=22 * 1024 * 1024),
        cost_estimate=LIGHT,
        name="late_weight_grad_halves",
    )(own, *earlier, *operands)


def core_parts_kernel(own_ref, kept_ref, got_ref, *refs):
    outs, total = refs[-5:-1], refs[-1]
    rows, padded, _ = total.shape
    share, small = kept_ref.shape[0] // rows, padded // 4
    for r in range(rows):
        part = slice(share * r, share * (r + 1))
        total[r, :share] = kept_ref[part].astype(jnp.float32) + got_ref[part].astype(jnp.float32)
        total[r, share:] = jnp.zeros((padded - share, total.shape[2]), jnp.float32)
    for step, out in enumerate(outs):
        first = pl.multiple_of((own_ref[0] ^ step) * small, 8)
        out[...] = total[:, pl.ds(first, small), :].astype(jnp.bfloat16)


def core_parts(sent, kept, *earlier):
    got = lax.ppermute(sent, "col", [(0, 1), (1, 0)])
    rows, images = lax.axis_size("row"), lax.axis_size("img")
    width = kept.shape[1]
    small = -(-kept.shape[0] // rows // (8 * images)) * 8
    own = lax.axis_index("img").astype(jnp.int32).reshape(1)
    return pl.pallas_call(
        core_parts_kernel,
        grid=(1,),
        out_shape=[jax.ShapeDtypeStruct((rows, small, width), jnp.bfloat16)] * images,
        in_specs=[pl.BlockSpec(memory_space=pltpu.SMEM)]
        + [pl.BlockSpec(kept.shape, lambda _: (0, 0))] * 2
        + [pl.BlockSpec(memory_space=pl.ANY)] * len(earlier),
        out_specs=[pl.BlockSpec((rows, small, width), lambda _: (0, 0, 0))] * images,
        scratch_shapes=[pltpu.VMEM((rows, images * small, width), jnp.float32)],
        compiler_params=pltpu.CompilerParams(vmem_limit_bytes=20 * 1024 * 1024),
        cost_estimate=LIGHT,
        name="core_parts",
    )(own, kept, got, *earlier)


def row_sum_kernel(kept, first, second, third, *refs):
    total = kept[...].astype(jnp.float32) + first[...].astype(jnp.float32)
    total += second[...].astype(jnp.float32)
    refs[-1][...] = (total + third[...].astype(jnp.float32)).astype(jnp.bfloat16)


def row_sum_after(parts, earlier):
    parts = [parts[0]] + exchanged(parts, "row")
    shape = parts[0].shape
    return pl.pallas_call(
        row_sum_kernel,
        grid=(1,),
        out_shape=jax.ShapeDtypeStruct(shape, jnp.bfloat16),
        in_specs=[pl.BlockSpec(shape, lambda _: (0, 0))] * 4 + [pl.BlockSpec(memory_space=pl.ANY)],
        out_specs=pl.BlockSpec(shape, lambda _: (0, 0)),
        compiler_params=pltpu.CompilerParams(vmem_limit_bytes=8 * 1024 * 1024),
        cost_estimate=LIGHT,
        name="row_sum",
    )(*parts, earlier)


def outputs_kernel(own_ref, *refs):
    parts, (qkv_ref, out_ref, early, late) = refs[:8], refs[8:]
    share = qkv_ref.shape[0]
    small = parts[0].shape[0]
    for step in range(4):
        first = pl.multiple_of((own_ref[0] ^ step) * small, 8)
        early[pl.ds(first, small), :] = parts[step][...].astype(jnp.float32)
        late[pl.ds(first, small), :] = parts[4 + step][...].astype(jnp.float32)
    qkv_ref[...] = jnp.concatenate([early[:share, :INNER], late[:share]], axis=1)
    out_ref[...] = early[:share, INNER:]


def written_outputs(early, late, share):
    small, width = early[0].shape
    parts = early + late
    own = lax.axis_index("img").astype(jnp.int32).reshape(1)
    shapes = [(share, 3 * INNER), (share, INNER)]
    return pl.pallas_call(
        outputs_kernel,
        grid=(1,),
        out_shape=[jax.ShapeDtypeStruct(shape, jnp.float32) for shape in shapes],
        in_specs=[pl.BlockSpec(memory_space=pltpu.SMEM)]
        + [pl.BlockSpec((small, width), lambda _: (0, 0))] * len(parts),
        out_specs=[pl.BlockSpec(shape, lambda _: (0, 0)) for shape in shapes],
        scratch_shapes=[pltpu.VMEM((len(early) * small, width), jnp.float32)] * 2,
        compiler_params=pltpu.CompilerParams(vmem_limit_bytes=16 * 1024 * 1024),
        cost_estimate=LIGHT,
        name="weight_grads",
    )(own, *parts)


def after(value, *earlier):
    return lax.optimization_barrier((value,) + earlier)[0]


def cut(block, axis, take):
    own = lax.axis_index(axis)
    return [take(block, own ^ step) for step in range(lax.axis_size(axis))]


def exchanged(parts, axis):
    got = []
    for step, part in enumerate(parts[1:], 1):
        pairs = [(i, i ^ step) for i in range(lax.axis_size(axis))]
        got.append(lax.ppermute(part, axis, pairs))
    return got


def added(kept, got, *earlier):
    if earlier:
        kept = after(kept, *earlier)
    total = kept.astype(jnp.float32)
    for g in got:
        total += g.astype(jnp.float32)
    return total.astype(jnp.bfloat16)


def row_parts(held):
    return cut(held, "row", lambda h, r: lax.dynamic_index_in_dim(h, r, 0, keepdims=False))


def plain_shares(part):
    held = lax.psum_scatter(part, ("row", "col"), scatter_dimension=0, tiled=True)
    return lax.psum(held, "img").astype(jnp.float32)


def local(tokens, qkv_weight, out_weight, upstream):
    _, tile_rows, tile_cols, width = tokens.shape
    token_count = tile_rows * tile_cols
    strips = tile_rows // SIDE
    chunk_own = SIDE * tile_cols
    row_count, col_count = lax.axis_size("row"), lax.axis_size("col")
    two_columns = col_count == 2
    col_id = lax.axis_index("col")
    token_rows = tokens.reshape(token_count, width)
    grad_rows = upstream.reshape(token_count, width)
    turns = (0,) if two_columns else (-1, 1)

    def moved(block, down, turn=None):
        pairs = []
        for r in range(row_count):
            for c in range(col_count):
                to_c = c if turn is None else (1 - c if turn == 0 else c + turn)
                if 0 <= r + down < row_count and 0 <= to_c < col_count:
                    pairs.append((r * col_count + c, (r + down) * col_count + to_c))
        return lax.ppermute(block, ("row", "col"), pairs)

    def edge(block, turn):
        if turn == 0:
            return lax.dynamic_slice_in_dim(block, (1 - col_id) * (tile_cols - REACH), REACH, 1)
        return block[:, tile_cols - REACH :] if turn == 1 else block[:, :REACH]

    def side_of(*blocks):
        got = []
        for turn in sorted(turns, reverse=True):
            near = [edge(block.reshape(-1, tile_cols, 2 * INNER), turn) for block in blocks]
            near = jnp.concatenate(near, axis=0) if len(near) > 1 else near[0]
            got.append(moved(near, 0, turn).reshape(-1, SIDE * REACH, 2 * INNER))
        got = got[0] if two_columns else jnp.concatenate(got, axis=1)
        return got.reshape(-1, 2 * INNER)

    queries, keyvals, top, bottom, near = project(token_rows, qkv_weight, tile_cols)
    above = moved(bottom, 1)
    below = moved(top, -1)
    if two_columns:
        cols = moved(near, 0, 0)
    else:
        cols = side_of(keyvals)
    corner = side_of(above, below)
    grad_att = lax.dot_general(
        out_weight, grad_rows, (((0,), (1,)), ((), ())), preferred_element_type=jnp.float32
    ).astype(jnp.bfloat16)
    attended, dquery, inner_grad, edge_grad, side_grad, corner_grad, sent, kept = attention(
        token_rows, grad_rows, queries, keyvals, grad_att, above, below, cols, corner
    )

    def outer(a, b):
        return lax.dot_general(
            a, b, (((0,), (0,)), ((), ())), preferred_element_type=jnp.float32
        ).astype(jnp.bfloat16)

    simple = two_columns and row_count == 4 and lax.axis_size("img") == 4
    if simple:
        early = core_parts(sent, kept)
    def outputs(attended, dqkv):
        sublayer_out = nt_dot(attended, out_weight).astype(jnp.bfloat16)
        return sublayer_out, nt_dot(dqkv, qkv_weight).astype(jnp.bfloat16)

    def spread(side, first):
        side = side.reshape(-1, SIDE, REACH, 2 * INNER).astype(jnp.float32)
        zeros = jnp.zeros((side.shape[0], SIDE, tile_cols - REACH, 2 * INNER), jnp.float32)
        order = [side, zeros] if first else [zeros, side]
        return jnp.concatenate(order, axis=2).reshape(-1, 2 * INNER)

    def sides_back(part):
        if two_columns:
            return moved(part, 0, 0).reshape(-1, SIDE * REACH, 2 * INNER)
        halves = part.reshape(-1, 2, SIDE * REACH, 2 * INNER)
        return jnp.stack([moved(halves[:, 0], 0, -1), moved(halves[:, 1], 0, 1)], axis=1)

    def returned(part):
        if two_columns:
            return jnp.where(col_id == 0, spread(part, False), spread(part, True))
        return spread(part[:, 0], False) + spread(part[:, 1], True)

    side, corner = sides_back(side_grad), sides_back(corner_grad)
    outer_grad = edge_grad.astype(jnp.float32) + returned(corner)
    outer_grad = outer_grad.astype(jnp.bfloat16)
    from_below = moved(outer_grad[:chunk_own], -1)
    from_above = moved(outer_grad[chunk_own:], 1)
    if simple:
        side = side.reshape(-1, 2 * INNER)
        sent, kept, dqkv, attended = late_halves(
            early[1:], token_rows, inner_grad, side, from_above, from_below, dquery, attended
        )
    else:
        dquery, attended = dquery[:, :INNER], attended[:, 64:]
        dkv = inner_grad.astype(jnp.float32) + returned(side)
        rest = jnp.zeros((token_count - chunk_own, 2 * INNER), jnp.float32)
        dkv = dkv + jnp.concatenate([from_above.astype(jnp.float32), rest], axis=0)
        dkv = dkv + jnp.concatenate([rest, from_below.astype(jnp.float32)], axis=0)
        dkv = dkv.astype(jnp.bfloat16)
        dqkv = jnp.concatenate([dquery, dkv], axis=1)
        sublayer_out, tokens_grad = outputs(attended, dqkv)
    if simple:
        early = added(early[0], exchanged(early, "img"))
        sublayer_out, tokens_grad = outputs(attended, dqkv)
        late = core_parts(sent, kept, early, sublayer_out, tokens_grad)
        late_got = exchanged(late, "img")
        late = added(late[0], late_got, early)
        early = row_sum_after(row_parts(early), late_got[0])
        late = row_parts(late)
        late = added(late[0], exchanged(late, "row"), early)
        share = width // (row_count * col_count)
        early = [early] + exchanged([early] * 4, "img")
        late = [late] + exchanged([late] * 4, "img")
        qkv_grad, out_grad = written_outputs(early, late, share)
    else:
        early = jnp.concatenate([outer(token_rows, dquery), outer(grad_rows, attended)], axis=1)
        early, late = plain_shares(early), plain_shares(outer(token_rows, dkv))
        qkv_grad = jnp.concatenate([early[:, :INNER], late], axis=1)
        out_grad = early[:, INNER:]
    return (
        sublayer_out.reshape(tokens.shape),
        tokens_grad.reshape(tokens.shape),
        qkv_grad,
        out_grad,
    )


def solution(mesh):
    return jax.shard_map(
        local,
        mesh=mesh,
        in_specs=(P("img", "row", "col", None), P(), P(), P("img", "row", "col", None)),
        out_specs=(
            P("img", "row", "col", None),
            P("img", "row", "col", None),
            P(("row", "col"), None),
            P(("row", "col"), None),
        ),
        check_vma=False,
    )
```

```python
import functools

import jax
import jax.numpy as jnp
from jax import lax
from jax.experimental import pallas as pl
from jax.experimental.pallas import tpu as pltpu
from jax.sharding import PartitionSpec as P

H = 8
DH = 72
INNER = H * DH
REACH = 8
WINDOW = 17
SIDE = 8
PAIRS = H // 2
SLAB = 256
V_SHIFT = 64
MASKED = -1e30
SCALE = DH ** (-0.5)
LIGHT = pl.CostEstimate(flops=1, bytes_accessed=1, transcendentals=0)


def shifted_pairs(count, by):
    return [(i, i + by) for i in range(count) if 0 <= i + by < count]


def dot(a, b):
    return jnp.dot(a, b, preferred_element_type=jnp.float32)


def nt_dot(a, b):
    return lax.dot_general(a, b, (((1,), (1,)), ((), ())), preferred_element_type=jnp.float32)


PIECE = 384
PIECES = 2 * INNER // PIECE
CUTS = 3


def fetch(pairs, sems):
    copies = [pltpu.make_async_copy(*pair, sems.at[n]) for n, pair in enumerate(pairs)]
    for copy in copies:
        copy.start()
    return copies


def weight_pieces(weight_ref, weight):
    part = PIECE // CUTS
    return [
        (weight_ref.at[pl.ds(INNER + part * p, part)], weight.at[pl.ds(part * p, part)])
        for p in range(PIECES * CUTS)
    ]


def edges_kernel(tokens_ref, weight_ref, top_ref, bottom_ref, tokens, weight, sems):
    edge = top_ref.shape[0]
    ends = [(0, 0), (edge, tokens_ref.shape[0] - edge)]
    token_pairs = [
        (tokens_ref.at[pl.ds(there, edge)], tokens.at[pl.ds(here, edge)]) for here, there in ends
    ]
    copies = fetch(token_pairs + weight_pieces(weight_ref, weight), sems)
    copies[0].wait()
    copies[1].wait()
    for p in range(PIECES):
        for copy in copies[2 + CUTS * p : 2 + CUTS * (p + 1)]:
            copy.wait()
        lanes = slice(PIECE * p, PIECE * (p + 1))
        part = nt_dot(tokens[...], weight[lanes]).astype(jnp.bfloat16)
        top_ref[:, lanes] = part[:edge]
        bottom_ref[:, lanes] = part[edge:]


def project_kernel(
    own_ref, top_ref, tokens_ref, weight_ref, qt_ref, kv_ref, near_ref, tokens, weight, q_weight, sems
):
    pairs = [(tokens_ref, tokens)] + weight_pieces(weight_ref, weight)
    copies = fetch(pairs + [(weight_ref.at[pl.ds(0, INNER)], q_weight)], sems)
    copies[0].wait()
    for p in range(PIECES):
        for copy in copies[1 + CUTS * p : 1 + CUTS * (p + 1)]:
            copy.wait()
        lanes = slice(PIECE * p, PIECE * (p + 1))
        part = nt_dot(tokens[...], weight[lanes])
        kv_ref[:, lanes] = part.astype(jnp.bfloat16)
        grid = part.reshape(near_ref.shape[0] // REACH, -1, PIECE)
        is_right = own_ref[0].astype(jnp.float32)
        near = grid[:, :REACH] * is_right + grid[:, -REACH:] * (1.0 - is_right)
        near_ref[:, lanes] = near.reshape(-1, PIECE).astype(jnp.bfloat16)
    copies[-1].wait()
    qt_ref[...] = nt_dot(q_weight[...], tokens[...]).astype(jnp.bfloat16)


def project(token_rows, weight, tile_cols):
    rows, width = token_rows.shape
    edge = SIDE * tile_cols
    own = lax.axis_index("col").astype(jnp.int32).reshape(1)
    shape = lambda count: jax.ShapeDtypeStruct((count, 2 * INNER), jnp.bfloat16)
    block = lambda count: pl.BlockSpec((count, 2 * INNER), lambda _: (0, 0))
    anywhere = pl.BlockSpec(memory_space=pl.ANY)
    top, bottom = pl.pallas_call(
        edges_kernel,
        grid=(1,),
        out_shape=[shape(edge)] * 2,
        in_specs=[anywhere] * 2,
        out_specs=[block(edge)] * 2,
        scratch_shapes=[
            pltpu.VMEM((2 * edge, width), jnp.bfloat16),
            pltpu.VMEM((2 * INNER, width), jnp.bfloat16),
            pltpu.SemaphoreType.DMA((PIECES * CUTS + 2,)),
        ],
        compiler_params=pltpu.CompilerParams(vmem_limit_bytes=56 * 1024 * 1024),
        cost_estimate=LIGHT,
        name="project_edges",
    )(token_rows, weight.T)
    near = rows // tile_cols * REACH
    queries, keyvals, near = pl.pallas_call(
        project_kernel,
        grid=(1,),
        out_shape=[jax.ShapeDtypeStruct((INNER, rows), jnp.bfloat16), shape(rows), shape(near)],
        in_specs=[pl.BlockSpec(memory_space=pltpu.SMEM)] + [anywhere] * 3,
        out_specs=[pl.BlockSpec((INNER, rows), lambda _: (0, 0)), block(rows), block(near)],
        scratch_shapes=[
            pltpu.VMEM((rows, width), jnp.bfloat16),
            pltpu.VMEM((2 * INNER, width), jnp.bfloat16),
            pltpu.VMEM((INNER, width), jnp.bfloat16),
            pltpu.SemaphoreType.DMA((PIECES * CUTS + 2,)),
        ],
        compiler_params=pltpu.CompilerParams(vmem_limit_bytes=56 * 1024 * 1024),
        cost_estimate=LIGHT,
        name="project",
    )(own, top, token_rows, weight.T)
    return queries, keyvals, top, bottom, near


def attention_kernel(
    counts,
    tile_ref,
    tokens_ref,
    upstream_ref,
    qt_ref,
    own_ref,
    g_ref,
    above_ref,
    below_ref,
    cols_ref,
    corner_ref,
    o_ref,
    dq_ref,
    inner_ref,
    edge_ref,
    side_ref,
    corner_grad_ref,
    sent_ref,
    kept_ref,
    kv,
    kvt,
    acc,
    ot,
    dqt,
    left,
    turned,
    key_row,
    col_bias,
    sems,
):
    strips, row_tiles, col_tiles = counts
    chunk = kv.shape[1]
    chunk_own = own_ref.shape[0] // strips
    chunk_side = chunk - chunk_own
    band = 3 * chunk
    token_count = own_ref.shape[0]
    last = strips + 1
    side_order = [strips] + list(range(strips)) + [strips + 1]

    def place(slot, first, part):
        count = part.shape[0]
        kv[slot, first : first + count] = part
        if count < 128:
            filler = jnp.zeros((128 - count, 2 * INNER), part.dtype)
            part = jnp.concatenate([part, filler], axis=0)
        kvt[slot, :, first : first + count] = part.T[:, :count]

    copies = fetch([(tokens_ref, left.at[0]), (upstream_ref, left.at[1])], sems)
    dqt[INNER:, :] = jnp.zeros((64, chunk_own), jnp.float32)
    ot[:64, :] = jnp.zeros((64, chunk_own), jnp.float32)
    for s in range(strips):
        place(s + 1, 0, own_ref[chunk_own * s : chunk_own * (s + 1)])
    for s in range(strips):
        place(s + 1, chunk_own, cols_ref[chunk_side * s : chunk_side * (s + 1)])
    place(0, 0, above_ref[...])
    place(last, 0, below_ref[...])
    for slot, at in ((0, 0), (last, 1)):
        place(slot, chunk_own, corner_ref[chunk_side * at : chunk_side * (at + 1)])
    acc[...] = jnp.zeros_like(acc)

    row = lax.broadcasted_iota(jnp.int32, (2 * DH, chunk_own), 0)
    first_head = row < DH
    mask_a = jnp.where(first_head, 1.0, 0.0).astype(jnp.bfloat16)
    mask_b = jnp.where(first_head, 0.0, 1.0).astype(jnp.bfloat16)
    ones = jnp.ones((16, chunk), jnp.bfloat16)

    def pair_block(part, above):
        block = jnp.concatenate([part * mask_a, part * mask_b], axis=1)
        parts = [block]
        if above:
            parts = [jnp.zeros((above, block.shape[1]), block.dtype)] + parts
        below = SLAB - 2 * DH - above
        if below:
            parts = parts + [jnp.zeros((below, block.shape[1]), block.dtype)]
        return jnp.concatenate(parts, axis=0)

    def pick(both):
        return jnp.where(first_head, both[:, :chunk_own], both[:, chunk_own:])

    tile_cols = chunk_own // SIDE
    log_cols = tile_cols.bit_length() - 1
    row_id, col_id = tile_ref[0], tile_ref[1]
    col_first = col_id * tile_cols
    left_first, right_first = col_first - REACH, col_first + tile_cols
    if col_tiles == 2:
        left_first = jnp.where(col_id == 0, right_first, left_first)
    key = lax.broadcasted_iota(jnp.int32, (band, chunk_own), 0)
    query = lax.broadcasted_iota(jnp.int32, (band, chunk_own), 1)
    query_row = query >> log_cols
    part = jnp.where(key >= 2 * chunk, 2, jnp.where(key >= chunk, 1, 0))
    within = key - chunk * part
    is_own = within < chunk_own
    beside = within - chunk_own
    is_right = beside >= SIDE * REACH
    beside = jnp.where(is_right, beside - SIDE * REACH, beside)
    side_col = jnp.where(is_right, right_first, left_first) + (beside & (REACH - 1))
    key_col = jnp.where(is_own, col_first + (within & (tile_cols - 1)), side_col)
    key_row[...] = SIDE * part + jnp.where(is_own, within >> log_cols, beside >> 3)
    query_col = col_first + (query & (tile_cols - 1))
    col_off = key_col - jnp.clip(query_col - REACH, 0, tile_cols * col_tiles - WINDOW)
    col_bias[...] = jnp.where((col_off >= 0) & (col_off < WINDOW), 0.0, MASKED)

    def strip(s, carry):
        here = row_id * strips + s
        first = jnp.clip(here - 1, 0, strips * row_tiles - 3)
        top = first - (row_id * strips - 1)
        rows = pl.ds(pl.multiple_of(s * chunk_own, chunk_own), chunk_own)
        row_start = jnp.clip(
            SIDE * here + query_row - REACH, 0, SIDE * strips * row_tiles - WINDOW
        )
        row_off = key_row[...] + SIDE * first - row_start
        bias = jnp.where((row_off >= 0) & (row_off < WINDOW), col_bias[...], MASKED)
        bias = jnp.concatenate([bias, bias], axis=1)
        heads = [slice(2 * DH * i, 2 * DH * (i + 1)) for i in range(PAIRS)]
        k_lanes = [slice(128 * i, 128 * i + SLAB) for i in range(PAIRS)]
        v_lanes = [slice(512 + 128 * i, 512 + 128 * i + SLAB) for i in range(PAIRS)]

        def band_of(lanes):
            return kv[pl.ds(top, 3), :, lanes].reshape(band, SLAB)

        def from_keys(lines, weights):
            got = jnp.zeros((2 * DH, SLAB), jnp.float32)
            for j in range(3):
                got += dot(kvt[top + j, lines, :], weights[chunk * j : chunk * (j + 1)])
            return got

        q2 = [pair_block(qt_ref[heads[i], rows], 16 * i) for i in range(PAIRS)]
        g2 = [pair_block(g_ref[heads[i], rows], V_SHIFT + 16 * i) for i in range(PAIRS)]
        prob, inv, row_dot, dscore = [], [], [], []
        for i in range(PAIRS):
            scores = dot(band_of(k_lanes[i]), q2[i]) * SCALE + bias
            top_score = jnp.max(scores, axis=0, keepdims=True)
            prob.append(jnp.exp(scores - top_score).astype(jnp.bfloat16))
        for i in range(PAIRS):
            total = jnp.zeros((16, SLAB), jnp.float32)
            for j in range(3):
                total += dot(ones, prob[i][chunk * j : chunk * (j + 1)])
            inv.append(1.0 / total[:1])
            v_rows = slice(INNER + heads[i].start, INNER + heads[i].stop)
            att = pick(from_keys(v_rows, prob[i]) * inv[i])
            ot[64 + heads[i].start : 64 + heads[i].stop, :] = att
            dots = att * g_ref[heads[i], rows].astype(jnp.float32)
            row_dot.append(
                jnp.concatenate(
                    [
                        jnp.sum(dots[:DH], axis=0, keepdims=True),
                        jnp.sum(dots[DH:], axis=0, keepdims=True),
                    ],
                    axis=1,
                )
            )
        for i in range(PAIRS):
            dprob = dot(band_of(v_lanes[i]), g2[i])
            inv_scale = inv[i] * SCALE
            change = dprob * inv_scale - row_dot[i] * inv_scale
            dscore.append((prob[i].astype(jnp.float32) * change).astype(jnp.bfloat16))
        for i in range(PAIRS):
            dv = nt_dot(prob[i], (g2[i].astype(jnp.float32) * inv[i]).astype(jnp.bfloat16))
            acc[pl.ds(top, 3), :, v_lanes[i]] += dv.reshape(3, chunk, SLAB)
        for i in range(PAIRS):
            dqt[heads[i], :] = pick(from_keys(heads[i], dscore[i]))
            dk = nt_dot(dscore[i], q2[i])
            acc[pl.ds(top, 3), :, k_lanes[i]] += dk.reshape(3, chunk, SLAB)
        o_ref[rows, :] = ot[...].T.astype(jnp.bfloat16)
        dq_ref[rows, :] = dqt[...].T.astype(jnp.bfloat16)
        for side in range(2):
            turned[side, :, rows] = left[side, rows, :].T
        return carry

    for copy in copies:
        copy.wait()
    lax.fori_loop(0, strips, strip, 0)
    share = sent_ref.shape[0] // 4
    for out_ref, half in ((sent_ref, 1 - tile_ref[1] % 2), (kept_ref, tile_ref[1] % 2)):
        products = []
        for side, right in enumerate((dq_ref, o_ref)):
            picked = [
                turned[side, pl.ds(pl.multiple_of((2 * r + half) * share, 16), share), :]
                for r in range(4)
            ]
            products.append(dot(jnp.concatenate(picked, axis=0), right[...]))
        first, second = products
        out_ref[:, :512] = first[:, :512].astype(jnp.bfloat16)
        out_ref[:, 512:640] = (first[:, 512:] + second[:, :128]).astype(jnp.bfloat16)
        out_ref[:, 640:] = second[:, 128:].astype(jnp.bfloat16)
    for slot, at in enumerate(side_order):
        own_grad = acc[slot, :chunk_own].astype(jnp.bfloat16)
        if at < strips:
            inner_ref[chunk_own * at : chunk_own * (at + 1), :] = own_grad
        else:
            edge_ref[chunk_own * (at - strips) : chunk_own * (at - strips + 1), :] = own_grad
        side_grad = acc[slot, chunk_own:].astype(jnp.bfloat16)
        if at < strips:
            side_ref[chunk_side * at : chunk_side * (at + 1), :] = side_grad
        else:
            at -= strips
            corner_grad_ref[chunk_side * at : chunk_side * (at + 1), :] = side_grad


def attention(token_rows, grad_rows, queries, own, grads, above, below, cols, corner):
    chunk_own = above.shape[0]
    strips = own.shape[0] // chunk_own
    chunk = chunk_own + cols.shape[0] // strips
    band = 3 * chunk
    counts = (strips, lax.axis_size("row"), lax.axis_size("col"))
    tile = jnp.stack([lax.axis_index("row"), lax.axis_index("col")]).astype(jnp.int32)
    token_count, width = own.shape
    whole = lambda a: pl.BlockSpec(
        a.shape, lambda _: (0,) * a.ndim, pipeline_mode=pl.Buffered(1)
    )
    outs = (
        jax.ShapeDtypeStruct((token_count, INNER + 64), jnp.bfloat16),
        jax.ShapeDtypeStruct((token_count, INNER + 64), jnp.bfloat16),
        jax.ShapeDtypeStruct(own.shape, jnp.bfloat16),
        jax.ShapeDtypeStruct((2 * chunk_own, width), jnp.bfloat16),
        jax.ShapeDtypeStruct(cols.shape, jnp.bfloat16),
        jax.ShapeDtypeStruct(corner.shape, jnp.bfloat16),
        jax.ShapeDtypeStruct((token_rows.shape[1] // 2, width), jnp.bfloat16),
        jax.ShapeDtypeStruct((token_rows.shape[1] // 2, width), jnp.bfloat16),
    )
    return pl.pallas_call(
        functools.partial(attention_kernel, counts),
        grid=(1,),
        out_shape=outs,
        in_specs=[
            pl.BlockSpec(memory_space=pltpu.SMEM),
            pl.BlockSpec(memory_space=pl.ANY),
            pl.BlockSpec(memory_space=pl.ANY),
            whole(queries),
            whole(own),
            whole(grads),
            whole(above),
            whole(below),
            whole(cols),
            whole(corner),
        ],
        out_specs=tuple(whole(o) for o in outs),
        scratch_shapes=[
            pltpu.VMEM((strips + 2, chunk, width), jnp.bfloat16),
            pltpu.VMEM((strips + 2, width, chunk), jnp.bfloat16),
            pltpu.VMEM((strips + 2, chunk, width), jnp.float32),
            pltpu.VMEM((640, chunk_own), jnp.float32),
            pltpu.VMEM((640, chunk_own), jnp.float32),
            pltpu.VMEM((2,) + token_rows.shape, jnp.bfloat16),
            pltpu.VMEM((2,) + token_rows.shape[::-1], jnp.bfloat16),
            pltpu.VMEM((band, chunk_own), jnp.int32),
            pltpu.VMEM((band, chunk_own), jnp.float32),
            pltpu.SemaphoreType.DMA((2,)),
        ],
        compiler_params=pltpu.CompilerParams(vmem_limit_bytes=30 * 1024 * 1024),
        cost_estimate=pl.CostEstimate(
            flops=12 * token_count * band * 2 * INNER,
            bytes_accessed=16 * 1024 * 1024,
            transcendentals=token_count * band * H,
        ),
        name="window_attention",
    )(tile, token_rows, grad_rows, queries, own, grads, above, below, cols, corner)


def late_kernel(
    own_ref, first, second, third, tokens_ref, inner_ref, side_ref, above_ref, below_ref,
    dq_ref, o_ref, sent_ref, kept_ref, all_ref, att_ref, turned, grad_ref,
):
    own = own_ref[0]
    count = inner_ref.shape[0]
    share = sent_ref.shape[0] // 4
    edge = above_ref.shape[0]
    width = inner_ref.shape[1]
    side = side_ref[: count // 2].astype(jnp.float32).reshape(-1, REACH, width)
    is_left = (own == 0).astype(jnp.float32)
    side = jnp.concatenate([side * (1.0 - is_left), side * is_left], axis=1)
    total = inner_ref[...].astype(jnp.float32) + side.reshape(count, width)
    grad_ref[:edge] = (total[:edge] + above_ref[...].astype(jnp.float32)).astype(jnp.bfloat16)
    grad_ref[edge : count - edge] = total[edge : count - edge].astype(jnp.bfloat16)
    grad_ref[count - edge :] = (
        total[count - edge :] + below_ref[...].astype(jnp.float32)
    ).astype(jnp.bfloat16)
    turned[...] = tokens_ref[...].T
    for out_ref, half in ((sent_ref, 1 - own), (kept_ref, own)):
        picked = [
            turned[pl.ds(pl.multiple_of((2 * r + half) * share, 16), share), :] for r in range(4)
        ]
        product = dot(jnp.concatenate(picked, axis=0), grad_ref[...])
        out_ref[...] = product.astype(jnp.bfloat16)
    all_ref[...] = jnp.concatenate([dq_ref[:, :INNER], grad_ref[...]], axis=1)
    att_ref[...] = o_ref[:, 64:]


def late_halves(earlier, token_rows, inner, side, above, below, dquery, attended):
    rows, width = token_rows.shape
    whole = lambda a: pl.BlockSpec(a.shape, lambda _: (0,) * a.ndim)
    out = jax.ShapeDtypeStruct((width // 2, 2 * INNER), jnp.bfloat16)
    grads = jax.ShapeDtypeStruct((rows, 3 * INNER), jnp.bfloat16)
    att = jax.ShapeDtypeStruct((rows, INNER), jnp.bfloat16)
    operands = (token_rows, inner, side, above, below, dquery, attended)
    own = lax.axis_index("col").astype(jnp.int32).reshape(1)
    return pl.pallas_call(
        late_kernel,
        grid=(1,),
        out_shape=(out, out, grads, att),
        in_specs=[pl.BlockSpec(memory_space=pltpu.SMEM)]
        + [pl.BlockSpec(memory_space=pl.ANY)] * 3
        + [whole(a) for a in operands],
        out_specs=(whole(out), whole(out), whole(grads), whole(att)),
        scratch_shapes=[
            pltpu.VMEM((width, rows), jnp.bfloat16),
            pltpu.VMEM((rows, 2 * INNER), jnp.bfloat16),
        ],
        compiler_params=pltpu.CompilerParams(vmem_limit_bytes=22 * 1024 * 1024),
        cost_estimate=LIGHT,
        name="late_weight_grad_halves",
    )(own, *earlier, *operands)


def core_parts_kernel(own_ref, kept_ref, got_ref, *refs):
    outs, total = refs[-5:-1], refs[-1]
    rows, padded, _ = total.shape
    share, small = kept_ref.shape[0] // rows, padded // 4
    for r in range(rows):
        part = slice(share * r, share * (r + 1))
        total[r, :share] = kept_ref[part].astype(jnp.float32) + got_ref[part].astype(jnp.float32)
        total[r, share:] = jnp.zeros((padded - share, total.shape[2]), jnp.float32)
    for step, out in enumerate(outs):
        first = pl.multiple_of((own_ref[0] ^ step) * small, 8)
        out[...] = total[:, pl.ds(first, small), :].astype(jnp.bfloat16)


def core_parts(sent, kept, *earlier):
    got = lax.ppermute(sent, "col", [(0, 1), (1, 0)])
    rows, images = lax.axis_size("row"), lax.axis_size("img")
    width = kept.shape[1]
    small = -(-kept.shape[0] // rows // (8 * images)) * 8
    own = lax.axis_index("img").astype(jnp.int32).reshape(1)
    return pl.pallas_call(
        core_parts_kernel,
        grid=(1,),
        out_shape=[jax.ShapeDtypeStruct((rows, small, width), jnp.bfloat16)] * images,
        in_specs=[pl.BlockSpec(memory_space=pltpu.SMEM)]
        + [pl.BlockSpec(kept.shape, lambda _: (0, 0))] * 2
        + [pl.BlockSpec(memory_space=pl.ANY)] * len(earlier),
        out_specs=[pl.BlockSpec((rows, small, width), lambda _: (0, 0, 0))] * images,
        scratch_shapes=[pltpu.VMEM((rows, images * small, width), jnp.float32)],
        compiler_params=pltpu.CompilerParams(vmem_limit_bytes=20 * 1024 * 1024),
        cost_estimate=LIGHT,
        name="core_parts",
    )(own, kept, got, *earlier)


def row_sum_kernel(kept, first, second, third, *refs):
    total = kept[...].astype(jnp.float32) + first[...].astype(jnp.float32)
    total += second[...].astype(jnp.float32)
    refs[-1][...] = (total + third[...].astype(jnp.float32)).astype(jnp.bfloat16)


def row_sum_after(parts, earlier):
    parts = [parts[0]] + exchanged(parts, "row")
    shape = parts[0].shape
    return pl.pallas_call(
        row_sum_kernel,
        grid=(1,),
        out_shape=jax.ShapeDtypeStruct(shape, jnp.bfloat16),
        in_specs=[pl.BlockSpec(shape, lambda _: (0, 0))] * 4 + [pl.BlockSpec(memory_space=pl.ANY)],
        out_specs=pl.BlockSpec(shape, lambda _: (0, 0)),
        compiler_params=pltpu.CompilerParams(vmem_limit_bytes=8 * 1024 * 1024),
        cost_estimate=LIGHT,
        name="row_sum",
    )(*parts, earlier)


def outputs_kernel(own_ref, *refs):
    parts, (qkv_ref, out_ref, early, late) = refs[:8], refs[8:]
    share = qkv_ref.shape[0]
    small = parts[0].shape[0]
    for step in range(4):
        first = pl.multiple_of((own_ref[0] ^ step) * small, 8)
        early[pl.ds(first, small), :] = parts[step][...].astype(jnp.float32)
        late[pl.ds(first, small), :] = parts[4 + step][...].astype(jnp.float32)
    qkv_ref[...] = jnp.concatenate([early[:share, :INNER], late[:share]], axis=1)
    out_ref[...] = early[:share, INNER:]


def written_outputs(early, late, share):
    small, width = early[0].shape
    parts = early + late
    own = lax.axis_index("img").astype(jnp.int32).reshape(1)
    shapes = [(share, 3 * INNER), (share, INNER)]
    return pl.pallas_call(
        outputs_kernel,
        grid=(1,),
        out_shape=[jax.ShapeDtypeStruct(shape, jnp.float32) for shape in shapes],
        in_specs=[pl.BlockSpec(memory_space=pltpu.SMEM)]
        + [pl.BlockSpec((small, width), lambda _: (0, 0))] * len(parts),
        out_specs=[pl.BlockSpec(shape, lambda _: (0, 0)) for shape in shapes],
        scratch_shapes=[pltpu.VMEM((len(early) * small, width), jnp.float32)] * 2,
        compiler_params=pltpu.CompilerParams(vmem_limit_bytes=16 * 1024 * 1024),
        cost_estimate=LIGHT,
        name="weight_grads",
    )(own, *parts)


def after(value, *earlier):
    return lax.optimization_barrier((value,) + earlier)[0]


def cut(block, axis, take):
    own = lax.axis_index(axis)
    return [take(block, own ^ step) for step in range(lax.axis_size(axis))]


def exchanged(parts, axis):
    got = []
    for step, part in enumerate(parts[1:], 1):
        pairs = [(i, i ^ step) for i in range(lax.axis_size(axis))]
        got.append(lax.ppermute(part, axis, pairs))
    return got


def added(kept, got, *earlier):
    if earlier:
        kept = after(kept, *earlier)
    total = kept.astype(jnp.float32)
    for g in got:
        total += g.astype(jnp.float32)
    return total.astype(jnp.bfloat16)


def row_parts(held):
    return cut(held, "row", lambda h, r: lax.dynamic_index_in_dim(h, r, 0, keepdims=False))


def plain_shares(part):
    held = lax.psum_scatter(part, ("row", "col"), scatter_dimension=0, tiled=True)
    return lax.psum(held, "img").astype(jnp.float32)


def local(tokens, qkv_weight, out_weight, upstream):
    _, tile_rows, tile_cols, width = tokens.shape
    token_count = tile_rows * tile_cols
    strips = tile_rows // SIDE
    chunk_own = SIDE * tile_cols
    row_count, col_count = lax.axis_size("row"), lax.axis_size("col")
    two_columns = col_count == 2
    col_id = lax.axis_index("col")
    token_rows = tokens.reshape(token_count, width)
    grad_rows = upstream.reshape(token_count, width)
    turns = (0,) if two_columns else (-1, 1)

    def moved(block, down, turn=None):
        pairs = []
        for r in range(row_count):
            for c in range(col_count):
                to_c = c if turn is None else (1 - c if turn == 0 else c + turn)
                if 0 <= r + down < row_count and 0 <= to_c < col_count:
                    pairs.append((r * col_count + c, (r + down) * col_count + to_c))
        return lax.ppermute(block, ("row", "col"), pairs)

    def edge(block, turn):
        if turn == 0:
            return lax.dynamic_slice_in_dim(block, (1 - col_id) * (tile_cols - REACH), REACH, 1)
        return block[:, tile_cols - REACH :] if turn == 1 else block[:, :REACH]

    def side_of(*blocks):
        got = []
        for turn in sorted(turns, reverse=True):
            near = [edge(block.reshape(-1, tile_cols, 2 * INNER), turn) for block in blocks]
            near = jnp.concatenate(near, axis=0) if len(near) > 1 else near[0]
            got.append(moved(near, 0, turn).reshape(-1, SIDE * REACH, 2 * INNER))
        got = got[0] if two_columns else jnp.concatenate(got, axis=1)
        return got.reshape(-1, 2 * INNER)

    queries, keyvals, top, bottom, near = project(token_rows, qkv_weight, tile_cols)
    above = moved(bottom, 1)
    below = moved(top, -1)
    if two_columns:
        cols = moved(near, 0, 0)
    else:
        cols = side_of(keyvals)
    corner = side_of(above, below)
    grad_att = lax.dot_general(
        out_weight, grad_rows, (((0,), (1,)), ((), ())), preferred_element_type=jnp.float32
    ).astype(jnp.bfloat16)
    attended, dquery, inner_grad, edge_grad, side_grad, corner_grad, sent, kept = attention(
        token_rows, grad_rows, queries, keyvals, grad_att, above, below, cols, corner
    )

    def outer(a, b):
        return lax.dot_general(
            a, b, (((0,), (0,)), ((), ())), preferred_element_type=jnp.float32
        ).astype(jnp.bfloat16)

    simple = two_columns and row_count == 4 and lax.axis_size("img") == 4
    if simple:
        early = core_parts(sent, kept)
    def outputs(attended, dqkv):
        sublayer_out = nt_dot(attended, out_weight).astype(jnp.bfloat16)
        return sublayer_out, nt_dot(dqkv, qkv_weight).astype(jnp.bfloat16)

    def spread(side, first):
        side = side.reshape(-1, SIDE, REACH, 2 * INNER).astype(jnp.float32)
        zeros = jnp.zeros((side.shape[0], SIDE, tile_cols - REACH, 2 * INNER), jnp.float32)
        order = [side, zeros] if first else [zeros, side]
        return jnp.concatenate(order, axis=2).reshape(-1, 2 * INNER)

    def sides_back(part):
        if two_columns:
            return moved(part, 0, 0).reshape(-1, SIDE * REACH, 2 * INNER)
        halves = part.reshape(-1, 2, SIDE * REACH, 2 * INNER)
        return jnp.stack([moved(halves[:, 0], 0, -1), moved(halves[:, 1], 0, 1)], axis=1)

    def returned(part):
        if two_columns:
            return jnp.where(col_id == 0, spread(part, False), spread(part, True))
        return spread(part[:, 0], False) + spread(part[:, 1], True)

    side, corner = sides_back(side_grad), sides_back(corner_grad)
    outer_grad = edge_grad.astype(jnp.float32) + returned(corner)
    outer_grad = outer_grad.astype(jnp.bfloat16)
    from_below = moved(outer_grad[:chunk_own], -1)
    from_above = moved(outer_grad[chunk_own:], 1)
    if simple:
        side = side.reshape(-1, 2 * INNER)
        sent, kept, dqkv, attended = late_halves(
            early[1:], token_rows, inner_grad, side, from_above, from_below, dquery, attended
        )
    else:
        dquery, attended = dquery[:, :INNER], attended[:, 64:]
        dkv = inner_grad.astype(jnp.float32) + returned(side)
        rest = jnp.zeros((token_count - chunk_own, 2 * INNER), jnp.float32)
        dkv = dkv + jnp.concatenate([from_above.astype(jnp.float32), rest], axis=0)
        dkv = dkv + jnp.concatenate([rest, from_below.astype(jnp.float32)], axis=0)
        dkv = dkv.astype(jnp.bfloat16)
        dqkv = jnp.concatenate([dquery, dkv], axis=1)
        sublayer_out, tokens_grad = outputs(attended, dqkv)
    if simple:
        early = added(early[0], exchanged(early, "img"))
        sublayer_out, tokens_grad = outputs(attended, dqkv)
        late = core_parts(sent, kept, early, sublayer_out, tokens_grad)
        late_got = exchanged(late, "img")
        late = added(late[0], late_got, early)
        early = row_sum_after(row_parts(early), late_got[0])
        late = row_parts(late)
        late = added(late[0], exchanged(late, "row"), early)
        share = width // (row_count * col_count)
        early = [early] + exchanged([early] * 4, "img")
        late = [late] + exchanged([late] * 4, "img")
        qkv_grad, out_grad = written_outputs(early, late, share)
    else:
        early = jnp.concatenate([outer(token_rows, dquery), outer(grad_rows, attended)], axis=1)
        early, late = plain_shares(early), plain_shares(outer(token_rows, dkv))
        qkv_grad = jnp.concatenate([early[:, :INNER], late], axis=1)
        out_grad = early[:, INNER:]
    return (
        sublayer_out.reshape(tokens.shape),
        tokens_grad.reshape(tokens.shape),
        qkv_grad,
        out_grad,
    )


def solution(mesh):
    return jax.shard_map(
        local,
        mesh=mesh,
        in_specs=(P("img", "row", "col", None), P(), P(), P("img", "row", "col", None)),
        out_specs=(
            P("img", "row", "col", None),
            P("img", "row", "col", None),
            P(("row", "col"), None),
            P(("row", "col"), None),
        ),
        check_vma=False,
    )
```

```python
import jax
import jax.numpy as jnp
from jax import lax
from jax.experimental import pallas as pl
from jax.experimental.pallas import tpu as pltpu
from jax.sharding import PartitionSpec as P

H = 8
DH = 72
INNER = H * DH
REACH = 8
WINDOW = 17
SIDE = 8
PAIRS = H // 2
SLAB = 256
V_SHIFT = 64
MASKED = -1e30
SCALE = DH ** (-0.5)
LIGHT = pl.CostEstimate(flops=1, bytes_accessed=1, transcendentals=0)


def shifted_pairs(count, by):
    return [(i, i + by) for i in range(count) if 0 <= i + by < count]


def dot(a, b):
    return jnp.dot(a, b, preferred_element_type=jnp.float32)


def nt_dot(a, b):
    return lax.dot_general(a, b, (((1,), (1,)), ((), ())), preferred_element_type=jnp.float32)


PIECE = 384
PIECES = 2 * INNER // PIECE
CUTS = 3


def fetch(pairs, sems):
    copies = [pltpu.make_async_copy(*pair, sems.at[n]) for n, pair in enumerate(pairs)]
    for copy in copies:
        copy.start()
    return copies


def weight_pieces(weight_ref, weight):
    part = PIECE // CUTS
    return [
        (weight_ref.at[pl.ds(INNER + part * p, part)], weight.at[pl.ds(part * p, part)])
        for p in range(PIECES * CUTS)
    ]


def edges_kernel(tokens_ref, weight_ref, top_ref, bottom_ref, tokens, weight, sems):
    edge = top_ref.shape[0]
    ends = [(0, 0), (edge, tokens_ref.shape[0] - edge)]
    token_pairs = [
        (tokens_ref.at[pl.ds(there, edge)], tokens.at[pl.ds(here, edge)]) for here, there in ends
    ]
    copies = fetch(token_pairs + weight_pieces(weight_ref, weight), sems)
    copies[0].wait()
    copies[1].wait()
    for p in range(PIECES):
        for copy in copies[2 + CUTS * p : 2 + CUTS * (p + 1)]:
            copy.wait()
        lanes = slice(PIECE * p, PIECE * (p + 1))
        part = nt_dot(tokens[...], weight[lanes]).astype(jnp.bfloat16)
        top_ref[:, lanes] = part[:edge]
        bottom_ref[:, lanes] = part[edge:]


def project_kernel(
    own_ref, top_ref, tokens_ref, weight_ref, qt_ref, kv_ref, near_ref, tokens, weight, q_weight, sems
):
    pairs = [(tokens_ref, tokens)] + weight_pieces(weight_ref, weight)
    copies = fetch(pairs + [(weight_ref.at[pl.ds(0, INNER)], q_weight)], sems)
    copies[0].wait()
    for p in range(PIECES):
        for copy in copies[1 + CUTS * p : 1 + CUTS * (p + 1)]:
            copy.wait()
        lanes = slice(PIECE * p, PIECE * (p + 1))
        part = nt_dot(tokens[...], weight[lanes])
        kv_ref[:, lanes] = part.astype(jnp.bfloat16)
        grid = part.reshape(near_ref.shape[0] // REACH, -1, PIECE)
        is_right = own_ref[0].astype(jnp.float32)
        near = grid[:, :REACH] * is_right + grid[:, -REACH:] * (1.0 - is_right)
        near_ref[:, lanes] = near.reshape(-1, PIECE).astype(jnp.bfloat16)
    copies[-1].wait()
    qt_ref[...] = nt_dot(q_weight[...], tokens[...]).astype(jnp.bfloat16)


def project(token_rows, weight, tile_cols):
    rows, width = token_rows.shape
    edge = SIDE * tile_cols
    own = lax.axis_index("col").astype(jnp.int32).reshape(1)
    shape = lambda count: jax.ShapeDtypeStruct((count, 2 * INNER), jnp.bfloat16)
    block = lambda count: pl.BlockSpec((count, 2 * INNER), lambda _: (0, 0))
    anywhere = pl.BlockSpec(memory_space=pl.ANY)
    top, bottom = pl.pallas_call(
        edges_kernel,
        grid=(1,),
        out_shape=[shape(edge)] * 2,
        in_specs=[anywhere] * 2,
        out_specs=[block(edge)] * 2,
        scratch_shapes=[
            pltpu.VMEM((2 * edge, width), jnp.bfloat16),
            pltpu.VMEM((2 * INNER, width), jnp.bfloat16),
            pltpu.SemaphoreType.DMA((PIECES * CUTS + 2,)),
        ],
        compiler_params=pltpu.CompilerParams(vmem_limit_bytes=56 * 1024 * 1024),
        cost_estimate=LIGHT,
        name="project_edges",
    )(token_rows, weight.T)
    near = rows // tile_cols * REACH
    queries, keyvals, near = pl.pallas_call(
        project_kernel,
        grid=(1,),
        out_shape=[jax.ShapeDtypeStruct((INNER, rows), jnp.bfloat16), shape(rows), shape(near)],
        in_specs=[pl.BlockSpec(memory_space=pltpu.SMEM)] + [anywhere] * 3,
        out_specs=[pl.BlockSpec((INNER, rows), lambda _: (0, 0)), block(rows), block(near)],
        scratch_shapes=[
            pltpu.VMEM((rows, width), jnp.bfloat16),
            pltpu.VMEM((2 * INNER, width), jnp.bfloat16),
            pltpu.VMEM((INNER, width), jnp.bfloat16),
            pltpu.SemaphoreType.DMA((PIECES * CUTS + 2,)),
        ],
        compiler_params=pltpu.CompilerParams(vmem_limit_bytes=56 * 1024 * 1024),
        cost_estimate=LIGHT,
        name="project",
    )(own, top, token_rows, weight.T)
    return queries, keyvals, top, bottom, near


def attention_kernel(
    start_ref,
    core_ref,
    tokens_ref,
    upstream_ref,
    qt_ref,
    own_ref,
    g_ref,
    above_ref,
    below_ref,
    cols_ref,
    corner_ref,
    bias_ref,
    o_ref,
    dq_ref,
    inner_ref,
    edge_ref,
    side_ref,
    corner_grad_ref,
    sent_ref,
    kept_ref,
    kv,
    kvt,
    acc,
    ot,
    dqt,
    left,
    turned,
    sems,
):
    strips = bias_ref.shape[0]
    chunk = kv.shape[1]
    chunk_own = own_ref.shape[0] // strips
    chunk_side = chunk - chunk_own
    band = 3 * chunk
    token_count = own_ref.shape[0]
    last = strips + 1
    side_order = [strips] + list(range(strips)) + [strips + 1]

    def place(slot, first, part):
        count = part.shape[0]
        kv[slot, first : first + count] = part
        if count < 128:
            filler = jnp.zeros((128 - count, 2 * INNER), part.dtype)
            part = jnp.concatenate([part, filler], axis=0)
        kvt[slot, :, first : first + count] = part.T[:, :count]

    copies = fetch([(tokens_ref, left.at[0]), (upstream_ref, left.at[1])], sems)
    dqt[INNER:, :] = jnp.zeros((64, chunk_own), jnp.float32)
    ot[:64, :] = jnp.zeros((64, chunk_own), jnp.float32)
    for s in range(strips):
        place(s + 1, 0, own_ref[chunk_own * s : chunk_own * (s + 1)])
    for s in range(strips):
        place(s + 1, chunk_own, cols_ref[chunk_side * s : chunk_side * (s + 1)])
    place(0, 0, above_ref[...])
    place(last, 0, below_ref[...])
    for slot, at in ((0, 0), (last, 1)):
        place(slot, chunk_own, corner_ref[chunk_side * at : chunk_side * (at + 1)])
    acc[...] = jnp.zeros_like(acc)

    row = lax.broadcasted_iota(jnp.int32, (2 * DH, chunk_own), 0)
    first_head = row < DH
    mask_a = jnp.where(first_head, 1.0, 0.0).astype(jnp.bfloat16)
    mask_b = jnp.where(first_head, 0.0, 1.0).astype(jnp.bfloat16)
    ones = jnp.ones((16, chunk), jnp.bfloat16)

    def pair_block(part, above):
        block = jnp.concatenate([part * mask_a, part * mask_b], axis=1)
        parts = [block]
        if above:
            parts = [jnp.zeros((above, block.shape[1]), block.dtype)] + parts
        below = SLAB - 2 * DH - above
        if below:
            parts = parts + [jnp.zeros((below, block.shape[1]), block.dtype)]
        return jnp.concatenate(parts, axis=0)

    def pick(both):
        return jnp.where(first_head, both[:, :chunk_own], both[:, chunk_own:])

    def strip(s, carry):
        top = start_ref[s]
        rows = pl.ds(pl.multiple_of(s * chunk_own, chunk_own), chunk_own)
        bias = bias_ref[s]
        bias = jnp.concatenate([bias, bias], axis=1)
        heads = [slice(2 * DH * i, 2 * DH * (i + 1)) for i in range(PAIRS)]
        k_lanes = [slice(128 * i, 128 * i + SLAB) for i in range(PAIRS)]
        v_lanes = [slice(512 + 128 * i, 512 + 128 * i + SLAB) for i in range(PAIRS)]

        def band_of(lanes):
            return kv[pl.ds(top, 3), :, lanes].reshape(band, SLAB)

        def from_keys(lines, weights):
            got = jnp.zeros((2 * DH, SLAB), jnp.float32)
            for j in range(3):
                got += dot(kvt[top + j, lines, :], weights[chunk * j : chunk * (j + 1)])
            return got

        q2 = [pair_block(qt_ref[heads[i], rows], 16 * i) for i in range(PAIRS)]
        g2 = [pair_block(g_ref[heads[i], rows], V_SHIFT + 16 * i) for i in range(PAIRS)]
        prob, inv, row_dot, dscore = [], [], [], []
        for i in range(PAIRS):
            scores = dot(band_of(k_lanes[i]), q2[i]) * SCALE + bias
            top_score = jnp.max(scores, axis=0, keepdims=True)
            prob.append(jnp.exp(scores - top_score).astype(jnp.bfloat16))
        for i in range(PAIRS):
            total = jnp.zeros((16, SLAB), jnp.float32)
            for j in range(3):
                total += dot(ones, prob[i][chunk * j : chunk * (j + 1)])
            inv.append(1.0 / total[:1])
            v_rows = slice(INNER + heads[i].start, INNER + heads[i].stop)
            att = pick(from_keys(v_rows, prob[i]) * inv[i])
            ot[64 + heads[i].start : 64 + heads[i].stop, :] = att
            dots = att * g_ref[heads[i], rows].astype(jnp.float32)
            row_dot.append(
                jnp.concatenate(
                    [
                        jnp.sum(dots[:DH], axis=0, keepdims=True),
                        jnp.sum(dots[DH:], axis=0, keepdims=True),
                    ],
                    axis=1,
                )
            )
        for i in range(PAIRS):
            dprob = dot(band_of(v_lanes[i]), g2[i])
            inv_scale = inv[i] * SCALE
            change = dprob * inv_scale - row_dot[i] * inv_scale
            dscore.append((prob[i].astype(jnp.float32) * change).astype(jnp.bfloat16))
        for i in range(PAIRS):
            dv = nt_dot(prob[i], (g2[i].astype(jnp.float32) * inv[i]).astype(jnp.bfloat16))
            acc[pl.ds(top, 3), :, v_lanes[i]] += dv.reshape(3, chunk, SLAB)
        for i in range(PAIRS):
            dqt[heads[i], :] = pick(from_keys(heads[i], dscore[i]))
            dk = nt_dot(dscore[i], q2[i])
            acc[pl.ds(top, 3), :, k_lanes[i]] += dk.reshape(3, chunk, SLAB)
        o_ref[rows, :] = ot[...].T.astype(jnp.bfloat16)
        dq_ref[rows, :] = dqt[...].T.astype(jnp.bfloat16)
        for side in range(2):
            turned[side, :, rows] = left[side, rows, :].T
        return carry

    for copy in copies:
        copy.wait()
    lax.fori_loop(0, strips, strip, 0)
    share = sent_ref.shape[0] // 4
    for out_ref, half in ((sent_ref, 1 - core_ref[0]), (kept_ref, core_ref[0])):
        products = []
        for side, right in enumerate((dq_ref, o_ref)):
            picked = [
                turned[side, pl.ds(pl.multiple_of((2 * r + half) * share, 16), share), :]
                for r in range(4)
            ]
            products.append(dot(jnp.concatenate(picked, axis=0), right[...]))
        first, second = products
        out_ref[:, :512] = first[:, :512].astype(jnp.bfloat16)
        out_ref[:, 512:640] = (first[:, 512:] + second[:, :128]).astype(jnp.bfloat16)
        out_ref[:, 640:] = second[:, 128:].astype(jnp.bfloat16)
    for slot, at in enumerate(side_order):
        own_grad = acc[slot, :chunk_own].astype(jnp.bfloat16)
        if at < strips:
            inner_ref[chunk_own * at : chunk_own * (at + 1), :] = own_grad
        else:
            edge_ref[chunk_own * (at - strips) : chunk_own * (at - strips + 1), :] = own_grad
        side_grad = acc[slot, chunk_own:].astype(jnp.bfloat16)
        if at < strips:
            side_ref[chunk_side * at : chunk_side * (at + 1), :] = side_grad
        else:
            at -= strips
            corner_grad_ref[chunk_side * at : chunk_side * (at + 1), :] = side_grad


def attention(start, token_rows, grad_rows, queries, own, grads, above, below, cols, corner, bias):
    strips, band, chunk_own = bias.shape
    chunk = band // 3
    token_count, width = own.shape
    whole = lambda a: pl.BlockSpec(
        a.shape, lambda _: (0,) * a.ndim, pipeline_mode=pl.Buffered(1)
    )
    outs = (
        jax.ShapeDtypeStruct((token_count, INNER + 64), jnp.bfloat16),
        jax.ShapeDtypeStruct((token_count, INNER + 64), jnp.bfloat16),
        jax.ShapeDtypeStruct(own.shape, jnp.bfloat16),
        jax.ShapeDtypeStruct((2 * chunk_own, width), jnp.bfloat16),
        jax.ShapeDtypeStruct(cols.shape, jnp.bfloat16),
        jax.ShapeDtypeStruct(corner.shape, jnp.bfloat16),
        jax.ShapeDtypeStruct((token_rows.shape[1] // 2, width), jnp.bfloat16),
        jax.ShapeDtypeStruct((token_rows.shape[1] // 2, width), jnp.bfloat16),
    )
    core = lax.axis_index("col").astype(jnp.int32).reshape(1) % 2
    return pl.pallas_call(
        attention_kernel,
        grid=(1,),
        out_shape=outs,
        in_specs=[
            pl.BlockSpec(memory_space=pltpu.SMEM),
            pl.BlockSpec(memory_space=pltpu.SMEM),
            pl.BlockSpec(memory_space=pl.ANY),
            pl.BlockSpec(memory_space=pl.ANY),
            whole(queries),
            whole(own),
            whole(grads),
            whole(above),
            whole(below),
            whole(cols),
            whole(corner),
            whole(bias),
        ],
        out_specs=tuple(whole(o) for o in outs),
        scratch_shapes=[
            pltpu.VMEM((strips + 2, chunk, width), jnp.bfloat16),
            pltpu.VMEM((strips + 2, width, chunk), jnp.bfloat16),
            pltpu.VMEM((strips + 2, chunk, width), jnp.float32),
            pltpu.VMEM((640, chunk_own), jnp.float32),
            pltpu.VMEM((640, chunk_own), jnp.float32),
            pltpu.VMEM((2,) + token_rows.shape, jnp.bfloat16),
            pltpu.VMEM((2,) + token_rows.shape[::-1], jnp.bfloat16),
            pltpu.SemaphoreType.DMA((2,)),
        ],
        compiler_params=pltpu.CompilerParams(vmem_limit_bytes=40 * 1024 * 1024),
        cost_estimate=pl.CostEstimate(
            flops=12 * token_count * band * 2 * INNER,
            bytes_accessed=16 * 1024 * 1024,
            transcendentals=token_count * band * H,
        ),
        name="window_attention",
    )(start, core, token_rows, grad_rows, queries, own, grads, above, below, cols, corner, bias)


def late_kernel(
    own_ref, first, second, third, tokens_ref, inner_ref, side_ref, above_ref, below_ref,
    dq_ref, o_ref, sent_ref, kept_ref, all_ref, att_ref, turned, grad_ref,
):
    own = own_ref[0]
    count = inner_ref.shape[0]
    share = sent_ref.shape[0] // 4
    edge = above_ref.shape[0]
    width = inner_ref.shape[1]
    side = side_ref[: count // 2].astype(jnp.float32).reshape(-1, REACH, width)
    is_left = (own == 0).astype(jnp.float32)
    side = jnp.concatenate([side * (1.0 - is_left), side * is_left], axis=1)
    total = inner_ref[...].astype(jnp.float32) + side.reshape(count, width)
    grad_ref[:edge] = (total[:edge] + above_ref[...].astype(jnp.float32)).astype(jnp.bfloat16)
    grad_ref[edge : count - edge] = total[edge : count - edge].astype(jnp.bfloat16)
    grad_ref[count - edge :] = (
        total[count - edge :] + below_ref[...].astype(jnp.float32)
    ).astype(jnp.bfloat16)
    turned[...] = tokens_ref[...].T
    for out_ref, half in ((sent_ref, 1 - own), (kept_ref, own)):
        picked = [
            turned[pl.ds(pl.multiple_of((2 * r + half) * share, 16), share), :] for r in range(4)
        ]
        product = dot(jnp.concatenate(picked, axis=0), grad_ref[...])
        out_ref[...] = product.astype(jnp.bfloat16)
    all_ref[...] = jnp.concatenate([dq_ref[:, :INNER], grad_ref[...]], axis=1)
    att_ref[...] = o_ref[:, 64:]


def late_halves(earlier, token_rows, inner, side, above, below, dquery, attended):
    rows, width = token_rows.shape
    whole = lambda a: pl.BlockSpec(a.shape, lambda _: (0,) * a.ndim)
    out = jax.ShapeDtypeStruct((width // 2, 2 * INNER), jnp.bfloat16)
    grads = jax.ShapeDtypeStruct((rows, 3 * INNER), jnp.bfloat16)
    att = jax.ShapeDtypeStruct((rows, INNER), jnp.bfloat16)
    operands = (token_rows, inner, side, above, below, dquery, attended)
    own = lax.axis_index("col").astype(jnp.int32).reshape(1)
    return pl.pallas_call(
        late_kernel,
        grid=(1,),
        out_shape=(out, out, grads, att),
        in_specs=[pl.BlockSpec(memory_space=pltpu.SMEM)]
        + [pl.BlockSpec(memory_space=pl.ANY)] * 3
        + [whole(a) for a in operands],
        out_specs=(whole(out), whole(out), whole(grads), whole(att)),
        scratch_shapes=[
            pltpu.VMEM((width, rows), jnp.bfloat16),
            pltpu.VMEM((rows, 2 * INNER), jnp.bfloat16),
        ],
        compiler_params=pltpu.CompilerParams(vmem_limit_bytes=22 * 1024 * 1024),
        cost_estimate=LIGHT,
        name="late_weight_grad_halves",
    )(own, *earlier, *operands)


def core_parts_kernel(own_ref, kept_ref, got_ref, *refs):
    outs, total = refs[-5:-1], refs[-1]
    rows, padded, _ = total.shape
    share, small = kept_ref.shape[0] // rows, padded // 4
    for r in range(rows):
        part = slice(share * r, share * (r + 1))
        total[r, :share] = kept_ref[part].astype(jnp.float32) + got_ref[part].astype(jnp.float32)
        total[r, share:] = jnp.zeros((padded - share, total.shape[2]), jnp.float32)
    for step, out in enumerate(outs):
        first = pl.multiple_of((own_ref[0] ^ step) * small, 8)
        out[...] = total[:, pl.ds(first, small), :].astype(jnp.bfloat16)


def core_parts(sent, kept, *earlier):
    got = lax.ppermute(sent, "col", [(0, 1), (1, 0)])
    rows, images = lax.axis_size("row"), lax.axis_size("img")
    width = kept.shape[1]
    small = -(-kept.shape[0] // rows // (8 * images)) * 8
    own = lax.axis_index("img").astype(jnp.int32).reshape(1)
    return pl.pallas_call(
        core_parts_kernel,
        grid=(1,),
        out_shape=[jax.ShapeDtypeStruct((rows, small, width), jnp.bfloat16)] * images,
        in_specs=[pl.BlockSpec(memory_space=pltpu.SMEM)]
        + [pl.BlockSpec(kept.shape, lambda _: (0, 0))] * 2
        + [pl.BlockSpec(memory_space=pl.ANY)] * len(earlier),
        out_specs=[pl.BlockSpec((rows, small, width), lambda _: (0, 0, 0))] * images,
        scratch_shapes=[pltpu.VMEM((rows, images * small, width), jnp.float32)],
        compiler_params=pltpu.CompilerParams(vmem_limit_bytes=20 * 1024 * 1024),
        cost_estimate=LIGHT,
        name="core_parts",
    )(own, kept, got, *earlier)


def row_sum_kernel(kept, first, second, third, *refs):
    total = kept[...].astype(jnp.float32) + first[...].astype(jnp.float32)
    total += second[...].astype(jnp.float32)
    refs[-1][...] = (total + third[...].astype(jnp.float32)).astype(jnp.bfloat16)


def row_sum_after(parts, earlier):
    parts = [parts[0]] + exchanged(parts, "row")
    shape = parts[0].shape
    return pl.pallas_call(
        row_sum_kernel,
        grid=(1,),
        out_shape=jax.ShapeDtypeStruct(shape, jnp.bfloat16),
        in_specs=[pl.BlockSpec(shape, lambda _: (0, 0))] * 4 + [pl.BlockSpec(memory_space=pl.ANY)],
        out_specs=pl.BlockSpec(shape, lambda _: (0, 0)),
        compiler_params=pltpu.CompilerParams(vmem_limit_bytes=8 * 1024 * 1024),
        cost_estimate=LIGHT,
        name="row_sum",
    )(*parts, earlier)


def outputs_kernel(own_ref, *refs):
    parts, (qkv_ref, out_ref, early, late) = refs[:8], refs[8:]
    share = qkv_ref.shape[0]
    small = parts[0].shape[0]
    for step in range(4):
        first = pl.multiple_of((own_ref[0] ^ step) * small, 8)
        early[pl.ds(first, small), :] = parts[step][...].astype(jnp.float32)
        late[pl.ds(first, small), :] = parts[4 + step][...].astype(jnp.float32)
    qkv_ref[...] = jnp.concatenate([early[:share, :INNER], late[:share]], axis=1)
    out_ref[...] = early[:share, INNER:]


def written_outputs(early, late, share):
    small, width = early[0].shape
    parts = early + late
    own = lax.axis_index("img").astype(jnp.int32).reshape(1)
    shapes = [(share, 3 * INNER), (share, INNER)]
    return pl.pallas_call(
        outputs_kernel,
        grid=(1,),
        out_shape=[jax.ShapeDtypeStruct(shape, jnp.float32) for shape in shapes],
        in_specs=[pl.BlockSpec(memory_space=pltpu.SMEM)]
        + [pl.BlockSpec((small, width), lambda _: (0, 0))] * len(parts),
        out_specs=[pl.BlockSpec(shape, lambda _: (0, 0)) for shape in shapes],
        scratch_shapes=[pltpu.VMEM((len(early) * small, width), jnp.float32)] * 2,
        compiler_params=pltpu.CompilerParams(vmem_limit_bytes=16 * 1024 * 1024),
        cost_estimate=LIGHT,
        name="weight_grads",
    )(own, *parts)


def window_starts(places, extent):
    return jnp.clip(places - REACH, 0, extent - WINDOW)


def window_bias(tile_rows, tile_cols, two_columns):
    row_id = lax.axis_index("row")
    col_id = lax.axis_index("col")
    frame_rows = tile_rows * lax.axis_size("row")
    frame_cols = tile_cols * lax.axis_size("col")
    strips = tile_rows // SIDE
    col_first = col_id * tile_cols
    strip_id = jnp.arange(strips, dtype=jnp.int32)
    first_chunk = row_id * strips - 1
    band_chunk = jnp.clip(row_id * strips + strip_id - 1, 0, frame_rows // SIDE - 3)
    side = jnp.arange(SIDE, dtype=jnp.int32)
    own_cols = col_first + jnp.arange(tile_cols, dtype=jnp.int32)
    low, high = col_first - REACH + side, col_first + tile_cols + side
    spans = [own_cols, jnp.where(col_id == 0, high, low)] if two_columns else [own_cols, low, high]
    chunk_rows = jnp.concatenate([jnp.repeat(side, span.shape[0]) for span in spans])
    chunk_cols = jnp.concatenate([jnp.tile(span, SIDE) for span in spans])
    in_band = jnp.concatenate([SIDE * j + chunk_rows for j in range(3)])
    key_col = jnp.tile(chunk_cols, 3)
    key_row = SIDE * band_chunk[:, None] + in_band[None, :]
    query_row = row_id * tile_rows + SIDE * strip_id[:, None] + jnp.repeat(side, tile_cols)[None, :]
    row_start = window_starts(query_row, frame_rows)
    col_start = window_starts(jnp.tile(own_cols, SIDE), frame_cols)
    row_off = key_row[:, :, None] - row_start[:, None, :]
    col_off = key_col[:, None] - col_start[None, :]
    row_ok = (row_off >= 0) & (row_off < WINDOW)
    col_ok = (col_off >= 0) & (col_off < WINDOW)
    bias = jnp.where(row_ok & col_ok[None], 0.0, MASKED).astype(jnp.float32)
    return (band_chunk - first_chunk).astype(jnp.int32), bias


def after(value, *earlier):
    return lax.optimization_barrier((value,) + earlier)[0]


def cut(block, axis, take):
    own = lax.axis_index(axis)
    return [take(block, own ^ step) for step in range(lax.axis_size(axis))]


def exchanged(parts, axis):
    got = []
    for step, part in enumerate(parts[1:], 1):
        pairs = [(i, i ^ step) for i in range(lax.axis_size(axis))]
        got.append(lax.ppermute(part, axis, pairs))
    return got


def added(kept, got, *earlier):
    if earlier:
        kept = after(kept, *earlier)
    total = kept.astype(jnp.float32)
    for g in got:
        total += g.astype(jnp.float32)
    return total.astype(jnp.bfloat16)


def row_parts(held):
    return cut(held, "row", lambda h, r: lax.dynamic_index_in_dim(h, r, 0, keepdims=False))


def plain_shares(part):
    held = lax.psum_scatter(part, ("row", "col"), scatter_dimension=0, tiled=True)
    return lax.psum(held, "img").astype(jnp.float32)


def local(tokens, qkv_weight, out_weight, upstream):
    _, tile_rows, tile_cols, width = tokens.shape
    token_count = tile_rows * tile_cols
    strips = tile_rows // SIDE
    chunk_own = SIDE * tile_cols
    row_count, col_count = lax.axis_size("row"), lax.axis_size("col")
    two_columns = col_count == 2
    col_id = lax.axis_index("col")
    token_rows = tokens.reshape(token_count, width)
    grad_rows = upstream.reshape(token_count, width)
    turns = (0,) if two_columns else (-1, 1)

    def moved(block, down, turn=None):
        pairs = []
        for r in range(row_count):
            for c in range(col_count):
                to_c = c if turn is None else (1 - c if turn == 0 else c + turn)
                if 0 <= r + down < row_count and 0 <= to_c < col_count:
                    pairs.append((r * col_count + c, (r + down) * col_count + to_c))
        return lax.ppermute(block, ("row", "col"), pairs)

    def edge(block, turn):
        if turn == 0:
            return lax.dynamic_slice_in_dim(block, (1 - col_id) * (tile_cols - REACH), REACH, 1)
        return block[:, tile_cols - REACH :] if turn == 1 else block[:, :REACH]

    def side_of(*blocks):
        got = []
        for turn in sorted(turns, reverse=True):
            near = [edge(block.reshape(-1, tile_cols, 2 * INNER), turn) for block in blocks]
            near = jnp.concatenate(near, axis=0) if len(near) > 1 else near[0]
            got.append(moved(near, 0, turn).reshape(-1, SIDE * REACH, 2 * INNER))
        got = got[0] if two_columns else jnp.concatenate(got, axis=1)
        return got.reshape(-1, 2 * INNER)

    queries, keyvals, top, bottom, near = project(token_rows, qkv_weight, tile_cols)
    above = moved(bottom, 1)
    below = moved(top, -1)
    if two_columns:
        cols = moved(near, 0, 0)
    else:
        cols = side_of(keyvals)
    corner = side_of(above, below)
    grad_att = lax.dot_general(
        out_weight, grad_rows, (((0,), (1,)), ((), ())), preferred_element_type=jnp.float32
    ).astype(jnp.bfloat16)
    start, bias = window_bias(tile_rows, tile_cols, two_columns)
    attended, dquery, inner_grad, edge_grad, side_grad, corner_grad, sent, kept = attention(
        start, token_rows, grad_rows, queries, keyvals, grad_att, above, below, cols, corner, bias
    )

    def outer(a, b):
        return lax.dot_general(
            a, b, (((0,), (0,)), ((), ())), preferred_element_type=jnp.float32
        ).astype(jnp.bfloat16)

    simple = two_columns and row_count == 4 and lax.axis_size("img") == 4
    if simple:
        early = core_parts(sent, kept)
    def outputs(attended, dqkv):
        sublayer_out = nt_dot(attended, out_weight).astype(jnp.bfloat16)
        return sublayer_out, nt_dot(dqkv, qkv_weight).astype(jnp.bfloat16)

    def spread(side, first):
        side = side.reshape(-1, SIDE, REACH, 2 * INNER).astype(jnp.float32)
        zeros = jnp.zeros((side.shape[0], SIDE, tile_cols - REACH, 2 * INNER), jnp.float32)
        order = [side, zeros] if first else [zeros, side]
        return jnp.concatenate(order, axis=2).reshape(-1, 2 * INNER)

    def sides_back(part):
        if two_columns:
            return moved(part, 0, 0).reshape(-1, SIDE * REACH, 2 * INNER)
        halves = part.reshape(-1, 2, SIDE * REACH, 2 * INNER)
        return jnp.stack([moved(halves[:, 0], 0, -1), moved(halves[:, 1], 0, 1)], axis=1)

    def returned(part):
        if two_columns:
            return jnp.where(col_id == 0, spread(part, False), spread(part, True))
        return spread(part[:, 0], False) + spread(part[:, 1], True)

    side, corner = sides_back(side_grad), sides_back(corner_grad)
    outer_grad = edge_grad.astype(jnp.float32) + returned(corner)
    outer_grad = outer_grad.astype(jnp.bfloat16)
    from_below = moved(outer_grad[:chunk_own], -1)
    from_above = moved(outer_grad[chunk_own:], 1)
    if simple:
        side = side.reshape(-1, 2 * INNER)
        sent, kept, dqkv, attended = late_halves(
            early[1:], token_rows, inner_grad, side, from_above, from_below, dquery, attended
        )
    else:
        dquery, attended = dquery[:, :INNER], attended[:, 64:]
        dkv = inner_grad.astype(jnp.float32) + returned(side)
        rest = jnp.zeros((token_count - chunk_own, 2 * INNER), jnp.float32)
        dkv = dkv + jnp.concatenate([from_above.astype(jnp.float32), rest], axis=0)
        dkv = dkv + jnp.concatenate([rest, from_below.astype(jnp.float32)], axis=0)
        dkv = dkv.astype(jnp.bfloat16)
        dqkv = jnp.concatenate([dquery, dkv], axis=1)
        sublayer_out, tokens_grad = outputs(attended, dqkv)
    if simple:
        early = added(early[0], exchanged(early, "img"))
        sublayer_out, tokens_grad = outputs(attended, dqkv)
        late = core_parts(sent, kept, early, sublayer_out, tokens_grad)
        late_got = exchanged(late, "img")
        late = added(late[0], late_got, early)
        early = row_sum_after(row_parts(early), late_got[0])
        late = row_parts(late)
        late = added(late[0], exchanged(late, "row"), early)
        share = width // (row_count * col_count)
        early = [early] + exchanged([early] * 4, "img")
        late = [late] + exchanged([late] * 4, "img")
        qkv_grad, out_grad = written_outputs(early, late, share)
    else:
        early = jnp.concatenate([outer(token_rows, dquery), outer(grad_rows, attended)], axis=1)
        early, late = plain_shares(early), plain_shares(outer(token_rows, dkv))
        qkv_grad = jnp.concatenate([early[:, :INNER], late], axis=1)
        out_grad = early[:, INNER:]
    return (
        sublayer_out.reshape(tokens.shape),
        tokens_grad.reshape(tokens.shape),
        qkv_grad,
        out_grad,
    )


def solution(mesh):
    return jax.shard_map(
        local,
        mesh=mesh,
        in_specs=(P("img", "row", "col", None), P(), P(), P("img", "row", "col", None)),
        out_specs=(
            P("img", "row", "col", None),
            P("img", "row", "col", None),
            P(("row", "col"), None),
            P(("row", "col"), None),
        ),
        check_vma=False,
    )
```
